32 devices in a mesh: seq: 16 (over z, y, core), head: 2 (over x).
Axes of the slice: x: 2, y: 2, z: 4, core: 2. Of those that a mesh axis runs over, the one named last changes fastest.
Arguments:
- tokens: bfloat16 [6144, 3072], P('seq'), may hold values from -70 to 70
- survive: int32 [6144], P('seq'), may hold values from 0 to 1, as said below
- norm_gain: float32 [3072], replicated, may hold values from 0.3 to 3
- w_qkv: bfloat16 [3072, 3, 3072], P(None, None, 'head'), may hold values from -0.109375 to 0.109375
- qk_gain: float32 [2, 24, 128], P(None, 'head'), may hold values from 0.5 to 2
- w_out: bfloat16 [3072, 3072], P('head'), may hold values from -0.109375 to 0.109375
Outputs:
- update: bfloat16 [6144, 3072], P('seq', 'head')
The draws below stay inside these ranges and needn't reach their ends.
Inputs may be any that keep to these rules, and one draw needn't show every extreme that they name: `survive`: exactly 3072 tokens run in all. The 384 positions of one sequence shard hold anywhere from none to all 384 running tokens; in every draw some shard holds all 384 and some shard none.
All inputs are finite; a program needn't handle non-finite values.
Results may differ from the reference program's by a relative error of at most 0.015.
Values may be sent and summed in bfloat16 or wider, within the bound.
No kernel may reach another device: no remote copies, remote signals or barrier semaphores. Data moves between devices by JAX's collectives and lax.ppermute only.
A program may use at most 128 MiB of HBM per device.

```python
import math
import jax
import jax.numpy as jnp
from jax import lax

MODEL_WIDTH = 3072
HEAD_COUNT = 24
HEAD_WIDTH = 128
KEEP_DEV = 192
ALL_HEAD_WIDTH = 3072
POS_DEV = 384
WINDOW_LENGTH = 6144
RUNNING_TOKENS = 3072


def draw_tokens(key, part):
    key_base, key_column, key_row = jax.random.split(jax.random.fold_in(key, 23), 3)
    gaussian = jax.random.truncated_normal(key_base, -4.0, 4.0, (WINDOW_LENGTH, MODEL_WIDTH), jnp.float32)
    column_scale = jnp.exp(jax.random.uniform(key_column, (1, MODEL_WIDTH), jnp.float32, math.log(0.3), math.log(3.0)))
    row_scale = jnp.exp(jax.random.uniform(key_row, (WINDOW_LENGTH, 1), jnp.float32, math.log(0.5), math.log(5.0)))
    values = gaussian * column_scale * row_scale
    return values.astype(jnp.bfloat16)


def draw_survive(key, part):
    key_swing, key_order, key_ranks = jax.random.split(jax.random.fold_in(key, 11), 3)
    shard_total = WINDOW_LENGTH // POS_DEV
    pair_count = shard_total // 2
    pair_swing = jax.random.randint(key_swing, (pair_count,), 0, KEEP_DEV + 1)
    pair_swing = pair_swing.at[0].set(KEEP_DEV)
    shard_counts = jnp.concatenate([KEEP_DEV + pair_swing, KEEP_DEV - pair_swing])
    shard_order = jax.random.permutation(key_order, shard_total)
    shard_counts = shard_counts[shard_order]
    position_ranks = jax.vmap(lambda sub_key: jax.random.permutation(sub_key, POS_DEV))(jax.random.split(key_ranks, shard_total))
    alive = (position_ranks < shard_counts[:, None]).astype(jnp.int32)
    return alive.reshape(WINDOW_LENGTH)


def levels(key, shape, cuts, least, top_value):
    level, own = 1.0, jax.random.fold_in(key, 6)
    for position, parts in cuts:
        draws = jnp.exp(jax.random.uniform(jax.random.fold_in(own, position), (parts,), jnp.float32, least / len(cuts), top_value / len(cuts)))
        level = level * jnp.repeat(draws, shape[position] // parts).reshape([-1 if axis == position else 1 for axis in range(len(shape))])
    return level


def normal_values(key, dims, width, bound, shards=(), kind=jnp.bfloat16):
    loudness = levels(key, dims, shards, -0.22, 0.18) if shards else 1.0
    entries = jax.random.normal(key, dims, jnp.float32) * width * loudness
    return jnp.minimum(jnp.maximum(entries, -bound), bound).astype(kind)


def setup_inputs(seed: int = 0) -> dict:
    arg_keys = jax.random.split(jax.random.key(seed), 7)
    return {
        "tokens": draw_tokens(jax.random.fold_in(arg_keys[6], 71), 0),
        "survive": draw_survive(jax.random.fold_in(arg_keys[6], 71), 0),
        "norm_gain": jnp.clip(jnp.exp(jax.random.uniform(arg_keys[2], (MODEL_WIDTH,), jnp.float32, math.log(0.3), math.log(3.0))), 0.3, 3.0),
        "w_qkv": normal_values(arg_keys[3], (MODEL_WIDTH, 3, ALL_HEAD_WIDTH), MODEL_WIDTH ** -0.5, 0.109375, ((2, 2),)),
        "qk_gain": jnp.clip(jnp.exp(math.log(2.0) - 1.3862944 * jax.random.uniform(arg_keys[4], (2, HEAD_COUNT, HEAD_WIDTH), jnp.float32) ** levels(arg_keys[4], (2, HEAD_COUNT, HEAD_WIDTH), ((1, 2),), -0.2, 0.2)), 0.5, 2.0),
        "w_out": normal_values(arg_keys[5], (ALL_HEAD_WIDTH, MODEL_WIDTH), ALL_HEAD_WIDTH ** -0.5, 0.109375, ((0, 2),)),
    }


epsilon = 1e-06

def layer_norm(values, gain):
    center = values - lax.optimization_barrier(jnp.mean(values, axis=-1, keepdims=True))
    spread = lax.optimization_barrier(jnp.mean(center * center, axis=-1, keepdims=True))
    return center * lax.rsqrt(spread + epsilon) * gain

def reference(tokens, survive, norm_gain, w_qkv, qk_gain, w_out):
    running_token_index = jnp.argsort(1 - survive, stable=True)[:RUNNING_TOKENS].astype(jnp.int32)
    source_tokens = tokens[running_token_index].astype(jnp.float32)
    normed = layer_norm(source_tokens, norm_gain).astype(jnp.bfloat16)
    projected_output = jnp.dot(normed, w_qkv.reshape(MODEL_WIDTH, 3 * ALL_HEAD_WIDTH), preferred_element_type=jnp.float32)
    query_rows = projected_output[:, :ALL_HEAD_WIDTH].reshape(RUNNING_TOKENS, HEAD_COUNT, HEAD_WIDTH)
    running_key_rows = projected_output[:, ALL_HEAD_WIDTH:2 * ALL_HEAD_WIDTH].reshape(RUNNING_TOKENS, HEAD_COUNT, HEAD_WIDTH)
    running_value_rows = projected_output[:, 2 * ALL_HEAD_WIDTH:].reshape(RUNNING_TOKENS, HEAD_COUNT, HEAD_WIDTH).astype(jnp.bfloat16)
    query_rows = layer_norm(query_rows, qk_gain[0]).astype(jnp.bfloat16)
    running_key_rows = layer_norm(running_key_rows, qk_gain[1]).astype(jnp.bfloat16)
    score_scale = 1.0 / math.sqrt(HEAD_WIDTH)

    def one_head(stacked):
        head_queries, head_keys, head_values = stacked
        scores = jnp.dot(head_queries, head_keys.T, preferred_element_type=jnp.float32) * score_scale
        weights = jnp.exp(scores)
        denominator = lax.optimization_barrier(jnp.sum(weights, axis=-1))
        numerator = jnp.dot(weights.astype(jnp.bfloat16), head_values, preferred_element_type=jnp.float32)
        return (numerator / denominator[:, None]).astype(jnp.bfloat16)
    split_per_head = lax.map(one_head, (jnp.transpose(query_rows, (1, 0, 2)), jnp.transpose(running_key_rows, (1, 0, 2)), jnp.transpose(running_value_rows, (1, 0, 2))))
    attended_output = jnp.transpose(split_per_head, (1, 0, 2)).reshape(RUNNING_TOKENS, ALL_HEAD_WIDTH)
    attention_branch = jnp.dot(attended_output, w_out, preferred_element_type=jnp.float32)
    return jnp.zeros((WINDOW_LENGTH, MODEL_WIDTH), jnp.bfloat16).at[running_token_index].set(attention_branch.astype(jnp.bfloat16))
```

```python
import functools
import math

import jax
import jax.numpy as jnp
from jax import lax
from jax.experimental import pallas as pl
from jax.experimental.pallas import tpu as pltpu
from jax.sharding import PartitionSpec as P

epsilon = 1e-06
mib = 1 << 20
f32 = jnp.float32
bf16 = jnp.bfloat16


def layer_norm(values, gain):
    center = values - jnp.mean(values, axis=-1, keepdims=True)
    spread = jnp.mean(center * center, axis=-1, keepdims=True)
    return center * lax.rsqrt(spread + epsilon) * gain


def cost(flops, bytes_accessed, exps=0):
    return pl.CostEstimate(
        flops=int(flops), bytes_accessed=int(bytes_accessed), transcendentals=int(exps)
    )


def pack_body(row_ref, col_ref, tokens_ref, gain_ref, normed_ref, back_ref, *, rows):
    positions = tokens_ref.shape[0]
    step = pl.program_id(0)
    first = lax.broadcasted_iota(jnp.int32, (positions, positions), 0)
    second = lax.broadcasted_iota(jnp.int32, (positions, positions), 1)
    live_row = jnp.broadcast_to(row_ref[...].astype(f32), (8, positions))
    upper = (first <= second).astype(f32).astype(bf16)
    rank_row = jnp.dot(live_row.astype(bf16), upper, preferred_element_type=f32)[:1]
    target = jnp.where(live_row[:1] > 0.5, rank_row - 1.0, -1.0).astype(jnp.int32)
    slots = lax.broadcasted_iota(jnp.int32, (rows, positions), 0) + step * rows
    chosen = (slots == target).astype(f32).astype(bf16)
    packed = jnp.dot(chosen, tokens_ref[...], preferred_element_type=f32)
    normed_ref[...] = layer_norm(packed, gain_ref[...]).astype(bf16)

    @pl.when(step == 0)
    def _():
        live_col = jnp.broadcast_to(col_ref[...].astype(f32), (positions, 128))
        lower = (first >= second).astype(f32).astype(bf16)
        rank_col = jnp.dot(lower, live_col.astype(bf16), preferred_element_type=f32)[:, :1]
        home = jnp.where(live_col[:, :1] > 0.5, rank_col - 1.0, -1.0).astype(jnp.int32)
        back_ref[...] = (second == home).astype(f32).astype(bf16)


def pack(tokens, survive, norm_gain):
    positions, width = tokens.shape
    rows = 128 if positions % 128 == 0 else positions
    whole = lambda i: (0, 0)
    return pl.pallas_call(
        functools.partial(pack_body, rows=rows),
        grid=(positions // rows,),
        in_specs=[
            pl.BlockSpec((1, positions), whole),
            pl.BlockSpec((positions, 1), whole),
            pl.BlockSpec((positions, width), whole),
            pl.BlockSpec((1, width), whole),
        ],
        out_specs=[
            pl.BlockSpec((rows, width), lambda i: (i, 0)),
            pl.BlockSpec((positions, positions), whole),
        ],
        out_shape=[
            jax.ShapeDtypeStruct((positions, width), bf16),
            jax.ShapeDtypeStruct((positions, positions), bf16),
        ],
        compiler_params=pltpu.CompilerParams(vmem_limit_bytes=32 * mib),
        cost_estimate=cost(2 * positions * positions * width, 4 * positions * width),
        name="pack",
    )(
        survive.reshape(1, positions),
        survive.reshape(positions, 1),
        tokens,
        norm_gain.reshape(1, width),
    )


def project_body(normed_ref, weight_ref, gain_ref, keyval_ref, query_ref, *, first_head, tile_heads):
    size = query_ref.shape[2]
    tile, kind = pl.program_id(0), pl.program_id(1)
    result = jnp.dot(normed_ref[...], weight_ref[0], preferred_element_type=f32)
    parts = [result[:, i * size : (i + 1) * size] for i in range(tile_heads)]

    def gain(which, i):
        return gain_ref[which, pl.ds(first_head + tile * tile_heads + i, 1), :]

    @pl.when(kind == 0)
    def _():
        for i, part in enumerate(parts):
            keyval_ref[i, :, :size] = layer_norm(part, gain(1, i)).astype(bf16)

    @pl.when(kind == 1)
    def _():
        for i, part in enumerate(parts):
            keyval_ref[i, :, size:] = part.astype(bf16)

    @pl.when(kind == 2)
    def _():
        for i, part in enumerate(parts):
            query_ref[i] = layer_norm(part, gain(0, i)).astype(bf16)


def project(normed, weights, qk_gain, chunk, groups):
    rows, width = normed.shape
    size = qk_gain.shape[2]
    tile_heads = 2 if groups % 2 == 0 else 1
    tiles = groups // tile_heads
    columns = tile_heads * size
    return pl.pallas_call(
        functools.partial(project_body, first_head=chunk * groups, tile_heads=tile_heads),
        grid=(tiles, 3),
        in_specs=[
            pl.BlockSpec((rows, width), lambda n, t: (0, 0)),
            pl.BlockSpec((1, width, columns), lambda n, t: ((t + 1) % 3, 0, chunk * tiles + n)),
            pl.BlockSpec(qk_gain.shape, lambda n, t: (0, 0, 0)),
        ],
        out_specs=[
            pl.BlockSpec((tile_heads, rows, 2 * size), lambda n, t: (n, 0, 0)),
            pl.BlockSpec((tile_heads, rows, size), lambda n, t: (n, 0, 0)),
        ],
        out_shape=[
            jax.ShapeDtypeStruct((groups, rows, 2 * size), bf16),
            jax.ShapeDtypeStruct((groups, rows, size), bf16),
        ],
        compiler_params=pltpu.CompilerParams(vmem_limit_bytes=32 * mib),
        cost_estimate=cost(
            2 * rows * width * 3 * groups * size, 6 * width * groups * size + 2 * rows * width
        ),
        name="project",
    )(normed, weights, qk_gain)


def attend_body(counts_ref, query_ref, *refs, sources, key_room, query_rows, key_cols):
    keyval_refs = refs[:sources]
    out_ref, keys, values, queries, results = refs[sources:]
    groups, rows, size = query_ref.shape
    piece = 128 if rows % 128 == 0 else rows
    scale = math.log2(math.e) / math.sqrt(size)
    align = lambda count: pl.multiple_of((count + 15) // 16 * 16, 16)
    line = lax.broadcasted_iota(jnp.int32, (piece, size), 0)

    def keep(source, block, offset, count):
        for part in range(rows // piece):

            @pl.when(part * piece < count)
            def _():
                here = pl.ds(pl.multiple_of(offset + part * piece, 16), piece)
                there = pl.ds(part * piece, piece)
                keys[here, :] = source[block, there, :size]
                values[here, :size] = source[block, there, size:]
                live = (line + part * piece < count).astype(f32).astype(bf16)
                values[here, size:] = live

        return pl.multiple_of(offset + align(count), 16)

    offset = jnp.int32(0)
    index = 0
    for source in keyval_refs:
        for block in range(source.shape[0]):
            offset = keep(source, block, offset, counts_ref[index])
            index += 1
    total_blocks = index

    def clear(step, carry):
        here = pl.ds(pl.multiple_of(offset + step * 16, 16), 16)
        keys[here, :] = jnp.zeros((16, size), bf16)
        values[here, :] = jnp.zeros((16, 2 * size), bf16)
        return carry

    lax.fori_loop(0, (key_room - offset) // 16, clear, 0)

    starts = []
    start = jnp.int32(0)
    for block in range(groups):
        count = counts_ref[total_blocks + block]
        starts.append(start)
        for part in range(rows // piece):

            @pl.when(part * piece < count)
            def _():
                here = pl.ds(pl.multiple_of(start + part * piece, 16), piece)
                queries[here, :] = query_ref[block, part * piece : (part + 1) * piece, :]

        start = pl.multiple_of(start + align(count), 16)

    def one_tile(tile, carry):
        here = pl.ds(pl.multiple_of(tile * query_rows, query_rows), query_rows)
        query = queries[here, :]
        total = jnp.zeros((query_rows, 2 * size), f32)
        for low in range(0, key_room, key_cols):
            high = min(low + key_cols, key_room)
            scores = lax.dot_general(
                query, keys[low:high, :], (((1,), (1,)), ((), ())), preferred_element_type=f32
            )
            weights = jnp.exp2(scores * scale).astype(bf16)
            total += jnp.dot(weights, values[low:high, :], preferred_element_type=f32)
        results[here, :] = (total[:, :size] / total[:, size:]).astype(bf16)
        return carry

    lax.fori_loop(0, (start + query_rows - 1) // query_rows, one_tile, 0)

    for block in range(groups):
        count = counts_ref[total_blocks + block]
        for part in range(rows // piece):
            here = pl.ds(pl.multiple_of(starts[block] + part * piece, 16), piece)
            found = results[here, :]
            live = line + part * piece < count
            out_ref[block, part * piece : (part + 1) * piece, :] = jnp.where(
                live, found.astype(f32), 0.0
            ).astype(bf16)


def attend(counts, query, keyvals, shards):
    groups, rows, size = query.shape
    running = shards * rows // 2
    key_room = -(-(running + 16 * shards) // 256) * 256
    query_rows = 256
    query_room = -(-groups * rows // query_rows) * query_rows + rows
    sources = len(keyvals)
    return pl.pallas_call(
        functools.partial(
            attend_body,
            sources=sources,
            key_room=key_room,
            query_rows=query_rows,
            key_cols=512,
        ),
        in_specs=[pl.BlockSpec(memory_space=pltpu.SMEM)]
        + [pl.BlockSpec(memory_space=pltpu.VMEM)] * (1 + sources),
        out_specs=pl.BlockSpec(memory_space=pltpu.VMEM),
        out_shape=jax.ShapeDtypeStruct((groups, rows, size), bf16),
        scratch_shapes=[
            pltpu.VMEM((key_room + rows, size), bf16),
            pltpu.VMEM((key_room + rows, 2 * size), bf16),
            pltpu.VMEM((query_room, size), bf16),
            pltpu.VMEM((query_room, size), bf16),
        ],
        compiler_params=pltpu.CompilerParams(vmem_limit_bytes=40 * mib),
        cost_estimate=cost(
            8 * groups * rows // 2 * running * size,
            4 * shards * rows * size,
            groups * rows // 2 * running,
        ),
        name="attend",
    )(counts, query, *keyvals)


def finish_body(place_ref, *refs, others, has_sum, last):
    refs = list(refs)
    out_ref = refs.pop()
    step = pl.program_id(0)
    total = refs.pop(0)[...] if has_sum else None

    def add(total, attended_ref, weight):
        groups = attended_ref.shape[0]
        wide = jnp.concatenate([attended_ref[g] for g in range(groups)], axis=-1)
        term = jnp.dot(wide, weight, preferred_element_type=f32)
        return term if total is None else total + term

    total = add(total, refs[0], refs[1][...])
    for m in range(others):
        attended_ref, near_ref, far_ref = refs[2 + 3 * m : 5 + 3 * m]
        total = add(total, attended_ref, jnp.where(step == 0, near_ref[...], far_ref[...]))
    if last:
        rounded = total.astype(bf16)
        out_ref[...] = jnp.dot(refs[-1][...], rounded, preferred_element_type=f32).astype(bf16)
    else:
        out_ref[...] = total


def column_split(out_width):
    return 2 if out_width % 256 == 0 else 1


def finish(place, total, attended, w_out, other_attended, other_weights, back, chunk, out_width):
    groups, rows, size = attended.shape
    split = column_split(out_width)
    half = out_width // split
    depth = groups * size
    mine = lambda i, place: (0, lax.bitwise_xor(place[0], i))
    block_a = pl.BlockSpec((groups, rows, size), lambda i, place: (0, 0, 0))
    block_w = pl.BlockSpec((depth, half), lambda i, place: (chunk, 0))
    specs, operands = [], []
    if total is not None:
        specs.append(pl.BlockSpec((rows, half), mine))
        operands.append(total)
    specs += [
        block_a,
        pl.BlockSpec(
            (depth, half), lambda i, place: (chunk, split * place[1] + lax.bitwise_xor(place[0], i))
        ),
    ]
    operands += [attended, w_out]
    for other, (near, far) in zip(other_attended, other_weights):
        specs += [block_a, block_w, block_w]
        operands += [other, near, far]
    if back is not None:
        specs.append(pl.BlockSpec(back.shape, lambda i, place: (0, 0)))
        operands.append(back)
    last = back is not None
    count = 1 + len(other_attended)
    return pl.pallas_call(
        functools.partial(
            finish_body, others=len(other_attended), has_sum=total is not None, last=last
        ),
        grid_spec=pltpu.PrefetchScalarGridSpec(
            num_scalar_prefetch=1,
            grid=(split,),
            in_specs=specs,
            out_specs=pl.BlockSpec((rows, half), mine),
        ),
        out_shape=jax.ShapeDtypeStruct((rows, out_width), bf16 if last else f32),
        compiler_params=pltpu.CompilerParams(vmem_limit_bytes=40 * mib),
        cost_estimate=cost(
            2 * rows * depth * count * out_width, 2 * depth * count * out_width + 8 * rows * out_width
        ),
        name="finish",
    )(place, *operands)


def flip(values, axis, mask):
    size = lax.axis_size(axis)
    return lax.ppermute(values, axis, [(i, i ^ mask) for i in range(size)])


def gather_counts(count):
    shards = lax.axis_size("seq")
    found = count.reshape(1)
    mask = 1
    while mask < shards:
        found = jnp.concatenate([found, flip(found, "seq", mask)])
        mask *= 2
    return found


def per_device(tokens, survive, norm_gain, w_qkv, qk_gain, w_out):
    positions = tokens.shape[0]
    heads, size = qk_gain.shape[1], qk_gain.shape[2]
    shards, head_shards = lax.axis_size("seq"), lax.axis_size("head")
    out_width = w_out.shape[1] // head_shards
    split = column_split(out_width)
    half = out_width // split
    groups = math.gcd(heads & -heads, shards)
    ring = shards // groups
    chunks = heads // groups
    me, side = lax.axis_index("seq"), lax.axis_index("head")
    core = me % split
    teams = [[r + ring * g for g in range(groups)] for r in range(ring)]

    def swap(values):
        if groups == 1:
            return values
        return lax.all_to_all(
            values, "seq", split_axis=0, concat_axis=0, axis_index_groups=teams, tiled=True
        )

    counts_by_mask = gather_counts(jnp.sum(survive))
    plane = me // ring
    masks = list(range(ring))
    wanted = jnp.array(
        [mask for mask in masks for _ in range(groups)] + [0] * groups, jnp.int32
    ) + ring * lax.bitwise_xor(
        jnp.array(list(range(groups)) * (ring + 1), jnp.int32), plane.astype(jnp.int32)
    )
    counts = counts_by_mask[wanted]

    normed, back = pack(tokens, survive, norm_gain)
    weights = jnp.transpose(w_qkv, (1, 0, 2))

    other_weights = []
    for mask in range(1, head_shards):
        column = lax.bitwise_xor(side, mask) * out_width + core * half
        near = flip(
            lax.dynamic_slice(w_out, (0, column), (w_out.shape[0], half)), "head", mask
        )
        other_weights.append((near, flip(near, "seq", 1) if split == 2 else near))

    place = jnp.stack([core, side]).astype(jnp.int32)
    total = None
    for chunk in range(chunks):
        keyval, query = project(normed, weights, qk_gain, chunk, groups)
        keyval = swap(keyval)
        query = swap(query)
        blocks = {0: keyval}
        mask = ring // 2
        while mask:
            for found in list(blocks):
                blocks[found | mask] = flip(blocks[found], "seq", mask)
            mask //= 2
        attended = attend(counts, query, [blocks[mask] for mask in masks], shards)
        attended = swap(attended)
        others = [flip(attended, "head", mask) for mask in range(1, head_shards)]
        total = finish(
            place,
            total,
            attended,
            w_out,
            others,
            other_weights,
            back if chunk == chunks - 1 else None,
            chunk,
            out_width,
        )
    return total


def solution(mesh):
    placed = (
        P("seq", None),
        P("seq"),
        P(),
        P(None, None, "head"),
        P(None, "head", None),
        P("head", None),
    )
    return jax.shard_map(
        per_device, mesh=mesh, in_specs=placed, out_specs=P("seq", "head"), check_vma=False
    )
```

```python
import functools
import math

import jax
import jax.numpy as jnp
from jax import lax
from jax.experimental import pallas as pl
from jax.experimental.pallas import tpu as pltpu
from jax.sharding import PartitionSpec as P

epsilon = 1e-06
dead_mark = 1e30
dead_limit = 1e15
mib = 1 << 20
f32 = jnp.float32
bf16 = jnp.bfloat16
params = pltpu.CompilerParams(vmem_limit_bytes=60 * mib)


def cost(flops, bytes_accessed, exps=0):
    return pl.CostEstimate(
        flops=int(flops), bytes_accessed=int(bytes_accessed), transcendentals=int(exps)
    )


def flip(values, axis, mask):
    size = lax.axis_size(axis)
    return lax.ppermute(values, axis, [(i, i ^ mask) for i in range(size)])


def pack_body(survive_ref, tokens_ref, gain_ref, normed_ref, back_ref, count_ref, *, rows):
    positions = tokens_ref.shape[0]
    step = pl.program_id(0)
    first = lax.broadcasted_iota(jnp.int32, (positions, positions), 0)
    second = lax.broadcasted_iota(jnp.int32, (positions, positions), 1)
    live = jnp.broadcast_to(survive_ref[...].reshape(1, positions), (8, positions)).astype(f32)
    upper = (first <= second).astype(f32).astype(bf16)
    rank = jnp.dot(live.astype(bf16), upper, preferred_element_type=f32)
    target = jnp.where(live > 0.5, rank - 1.0, -1.0)
    slots = lax.broadcasted_iota(jnp.int32, (rows, positions), 0) + step * rows
    chosen = (slots == target[:1].astype(jnp.int32)).astype(f32).astype(bf16)
    packed = jnp.dot(chosen, tokens_ref[...], preferred_element_type=f32)
    center = packed - jnp.mean(packed, axis=-1, keepdims=True)
    spread = jnp.mean(center * center, axis=-1, keepdims=True)
    gain = gain_ref[...].reshape(1, gain_ref.shape[0])
    normed_ref[...] = (center * lax.rsqrt(spread + epsilon) * gain).astype(bf16)

    @pl.when(step == 0)
    def _():
        home = jnp.transpose(target)[:, :1].astype(jnp.int32)
        back_ref[...] = (second == home).astype(f32).astype(bf16)
        count_ref[0, 0] = jnp.max(rank).astype(jnp.int32)


def pack(tokens, survive, norm_gain):
    positions, width = tokens.shape
    rows = 128 if positions % 128 == 0 else positions
    return pl.pallas_call(
        functools.partial(pack_body, rows=rows),
        grid=(positions // rows,),
        in_specs=[
            pl.BlockSpec((positions,), lambda i: (0,)),
            pl.BlockSpec((positions, width), lambda i: (0, 0)),
            pl.BlockSpec((width,), lambda i: (0,)),
        ],
        out_specs=[
            pl.BlockSpec((rows, width), lambda i: (i, 0)),
            pl.BlockSpec((positions, positions), lambda i: (0, 0)),
            pl.BlockSpec(memory_space=pltpu.SMEM),
        ],
        out_shape=[
            jax.ShapeDtypeStruct((positions, width), bf16),
            jax.ShapeDtypeStruct((positions, positions), bf16),
            jax.ShapeDtypeStruct((1, 1), jnp.int32),
        ],
        compiler_params=params,
        cost_estimate=cost(2 * positions * positions * width, 4 * positions * width),
        name="pack",
    )(survive, tokens, norm_gain)


def project_body(place_ref, count_ref, normed_ref, weight_ref, gain_ref, *refs, kinds, chunks, groups, pair):
    outs, result_ref = list(refs[:-1]), refs[-1]
    keyval_refs = outs[:groups] if 1 in kinds else []
    query_refs = outs[-groups:] if 0 in kinds else []
    rows = normed_ref.shape[0]
    size = gain_ref.shape[2]
    wide = pair * size
    plane = place_ref[0]
    tile = lax.bitwise_xor(pl.program_id(1), plane // pair)
    head = (chunks[0] + pl.program_id(0)) * groups + tile * pair

    def write(refs, low, values, steps):
        result_ref[...] = values
        for n in range(groups // pair):

            @pl.when(pl.program_id(1) == n)
            def _():
                for i in range(pair):
                    start = pl.multiple_of(lax.bitwise_xor(plane % pair, i) * size, size)
                    found = result_ref[:, pl.ds(start, size)].astype(bf16)
                    refs[n * pair + i][0, :, low : low + size] = found

    for step, kind in enumerate(kinds):

        @pl.when(pl.program_id(2) == step)
        def _():
            result = jnp.dot(normed_ref[...], weight_ref[0], preferred_element_type=f32)
            if kind == 2:
                write(keyval_refs, size, result, step)
                return
            of_row = lax.broadcasted_iota(jnp.int32, (wide, wide), 0) // size
            of_col = lax.broadcasted_iota(jnp.int32, (wide, wide), 1) // size
            average = jnp.where(of_row == of_col, 1.0 / size, 0.0).astype(bf16)

            def mean(values):
                coarse = values.astype(bf16)
                fine = (values - coarse.astype(f32)).astype(bf16)
                return jnp.dot(coarse, average, preferred_element_type=f32) + jnp.dot(
                    fine, average, preferred_element_type=f32
                )

            center = result - mean(result)
            gain = jnp.concatenate(
                [gain_ref[head + i, kind : kind + 1, :] for i in range(pair)], axis=-1
            )
            if kind == 0:
                gain = gain * (1.0 / math.sqrt(size))
            normed = center * lax.rsqrt(mean(center * center) + epsilon) * gain
            if kind == 1:
                row = lax.broadcasted_iota(jnp.int32, (rows, wide), 0)
                normed = jnp.where(row < count_ref[0, 0], normed, dead_mark)
                write(keyval_refs, 0, normed, step)
            else:
                write(query_refs, 0, normed, step)


def project(place, count, normed, weights, gains, kinds, chunks, groups):
    rows, width = normed.shape
    size = gains.shape[2]
    pair = 2 if groups % 2 == 0 else 1
    tiles = groups // pair
    columns = pair * size

    def weight_index(c, n, t, place):
        kind = 0
        for step, value in enumerate(kinds):
            kind = jnp.where(t == step, value, kind)
        tile = lax.bitwise_xor(n, place[0] // pair)
        return (kind, 0, (chunks[0] + c) * tiles + tile)

    widths = ([2 * size] * groups if 1 in kinds else []) + ([size] * groups if 0 in kinds else [])
    found = pl.pallas_call(
        functools.partial(project_body, kinds=kinds, chunks=chunks, groups=groups, pair=pair),
        grid_spec=pltpu.PrefetchScalarGridSpec(
            num_scalar_prefetch=1,
            grid=(len(chunks), tiles, len(kinds)),
            in_specs=[
                pl.BlockSpec(memory_space=pltpu.SMEM),
                pl.BlockSpec((rows, width), lambda c, n, t, place: (0, 0)),
                pl.BlockSpec((1, width, columns), weight_index),
                pl.BlockSpec(gains.shape, lambda c, n, t, place: (0, 0, 0)),
            ],
            out_specs=[
                pl.BlockSpec((1, rows, wide), lambda c, n, t, place: (c, 0, 0)) for wide in widths
            ],
            scratch_shapes=[pltpu.VMEM((rows, columns), f32)],
        ),
        out_shape=[jax.ShapeDtypeStruct((len(chunks), rows, wide), bf16) for wide in widths],
        compiler_params=params,
        cost_estimate=cost(
            2 * rows * width * len(kinds) * len(chunks) * groups * size,
            2 * width * len(kinds) * len(chunks) * groups * size + 2 * rows * width,
        ),
        name="project",
    )(place, count, normed, weights, gains)
    keyval = found[:groups] if 1 in kinds else None
    query = found[-groups:] if 0 in kinds else None
    return keyval, query


def attend_body(*refs, groups, sources, key_room, query_rows, key_cols):
    query_refs = refs[:groups]
    keyval_refs = refs[groups : groups + sources]
    out_refs = refs[groups + sources : 2 * groups + sources]
    keys, values, queries, results = refs[2 * groups + sources :]
    rows, size = query_refs[0].shape[1:]
    piece = 128 if rows % 128 == 0 else rows
    align = lambda count: pl.multiple_of((count + 15) // 16 * 16, 16)
    line = lax.broadcasted_iota(jnp.int32, (piece, size), 0)

    counts = []
    for source in keyval_refs:
        for block in range(source.shape[0]):
            live = (source[block, :, :size].astype(f32) < dead_limit).astype(f32)
            counts.append(jnp.max(jnp.sum(live, axis=0, keepdims=True)).astype(jnp.int32))

    offset = jnp.int32(0)
    index = 0
    for source in keyval_refs:
        for block in range(source.shape[0]):
            count = counts[index]
            for part in range(rows // piece):

                @pl.when(part * piece < count)
                def _():
                    here = pl.ds(pl.multiple_of(offset + part * piece, 16), piece)
                    there = pl.ds(part * piece, piece)
                    live = line + part * piece < count
                    found = jnp.where(live, source[block, there, :size].astype(f32), 0.0)
                    keys[here, :] = found.astype(bf16)
                    values[here, :size] = source[block, there, size:]
                    values[here, size:] = live.astype(f32).astype(bf16)

            offset = pl.multiple_of(offset + align(count), 16)
            index += 1

    def clear(step, carry):
        here = pl.ds(pl.multiple_of(offset + step * 16, 16), 16)
        keys[here, :] = jnp.zeros((16, size), bf16)
        values[here, :] = jnp.zeros((16, 2 * size), bf16)
        return carry

    lax.fori_loop(0, (key_room - offset) // 16, clear, 0)

    starts = []
    start = jnp.int32(0)
    for block in range(groups):
        starts.append(start)
        for part in range(rows // piece):

            @pl.when(part * piece < counts[block])
            def _():
                here = pl.ds(pl.multiple_of(start + part * piece, 16), piece)
                queries[here, :] = query_refs[block][0, part * piece : (part + 1) * piece, :]

        start = pl.multiple_of(start + align(counts[block]), 16)

    def one_tile(tile, carry):
        here = pl.ds(pl.multiple_of(tile * query_rows, query_rows), query_rows)
        query = queries[here, :]
        total = jnp.zeros((query_rows, 2 * size), f32)
        for low in range(0, key_room, key_cols):
            high = min(low + key_cols, key_room)
            scores = lax.dot_general(
                query, keys[low:high, :], (((1,), (1,)), ((), ())), preferred_element_type=f32
            )
            weights = jnp.exp(scores).astype(bf16)
            total += jnp.dot(weights, values[low:high, :], preferred_element_type=f32)
        results[here, :] = (total[:, :size] / total[:, size:]).astype(bf16)
        return carry

    lax.fori_loop(0, (start + query_rows - 1) // query_rows, one_tile, 0)

    for block in range(groups):
        for part in range(rows // piece):
            here = pl.ds(pl.multiple_of(starts[block] + part * piece, 16), piece)
            live = line + part * piece < counts[block]
            out_refs[block][0, part * piece : (part + 1) * piece, :] = jnp.where(
                live, results[here, :].astype(f32), 0.0
            ).astype(bf16)


def attend(queries, which, keyvals, shards):
    groups = len(queries)
    rows, size = queries[0].shape[1:]
    running = shards * rows // 2
    key_room = -(-(running + 16 * shards) // 256) * 256
    query_rows = 256
    query_room = -(-groups * rows // query_rows) * query_rows + rows
    return pl.pallas_call(
        functools.partial(
            attend_body,
            groups=groups,
            sources=len(keyvals),
            key_room=key_room,
            query_rows=query_rows,
            key_cols=512,
        ),
        grid=(1,),
        in_specs=[pl.BlockSpec((1, rows, size), lambda i: (which, 0, 0))] * groups
        + [pl.BlockSpec(keyval.shape, lambda i: (0, 0, 0)) for keyval in keyvals],
        out_specs=[pl.BlockSpec((1, rows, size), lambda i: (0, 0, 0))] * groups,
        out_shape=[jax.ShapeDtypeStruct((1, rows, size), bf16)] * groups,
        scratch_shapes=[
            pltpu.VMEM((key_room + rows, size), bf16),
            pltpu.VMEM((key_room + rows, 2 * size), bf16),
            pltpu.VMEM((query_room, size), bf16),
            pltpu.VMEM((query_room, size), bf16),
        ],
        compiler_params=params,
        cost_estimate=cost(
            8 * groups * rows // 2 * running * size,
            4 * shards * rows * size,
            groups * rows // 2 * running,
        ),
        name="attend",
    )(*queries, *keyvals)


def finish_body(place_ref, *refs, others, has_sum, last):
    refs = list(refs)
    wide_ref = refs.pop()
    out_ref = refs.pop()
    plane = place_ref[0]
    total = refs.pop(0)[...] if has_sum else None
    groups, rows, size = refs[0].shape

    def gathered(attended_ref, slot):
        for g in range(groups):
            start = pl.multiple_of(lax.bitwise_xor(plane, g) * size, size)
            wide_ref[slot, :, pl.ds(start, size)] = attended_ref[g]

    @pl.when((pl.program_id(0) == 0) & (pl.program_id(1) == 0))
    def _():
        gathered(refs[0], 0)
        for m in range(others):
            gathered(refs[2 + 3 * m], 1 + m)

    def add(total, slot, weight):
        term = jnp.dot(wide_ref[slot], weight, preferred_element_type=f32)
        return term if total is None else total + term

    total = add(total, 0, refs[1][...])
    for m in range(others):
        near_ref, far_ref = refs[3 + 3 * m : 5 + 3 * m]
        total = add(total, 1 + m, jnp.where(pl.program_id(0) == 0, near_ref[...], far_ref[...]))
    if last:
        rounded = total.astype(bf16)
        out_ref[...] = jnp.dot(refs[-1][...], rounded, preferred_element_type=f32).astype(bf16)
    else:
        out_ref[...] = total


def column_split(out_width):
    return 2 if out_width % 256 == 0 else 1


def finish(place, total, attended, w_out, other_attended, other_weights, back, chunk, out_width):
    groups, rows, size = attended.shape
    split = column_split(out_width)
    half = out_width // split
    parts = column_split(half)
    tile = half // parts
    depth = groups * size
    column = lambda i, s, place: lax.bitwise_xor(place[1], i) * parts + s
    mine = lambda i, s, place: (0, column(i, s, place))
    own = lambda i, s, place: (chunk, place[2] * split * parts + column(i, s, place))
    near = lambda i, s, place: (chunk, jnp.where(i == 0, s, parts - 1))
    far = lambda i, s, place: (chunk, jnp.where(i == 0, 0, s))
    block_a = pl.BlockSpec((groups, rows, size), lambda i, s, place: (0, 0, 0))
    specs, operands = [], []
    if total is not None:
        specs.append(pl.BlockSpec((rows, tile), mine))
        operands.append(total)
    specs += [block_a, pl.BlockSpec((depth, tile), own)]
    operands += [attended, w_out]
    for other, weights in zip(other_attended, other_weights):
        specs += [block_a, pl.BlockSpec((depth, tile), near), pl.BlockSpec((depth, tile), far)]
        operands += [other, *weights]
    if back is not None:
        specs.append(pl.BlockSpec(back.shape, lambda i, s, place: (0, 0)))
        operands.append(back)
    last = back is not None
    count = 1 + len(other_attended)
    return pl.pallas_call(
        functools.partial(
            finish_body, others=len(other_attended), has_sum=total is not None, last=last
        ),
        grid_spec=pltpu.PrefetchScalarGridSpec(
            num_scalar_prefetch=1,
            grid=(split, parts),
            in_specs=specs,
            out_specs=pl.BlockSpec((rows, tile), mine),
            scratch_shapes=[pltpu.VMEM((count, rows, depth), bf16)],
        ),
        out_shape=jax.ShapeDtypeStruct((rows, out_width), bf16 if last else f32),
        compiler_params=params,
        cost_estimate=cost(
            2 * rows * depth * count * out_width, 2 * depth * count * out_width + 8 * rows * out_width
        ),
        name="finish",
    )(place, *operands)


def per_device(tokens, survive, norm_gain, w_qkv, qk_gain, w_out):
    heads = qk_gain.shape[1]
    shards, head_shards = lax.axis_size("seq"), lax.axis_size("head")
    out_width = w_out.shape[1] // head_shards
    split = column_split(out_width)
    half = out_width // split
    groups = math.gcd(heads & -heads, shards & -shards)
    ring = shards // groups
    chunks = heads // groups
    me, side = lax.axis_index("seq"), lax.axis_index("head")
    core = me % split
    place = jnp.stack([me // ring, core, side]).astype(jnp.int32)

    def swap(blocks):
        return [blocks[0]] + [flip(blocks[k], "seq", k * ring) for k in range(1, groups)]

    def after(values, blocks):
        return lax.optimization_barrier((values, blocks[1]))[0] if groups > 1 else values

    def everywhere(blocks):
        found = {0: jnp.concatenate(blocks) if groups > 1 else blocks[0]}
        mask = ring // 2
        while mask:
            for known in list(found):
                found[known | mask] = flip(found[known], "seq", mask)
            mask //= 2
        return [found[mask] for mask in range(ring)]

    normed, back, count = pack(tokens, survive, norm_gain)
    weights = jnp.transpose(w_qkv, (1, 0, 2))
    gains = jnp.transpose(qk_gain, (1, 0, 2))
    produce = functools.partial(project, place, count)

    keyval, query = produce(normed, weights, gains, (1, 2, 0), (0,), groups)
    keyval, query = swap(keyval), swap(query)
    keyvals, queries = [keyval], [(query, 0)]
    for chunk in range(1, chunks):
        keyval, _ = produce(after(normed, keyval), weights, gains, (1, 2), (chunk,), groups)
        keyval = swap(keyval)
        keyvals.append(keyval)
    if chunks > 1:
        rest = tuple(range(1, chunks))
        _, query = produce(after(normed, keyval), weights, gains, (0,), rest, groups)
        query = swap(query)
        queries += [(query, i) for i in range(chunks - 1)]

    other_weights = []
    for mask in range(1, head_shards):
        column = lax.bitwise_xor(side, mask) * out_width + core * half
        near = flip(lax.dynamic_slice(w_out, (0, column), (w_out.shape[0], half)), "head", mask)
        other_weights.append((near, flip(near, "seq", 1) if split == 2 else near))

    total = None
    for chunk in range(chunks):
        query, which = queries[chunk]
        attended = swap(attend(query, which, everywhere(keyvals[chunk]), shards))
        attended = jnp.concatenate(attended) if groups > 1 else attended[0]
        others = [flip(attended, "head", mask) for mask in range(1, head_shards)]
        total = finish(
            place,
            total,
            attended,
            w_out,
            others,
            other_weights,
            back if chunk == chunks - 1 else None,
            chunk,
            out_width,
        )
    return total


def solution(mesh):
    placed = (
        P("seq", None),
        P("seq"),
        P(),
        P(None, None, "head"),
        P(None, "head", None),
        P("head", None),
    )
    return jax.shard_map(
        per_device, mesh=mesh, in_specs=placed, out_specs=P("seq", "head"), check_vma=False
    )
```

```python
import functools
import math

import jax
import jax.numpy as jnp
from jax import lax
from jax.experimental import pallas as pl
from jax.experimental.pallas import tpu as pltpu
from jax.sharding import PartitionSpec as P

epsilon = 1e-06
dead_mark = 1e30
dead_limit = 1e15
mib = 1 << 20
f32 = jnp.float32
bf16 = jnp.bfloat16
params = pltpu.CompilerParams(vmem_limit_bytes=60 * mib)


def cost(flops, bytes_accessed, exps=0):
    return pl.CostEstimate(
        flops=int(flops), bytes_accessed=int(bytes_accessed), transcendentals=int(exps)
    )


def flip(values, axis, mask):
    size = lax.axis_size(axis)
    return lax.ppermute(values, axis, [(i, i ^ mask) for i in range(size)])


def pack_body(survive_ref, tokens_ref, gain_ref, normed_ref, back_ref, count_ref, *, rows):
    positions = tokens_ref.shape[0]
    step = pl.program_id(0)
    first = lax.broadcasted_iota(jnp.int32, (positions, positions), 0)
    second = lax.broadcasted_iota(jnp.int32, (positions, positions), 1)
    live = jnp.broadcast_to(survive_ref[...].reshape(1, positions), (8, positions)).astype(f32)
    upper = (first <= second).astype(f32).astype(bf16)
    rank = jnp.dot(live.astype(bf16), upper, preferred_element_type=f32)
    target = jnp.where(live > 0.5, rank - 1.0, -1.0)
    slots = lax.broadcasted_iota(jnp.int32, (rows, positions), 0) + step * rows
    chosen = (slots == target[:1].astype(jnp.int32)).astype(f32).astype(bf16)
    packed = jnp.dot(chosen, tokens_ref[...], preferred_element_type=f32)
    center = packed - jnp.mean(packed, axis=-1, keepdims=True)
    spread = jnp.mean(center * center, axis=-1, keepdims=True)
    gain = gain_ref[...].reshape(1, gain_ref.shape[0])
    normed_ref[...] = (center * lax.rsqrt(spread + epsilon) * gain).astype(bf16)

    @pl.when(step == 0)
    def _():
        home = jnp.transpose(target)[:, :1].astype(jnp.int32)
        back_ref[...] = (second == home).astype(f32).astype(bf16)
        count_ref[0, 0] = jnp.max(rank).astype(jnp.int32)


def pack(tokens, survive, norm_gain):
    positions, width = tokens.shape
    rows = 128 if positions % 128 == 0 else positions
    return pl.pallas_call(
        functools.partial(pack_body, rows=rows),
        grid=(positions // rows,),
        in_specs=[
            pl.BlockSpec((positions,), lambda i: (0,)),
            pl.BlockSpec((positions, width), lambda i: (0, 0)),
            pl.BlockSpec((width,), lambda i: (0,)),
        ],
        out_specs=[
            pl.BlockSpec((rows, width), lambda i: (i, 0)),
            pl.BlockSpec((positions, positions), lambda i: (0, 0)),
            pl.BlockSpec(memory_space=pltpu.SMEM),
        ],
        out_shape=[
            jax.ShapeDtypeStruct((positions, width), bf16),
            jax.ShapeDtypeStruct((positions, positions), bf16),
            jax.ShapeDtypeStruct((1, 1), jnp.int32),
        ],
        compiler_params=params,
        cost_estimate=cost(2 * positions * positions * width, 4 * positions * width),
        name="pack",
    )(survive, tokens, norm_gain)


def project_body(place_ref, count_ref, normed_ref, weight_ref, gain_ref, *refs, kinds, chunks, groups):
    outs, result_ref = refs[:-1], refs[-1]
    rows = normed_ref.shape[0]
    size = gain_ref.shape[2]
    plane = place_ref[0]
    first = (chunks[0] + pl.program_id(0)) * groups
    for step, kind in enumerate(kinds):

        @pl.when(pl.program_id(1) == step)
        def _():
            result = jnp.dot(normed_ref[...], weight_ref[0], preferred_element_type=f32)
            for g in range(groups):
                part = result[:, g * size : (g + 1) * size]
                if kind != 2:
                    gain = gain_ref[first + g, kind : kind + 1, :]
                    if kind == 0:
                        gain = gain * (1.0 / math.sqrt(size))
                    center = part - jnp.mean(part, axis=-1, keepdims=True)
                    spread = jnp.mean(center * center, axis=-1, keepdims=True)
                    part = center * lax.rsqrt(spread + epsilon) * gain
                if kind == 1:
                    row = lax.broadcasted_iota(jnp.int32, (rows, size), 0)
                    part = jnp.where(row < count_ref[0, 0], part, dead_mark)
                result_ref[:, g * size : (g + 1) * size] = part.astype(bf16)
            for k in range(groups):
                start = pl.multiple_of(lax.bitwise_xor(plane, k) * size, size)
                outs[k][0, :, step * size : (step + 1) * size] = result_ref[:, pl.ds(start, size)]


def project(place, count, normed, weights, gains, kinds, chunks, groups):
    rows, width = normed.shape
    size = gains.shape[2]
    columns = groups * size
    wide = len(kinds) * size

    def weight_index(c, t, place):
        kind = 0
        for step, value in enumerate(kinds):
            kind = jnp.where(t == step, value, kind)
        return (kind, 0, chunks[0] + c)

    return pl.pallas_call(
        functools.partial(project_body, kinds=kinds, chunks=chunks, groups=groups),
        grid_spec=pltpu.PrefetchScalarGridSpec(
            num_scalar_prefetch=1,
            grid=(len(chunks), len(kinds)),
            in_specs=[
                pl.BlockSpec(memory_space=pltpu.SMEM),
                pl.BlockSpec((rows, width), lambda c, t, place: (0, 0)),
                pl.BlockSpec((1, width, columns), weight_index),
                pl.BlockSpec(gains.shape, lambda c, t, place: (0, 0, 0)),
            ],
            out_specs=[pl.BlockSpec((1, rows, wide), lambda c, t, place: (c, 0, 0))] * groups,
            scratch_shapes=[pltpu.VMEM((rows, columns), bf16)],
        ),
        out_shape=[jax.ShapeDtypeStruct((len(chunks), rows, wide), bf16)] * groups,
        compiler_params=params,
        cost_estimate=cost(
            2 * rows * width * len(kinds) * len(chunks) * columns,
            2 * width * len(kinds) * len(chunks) * columns + 2 * rows * width,
        ),
        name="project",
    )(place, count, normed, weights, gains)


def attend_body(place_ref, *refs, groups, low_lane, key_room, query_rows, key_cols):
    query_refs = refs[:groups]
    keyval_ref, out_ref, keys, values, queries, results, counts = refs[groups:]
    blocks = keyval_ref.shape[0]
    rows, size = out_ref.shape[1:]
    plane, place = place_ref[0], place_ref[1]
    piece = 128 if rows % 128 == 0 else rows
    align = lambda count: pl.multiple_of((count + 15) // 16 * 16, 16)
    line = lax.broadcasted_iota(jnp.int32, (piece, size), 0)

    found = []
    for block in range(blocks):
        live = (keyval_ref[block, :, :size].astype(f32) < dead_limit).astype(f32)
        found.append(jnp.max(jnp.sum(live, axis=0, keepdims=True)).astype(jnp.int32))
        counts[block] = found[block]

    offset = jnp.int32(0)
    for block in range(blocks):
        count = found[block]
        for part in range(rows // piece):

            @pl.when(part * piece < count)
            def _():
                here = pl.ds(pl.multiple_of(offset + part * piece, 16), piece)
                there = pl.ds(part * piece, piece)
                live = line + part * piece < count
                key = jnp.where(live, keyval_ref[block, there, :size].astype(f32), 0.0)
                keys[here, :] = key.astype(bf16)
                values[here, :size] = keyval_ref[block, there, size:]
                values[here, size:] = live.astype(f32).astype(bf16)

        offset = pl.multiple_of(offset + align(count), 16)

    def clear(step, carry):
        here = pl.ds(pl.multiple_of(offset + step * 16, 16), 16)
        keys[here, :] = jnp.zeros((16, size), bf16)
        values[here, :] = jnp.zeros((16, 2 * size), bf16)
        return carry

    lax.fori_loop(0, (key_room - offset) // 16, clear, 0)

    mine = [counts[place * groups + k] for k in range(groups)]
    starts = []
    start = jnp.int32(0)
    for k in range(groups):
        starts.append(start)
        for part in range(rows // piece):

            @pl.when(part * piece < mine[k])
            def _():
                here = pl.ds(pl.multiple_of(start + part * piece, 16), piece)
                there = pl.ds(part * piece, piece)
                queries[here, :] = query_refs[k][0, there, low_lane : low_lane + size]

        start = pl.multiple_of(start + align(mine[k]), 16)

    def one_tile(tile, carry):
        here = pl.ds(pl.multiple_of(tile * query_rows, query_rows), query_rows)
        query = queries[here, :]
        total = jnp.zeros((query_rows, 2 * size), f32)
        for low in range(0, key_room, key_cols):
            high = min(low + key_cols, key_room)
            scores = lax.dot_general(
                query, keys[low:high, :], (((1,), (1,)), ((), ())), preferred_element_type=f32
            )
            weights = jnp.exp(scores).astype(bf16)
            total += jnp.dot(weights, values[low:high, :], preferred_element_type=f32)
        results[here, :] = (total[:, :size] / total[:, size:]).astype(bf16)
        return carry

    lax.fori_loop(0, (start + query_rows - 1) // query_rows, one_tile, 0)

    for k in range(groups):
        for part in range(rows // piece):
            here = pl.ds(pl.multiple_of(starts[k] + part * piece, 16), piece)
            live = line + part * piece < mine[k]
            out_ref[lax.bitwise_xor(plane, k), part * piece : (part + 1) * piece, :] = jnp.where(
                live, results[here, :].astype(f32), 0.0
            ).astype(bf16)


def attend(place, queries, which, low_lane, keyval, shards):
    groups = len(queries)
    rows = keyval.shape[1]
    size = keyval.shape[2] // 2
    running = shards * rows // 2
    key_room = -(-(running + 16 * shards) // 256) * 256
    query_rows = 256
    query_room = -(-groups * rows // query_rows) * query_rows + rows
    query_block = (1,) + queries[0].shape[1:]
    return pl.pallas_call(
        functools.partial(
            attend_body,
            groups=groups,
            low_lane=low_lane,
            key_room=key_room,
            query_rows=query_rows,
            key_cols=1280,
        ),
        grid_spec=pltpu.PrefetchScalarGridSpec(
            num_scalar_prefetch=1,
            grid=(1,),
            in_specs=[pl.BlockSpec(query_block, lambda i, place: (which, 0, 0))] * groups
            + [pl.BlockSpec(keyval.shape, lambda i, place: (0, 0, 0))],
            out_specs=pl.BlockSpec((groups, rows, size), lambda i, place: (0, 0, 0)),
            scratch_shapes=[
                pltpu.VMEM((key_room + rows, size), bf16),
                pltpu.VMEM((key_room + rows, 2 * size), bf16),
                pltpu.VMEM((query_room, size), bf16),
                pltpu.VMEM((query_room, size), bf16),
                pltpu.SMEM((keyval.shape[0],), jnp.int32),
            ],
        ),
        out_shape=jax.ShapeDtypeStruct((groups, rows, size), bf16),
        compiler_params=params,
        cost_estimate=cost(
            8 * groups * rows // 2 * running * size,
            4 * shards * rows * size,
            groups * rows // 2 * running,
        ),
        name="attend",
    )(place, *queries, keyval)


def finish_body(place_ref, *refs, others, has_sum, last):
    refs = list(refs)
    out_ref = refs.pop()
    total = refs.pop(0)[...] if has_sum else None

    def add(total, attended_ref, weight):
        groups = attended_ref.shape[1]
        wide = jnp.concatenate([attended_ref[0, g] for g in range(groups)], axis=-1)
        term = jnp.dot(wide, weight, preferred_element_type=f32)
        return term if total is None else total + term

    total = add(total, refs[0], refs[1][...])
    for m in range(others):
        total = add(total, refs[2 + 2 * m], refs[3 + 2 * m][0, 0])
    if last:
        rounded = total.astype(bf16)
        out_ref[...] = jnp.dot(refs[-1][...], rounded, preferred_element_type=f32).astype(bf16)
    else:
        out_ref[...] = total


def finish(place, total, attended, w_out, other_weights, back, chunk):
    head_shards, groups, rows, size = attended.shape
    split, _, _, half = other_weights.shape
    parts = 2 if half % 256 == 0 else 1
    tile = half // parts
    out_width = split * half
    depth = groups * size
    mine = lambda i, s, place: (0, i * parts + s)
    own = lambda i, s, place: (chunk, (place[2] * split + i) * parts + s)
    specs, operands = [], []
    if total is not None:
        specs.append(pl.BlockSpec((rows, tile), mine))
        operands.append(total)
    for mask in range(head_shards):
        specs.append(
            pl.BlockSpec(
                (1, groups, rows, size),
                lambda i, s, place, mask=mask: (lax.bitwise_xor(place[2], mask), 0, 0, 0),
            )
        )
        operands.append(attended)
        if mask == 0:
            specs.append(pl.BlockSpec((depth, tile), own))
            operands.append(w_out)
        else:
            specs.append(
                pl.BlockSpec(
                    (1, 1, depth, tile),
                    lambda i, s, place, mask=mask: (i, lax.bitwise_xor(place[2], mask), chunk, s),
                )
            )
            operands.append(other_weights)
    last = back is not None
    if last:
        specs.append(pl.BlockSpec(back.shape, lambda i, s, place: (0, 0)))
        operands.append(back)
    return pl.pallas_call(
        functools.partial(
            finish_body, others=head_shards - 1, has_sum=total is not None, last=last
        ),
        grid_spec=pltpu.PrefetchScalarGridSpec(
            num_scalar_prefetch=1,
            grid=(split, parts),
            in_specs=specs,
            out_specs=pl.BlockSpec((rows, tile), mine),
        ),
        out_shape=jax.ShapeDtypeStruct((rows, out_width), bf16 if last else f32),
        compiler_params=pltpu.CompilerParams(vmem_limit_bytes=32 * mib),
        cost_estimate=cost(
            2 * rows * depth * head_shards * out_width,
            2 * depth * head_shards * out_width + 8 * rows * out_width,
        ),
        name="finish",
    )(place, *operands)


def fetch_weights(w_out, me, side, head_shards):
    depth, width = w_out.shape
    out_width = width // head_shards
    if head_shards != 2 or out_width % 256 != 0:
        blocks = jnp.transpose(w_out.reshape(depth, head_shards, out_width), (1, 0, 2))
        return lax.all_to_all(blocks, "head", split_axis=0, concat_axis=0, tiled=True)[None]
    half = out_width // 2
    column = (1 - side) * out_width + (me % 2) * half
    pairs = [[i, i + 1] for i in range(0, lax.axis_size("seq"), 2)]
    found = lax.all_gather(lax.dynamic_slice(w_out, (0, column), (depth, half)), "head")
    return lax.all_gather(found, "seq", axis_index_groups=pairs)


def per_device(tokens, survive, norm_gain, w_qkv, qk_gain, w_out):
    heads = qk_gain.shape[1]
    shards, head_shards = lax.axis_size("seq"), lax.axis_size("head")
    groups = math.gcd(heads & -heads, shards & -shards)
    ring = shards // groups
    chunks = heads // groups
    me, side = lax.axis_index("seq"), lax.axis_index("head")
    place = jnp.stack([me // ring, me % ring, side]).astype(jnp.int32)
    planes = [[i + ring * g for g in range(groups)] for i in range(ring)]
    rings = [[i + ring * g for i in range(ring)] for g in range(groups)]

    def swap(blocks):
        return [blocks[0]] + [flip(blocks[k], "seq", k * ring) for k in range(1, groups)]

    def after(values, blocks):
        return lax.optimization_barrier((values, blocks[1]))[0] if groups > 1 else values

    def everywhere(blocks):
        size = qk_gain.shape[2]
        stacked = jnp.concatenate([block[:, :, : 2 * size] for block in blocks])
        return lax.all_gather(stacked, "seq", axis=0, tiled=True, axis_index_groups=rings)

    def send_back(blocks):
        if groups > 1:
            blocks = lax.all_to_all(
                blocks, "seq", split_axis=0, concat_axis=0, axis_index_groups=planes, tiled=True
            )
        return lax.all_gather(blocks, "head")

    normed, back, count = pack(tokens, survive, norm_gain)
    weights = jnp.transpose(w_qkv, (1, 0, 2))
    gains = jnp.transpose(qk_gain, (1, 0, 2))
    produce = functools.partial(project, place, count)

    blocks = swap(produce(normed, weights, gains, (1, 2, 0), (0,), groups))
    keyvals, queries = [everywhere(blocks)], [(blocks, 0, 2 * qk_gain.shape[2])]
    for chunk in range(1, chunks):
        blocks = swap(produce(after(normed, blocks), weights, gains, (1, 2), (chunk,), groups))
        keyvals.append(everywhere(blocks))
    if chunks > 1:
        rest = tuple(range(1, chunks))
        blocks = swap(produce(after(normed, blocks), weights, gains, (0,), rest, groups))
        queries += [(blocks, i, 0) for i in range(chunks - 1)]

    other_weights = fetch_weights(w_out, me, side, head_shards)
    total = None
    for chunk in range(chunks):
        query, which, low_lane = queries[chunk]
        attended = send_back(attend(place, query, which, low_lane, keyvals[chunk], shards))
        last = chunk == chunks - 1
        total = finish(place, total, attended, w_out, other_weights, back if last else None, chunk)
    return total


def solution(mesh):
    placed = (
        P("seq", None),
        P("seq"),
        P(),
        P(None, None, "head"),
        P(None, "head", None),
        P("head", None),
    )
    return jax.shard_map(
        per_device, mesh=mesh, in_specs=placed, out_specs=P("seq", "head"), check_vma=False
    )
```

```python
import functools
import math

import jax
import jax.numpy as jnp
from jax import lax
from jax.experimental import pallas as pl
from jax.experimental.pallas import tpu as pltpu
from jax.sharding import PartitionSpec as P

epsilon = 1e-06
dead_mark = 1e30
dead_limit = 1e15
mib = 1 << 20
f32 = jnp.float32
bf16 = jnp.bfloat16
params = pltpu.CompilerParams(vmem_limit_bytes=60 * mib)


def cost(flops, bytes_accessed, exps=0):
    return pl.CostEstimate(
        flops=int(flops), bytes_accessed=int(bytes_accessed), transcendentals=int(exps)
    )


def flip(values, axis, mask):
    size = lax.axis_size(axis)
    return lax.ppermute(values, axis, [(i, i ^ mask) for i in range(size)])


def chain(values, *earlier):
    return lax.optimization_barrier((values, earlier))[0]


def layer_norm(values, gain):
    center = values - jnp.mean(values, axis=-1, keepdims=True)
    spread = jnp.mean(center * center, axis=-1, keepdims=True)
    return center * lax.rsqrt(spread + epsilon) * gain


def prepare(survive_ref, tokens_ref, gain_ref, normed_ref, chosen_ref, back_ref, count_ref):
    positions = tokens_ref.shape[0]
    first = lax.broadcasted_iota(jnp.int32, (positions, positions), 0)
    second = lax.broadcasted_iota(jnp.int32, (positions, positions), 1)
    live = jnp.broadcast_to(survive_ref[...].reshape(1, positions), (8, positions)).astype(f32)
    upper = (first <= second).astype(f32).astype(bf16)
    rank = jnp.dot(live.astype(bf16), upper, preferred_element_type=f32)
    target = jnp.where(live > 0.5, rank - 1.0, -1.0)
    chosen_ref[...] = (first == target[:1].astype(jnp.int32)).astype(f32).astype(bf16)
    home = jnp.transpose(target)[:, :1].astype(jnp.int32)
    back_ref[...] = (second == home).astype(f32).astype(bf16)
    count_ref[0, 0] = jnp.max(rank).astype(jnp.int32)
    gain = gain_ref[...].reshape(1, gain_ref.shape[0])
    rows = 128 if positions % 128 == 0 else positions
    for low in range(0, positions, rows):
        part = tokens_ref[low : low + rows, :].astype(f32)
        normed_ref[low : low + rows, :] = layer_norm(part, gain).astype(bf16)


def project_body(place_ref, *refs, kinds, chunk, groups, first):
    refs = list(refs)
    result_ref = refs.pop()
    if first:
        (survive_ref, tokens_ref, norm_gain_ref, weight_ref, gain_ref), outs = refs[:5], refs[5:]
        normed_ref, chosen_ref, back_ref, count_ref = outs[groups:]

        @pl.when(pl.program_id(0) == 0)
        def _():
            prepare(
                survive_ref, tokens_ref, norm_gain_ref, normed_ref, chosen_ref, back_ref, count_ref
            )

    else:
        (count_ref, normed_ref, chosen_ref, weight_ref, gain_ref), outs = refs[:5], refs[5:]
    rows = normed_ref.shape[0]
    size = gain_ref.shape[2]
    plane = place_ref[0]
    for step, kind in enumerate(kinds):

        @pl.when(pl.program_id(0) == step)
        def _():
            result = jnp.dot(normed_ref[...], weight_ref[0], preferred_element_type=f32)
            for g in range(groups):
                part = result[:, g * size : (g + 1) * size]
                if kind != 2:
                    gain = gain_ref[chunk * groups + g, kind : kind + 1, :]
                    if kind == 0:
                        gain = gain * (1.0 / math.sqrt(size))
                    part = layer_norm(part, gain)
                result_ref[:, g * size : (g + 1) * size] = part.astype(bf16)
            packed = jnp.dot(chosen_ref[...], result_ref[...], preferred_element_type=f32)
            if kind == 1:
                row = lax.broadcasted_iota(jnp.int32, (rows, groups * size), 0)
                packed = jnp.where(row < count_ref[0, 0], packed, dead_mark)
            result_ref[...] = packed.astype(bf16)
            for k in range(groups):
                start = pl.multiple_of(lax.bitwise_xor(plane, k) * size, size)
                outs[k][0, :, step * size : (step + 1) * size] = result_ref[:, pl.ds(start, size)]


def project(place, prepared, weights, gains, kinds, chunk, groups, first=None):
    heads, _, size = gains.shape
    width = weights.shape[1]
    columns = groups * size
    wide = len(kinds) * size
    fixed = lambda t, place: (0, 0)
    smem = pl.BlockSpec(memory_space=pltpu.SMEM)
    rows = (first or prepared)[1].shape[0]
    square = pl.BlockSpec((rows, rows), fixed)
    whole = pl.BlockSpec((rows, width), fixed)

    def weight_index(t, place):
        kind = 0
        for step, value in enumerate(kinds):
            kind = jnp.where(t == step, value, kind)
        return (kind, 0, chunk)

    out_specs = [pl.BlockSpec((1, rows, wide), lambda t, place: (0, 0, 0))] * groups
    out_shape = [jax.ShapeDtypeStruct((1, rows, wide), bf16)] * groups
    if first:
        in_specs = [
            pl.BlockSpec((rows,), lambda t, place: (0,)),
            whole,
            pl.BlockSpec((width,), lambda t, place: (0,)),
        ]
        out_specs += [whole, square, square, smem]
        out_shape += [
            jax.ShapeDtypeStruct((rows, width), bf16),
            jax.ShapeDtypeStruct((rows, rows), bf16),
            jax.ShapeDtypeStruct((rows, rows), bf16),
            jax.ShapeDtypeStruct((1, 1), jnp.int32),
        ]
    else:
        in_specs = [smem, whole, square]
    return pl.pallas_call(
        functools.partial(
            project_body, kinds=kinds, chunk=chunk, groups=groups, first=first is not None
        ),
        grid_spec=pltpu.PrefetchScalarGridSpec(
            num_scalar_prefetch=1,
            grid=(len(kinds),),
            in_specs=in_specs
            + [
                pl.BlockSpec((1, width, columns), weight_index),
                pl.BlockSpec(gains.shape, lambda t, place: (0, 0, 0)),
            ],
            out_specs=out_specs,
            scratch_shapes=[pltpu.VMEM((rows, columns), bf16)],
        ),
        out_shape=out_shape,
        compiler_params=params,
        cost_estimate=cost(
            2 * rows * width * len(kinds) * columns,
            2 * width * len(kinds) * columns + 2 * rows * width,
        ),
        name="project",
    )(place, *(first or prepared), weights, gains)


def attend_body(place_ref, *refs, groups, low_lane, key_room, query_rows, key_cols):
    query_refs, sources = refs[:groups], refs[groups:-5]
    out_ref, keys, values, queries, results = refs[-5:]
    rows, size = out_ref.shape[1:]
    plane = place_ref[0]
    blocks = [(source, k) for source in sources for k in range(groups)]
    piece = 128 if rows % 128 == 0 else rows
    align = lambda count: pl.multiple_of((count + 15) // 16 * 16, 16)
    line = lax.broadcasted_iota(jnp.int32, (piece, size), 0)

    found = []
    for source, block in blocks:
        live = (source[block, :, :size].astype(f32) < dead_limit).astype(f32)
        found.append(jnp.max(jnp.sum(live, axis=0, keepdims=True)).astype(jnp.int32))

    offset = jnp.int32(0)
    for (source, block), count in zip(blocks, found):
        for part in range(rows // piece):

            @pl.when(part * piece < count)
            def _():
                here = pl.ds(pl.multiple_of(offset + part * piece, 16), piece)
                there = pl.ds(part * piece, piece)
                live = line + part * piece < count
                key = jnp.where(live, source[block, there, :size].astype(f32), 0.0)
                keys[here, :] = key.astype(bf16)
                values[here, :size] = source[block, there, size:]
                values[here, size:] = live.astype(f32).astype(bf16)

        offset = pl.multiple_of(offset + align(count), 16)

    def clear(step, carry):
        here = pl.ds(pl.multiple_of(offset + step * 16, 16), 16)
        keys[here, :] = jnp.zeros((16, size), bf16)
        values[here, :] = jnp.zeros((16, 2 * size), bf16)
        return carry

    lax.fori_loop(0, (key_room - offset) // 16, clear, 0)

    mine = found[:groups]
    starts = []
    start = jnp.int32(0)
    for k in range(groups):
        starts.append(start)
        for part in range(rows // piece):

            @pl.when(part * piece < mine[k])
            def _():
                here = pl.ds(pl.multiple_of(start + part * piece, 16), piece)
                there = pl.ds(part * piece, piece)
                queries[here, :] = query_refs[k][0, there, low_lane : low_lane + size]

        start = pl.multiple_of(start + align(mine[k]), 16)

    def one_tile(tile, carry):
        here = pl.ds(pl.multiple_of(tile * query_rows, query_rows), query_rows)
        query = queries[here, :]
        total = jnp.zeros((query_rows, 2 * size), f32)
        for low in range(0, key_room, key_cols):
            high = min(low + key_cols, key_room)
            scores = lax.dot_general(
                query, keys[low:high, :], (((1,), (1,)), ((), ())), preferred_element_type=f32
            )
            weights = jnp.exp(scores).astype(bf16)
            total += jnp.dot(weights, values[low:high, :], preferred_element_type=f32)
        results[here, :] = (total[:, :size] / total[:, size:]).astype(bf16)
        return carry

    lax.fori_loop(0, (start + query_rows - 1) // query_rows, one_tile, 0)

    for k in range(groups):
        for part in range(rows // piece):
            here = pl.ds(pl.multiple_of(starts[k] + part * piece, 16), piece)
            live = line + part * piece < mine[k]
            out_ref[lax.bitwise_xor(plane, k), part * piece : (part + 1) * piece, :] = jnp.where(
                live, results[here, :].astype(f32), 0.0
            ).astype(bf16)


def attend(place, queries, low_lane, keyvals, shards):
    groups = len(queries)
    rows = keyvals[0].shape[1]
    size = keyvals[0].shape[2] // 2
    running = shards * rows // 2
    key_room = -(-(running + 16 * shards) // 256) * 256
    query_rows = 256
    query_room = -(-groups * rows // query_rows) * query_rows + rows
    query_block = (1,) + queries[0].shape[1:]
    return pl.pallas_call(
        functools.partial(
            attend_body,
            groups=groups,
            low_lane=low_lane,
            key_room=key_room,
            query_rows=query_rows,
            key_cols=256,
        ),
        grid_spec=pltpu.PrefetchScalarGridSpec(
            num_scalar_prefetch=1,
            grid=(1,),
            in_specs=[pl.BlockSpec(query_block, lambda i, place: (0, 0, 0))] * groups
            + [pl.BlockSpec(keyvals[0].shape, lambda i, place: (0, 0, 0))] * len(keyvals),
            out_specs=pl.BlockSpec((groups, rows, size), lambda i, place: (0, 0, 0)),
            scratch_shapes=[
                pltpu.VMEM((key_room + rows, size), bf16),
                pltpu.VMEM((key_room + rows, 2 * size), bf16),
                pltpu.VMEM((query_room, size), bf16),
                pltpu.VMEM((query_room, size), bf16),
            ],
        ),
        out_shape=jax.ShapeDtypeStruct((groups, rows, size), bf16),
        compiler_params=params,
        cost_estimate=cost(
            8 * groups * rows // 2 * running * size,
            4 * shards * rows * size,
            groups * rows // 2 * running,
        ),
        name="attend",
    )(place, *queries, *keyvals)


def finish_body(place_ref, *refs, others, has_sum, last):
    refs = list(refs)
    out_ref = refs.pop()
    total = refs.pop(0)[...] if has_sum else None

    def add(total, attended_ref, weight):
        groups = attended_ref.shape[0]
        wide = jnp.concatenate([attended_ref[g] for g in range(groups)], axis=-1)
        term = jnp.dot(wide, weight, preferred_element_type=f32)
        return term if total is None else total + term

    total = add(total, refs[0], refs[1][...])
    for m in range(others):
        attended_ref, near_ref, far_ref = refs[2 + 3 * m : 5 + 3 * m]
        weight = jnp.where(pl.program_id(0) == 0, near_ref[...], far_ref[...])
        total = add(total, attended_ref, weight)
    if last:
        rounded = total.astype(bf16)
        out_ref[...] = jnp.dot(refs[-1][...], rounded, preferred_element_type=f32).astype(bf16)
    else:
        out_ref[...] = total


def column_split(out_width):
    return 2 if out_width % 256 == 0 else 1


def finish(place, total, attended, w_out, other_attended, other_weights, back, chunk, out_width):
    groups, rows, size = attended.shape
    split = column_split(out_width)
    half = out_width // split
    depth = groups * size
    mine = lambda i, place: (0, lax.bitwise_xor(place[1], i))
    own = lambda i, place: (chunk, split * place[2] + lax.bitwise_xor(place[1], i))
    block_a = pl.BlockSpec((groups, rows, size), lambda i, place: (0, 0, 0))
    block_w = pl.BlockSpec((depth, half), lambda i, place: (chunk, 0))
    specs, operands = [], []
    if total is not None:
        specs.append(pl.BlockSpec((rows, half), mine))
        operands.append(total)
    specs += [block_a, pl.BlockSpec((depth, half), own)]
    operands += [attended, w_out]
    for other, weights in zip(other_attended, other_weights):
        specs += [block_a, block_w, block_w]
        operands += [other, *weights]
    last = back is not None
    if last:
        specs.append(pl.BlockSpec(back.shape, lambda i, place: (0, 0)))
        operands.append(back)
    count = 1 + len(other_attended)
    return pl.pallas_call(
        functools.partial(
            finish_body, others=len(other_attended), has_sum=total is not None, last=last
        ),
        grid_spec=pltpu.PrefetchScalarGridSpec(
            num_scalar_prefetch=1,
            grid=(split,),
            in_specs=specs,
            out_specs=pl.BlockSpec((rows, half), mine),
        ),
        out_shape=jax.ShapeDtypeStruct((rows, out_width), bf16 if last else f32),
        compiler_params=pltpu.CompilerParams(vmem_limit_bytes=32 * mib),
        cost_estimate=cost(
            2 * rows * depth * count * out_width, 2 * depth * count * out_width + 8 * rows * out_width
        ),
        name="finish",
    )(place, *operands)


def per_device(tokens, survive, norm_gain, w_qkv, qk_gain, w_out):
    heads, size = qk_gain.shape[1:]
    shards, head_shards = lax.axis_size("seq"), lax.axis_size("head")
    out_width = w_out.shape[1] // head_shards
    split = column_split(out_width)
    half = out_width // split
    groups = math.gcd(heads & -heads, shards & -shards)
    ring = shards // groups
    chunks = heads // groups
    me, side = lax.axis_index("seq"), lax.axis_index("head")
    core = me % split
    place = jnp.stack([me // ring, core, side]).astype(jnp.int32)
    planes = [[i + ring * g for g in range(groups)] for i in range(ring)]

    def swap(blocks):
        return [blocks[0]] + [flip(blocks[k], "seq", k * ring) for k in range(1, groups)]

    def everywhere(blocks):
        stacked = jnp.concatenate([block[:, :, : 2 * size] for block in blocks])
        found = {0: stacked}
        mask = ring // 2
        while mask:
            for known in list(found):
                found[known | mask] = flip(found[known], "seq", mask)
            mask //= 2
        return [found[mask] for mask in range(ring)]

    def send_back(blocks):
        if groups > 1:
            blocks = lax.all_to_all(
                blocks, "seq", split_axis=0, concat_axis=0, axis_index_groups=planes, tiled=True
            )
        return blocks, [flip(blocks, "head", mask) for mask in range(1, head_shards)]

    weights = jnp.transpose(w_qkv, (1, 0, 2))
    gains = jnp.transpose(qk_gain, (1, 0, 2))

    plan = [((1, 2, 0), 0)]
    plan += [((1, 2), chunk) for chunk in range(1, chunks)]
    plan += [((0,), chunk) for chunk in range(1, chunks)]
    keyvals, queries = {}, {}
    normed = chosen = back = count = None
    waiting = None
    for kinds, chunk in plan:
        if normed is None:
            found = project(
                place, None, weights, gains, kinds, chunk, groups, (survive, tokens, norm_gain)
            )
            normed, chosen, back, count = found[groups:]
        else:
            source = chain(normed, blocks[1]) if groups > 1 else normed
            found = project(place, (count, source, chosen), weights, gains, kinds, chunk, groups)
        sent = found[:groups]
        if waiting is not None:
            ready, owner = waiting
            keyvals[owner] = everywhere(list(chain(tuple(ready), sent[0])))
        blocks = swap(sent)
        waiting = (blocks, chunk) if 1 in kinds else None
        if 0 in kinds:
            queries[chunk] = (blocks, (len(kinds) - 1) * size)
    if waiting is not None:
        keyvals[waiting[1]] = everywhere(waiting[0])

    other_weights = []
    for mask in range(1, head_shards):
        column = lax.bitwise_xor(side, mask) * out_width + core * half
        rows = lax.dynamic_slice(chain(w_out, normed), (0, column), (w_out.shape[0], half))
        near = flip(rows, "head", mask)
        other_weights.append((near, flip(near, "seq", 1) if split == 2 else near))

    total = None
    for chunk in range(chunks):
        query, low_lane = queries[chunk]
        attended, others = send_back(attend(place, query, low_lane, keyvals[chunk], shards))
        last = back if chunk == chunks - 1 else None
        total = finish(
            place, total, attended, w_out, others, other_weights, last, chunk, out_width
        )
    return total


def solution(mesh):
    placed = (
        P("seq", None),
        P("seq"),
        P(),
        P(None, None, "head"),
        P(None, "head", None),
        P("head", None),
    )
    return jax.shard_map(
        per_device, mesh=mesh, in_specs=placed, out_specs=P("seq", "head"), check_vma=False
    )
```

```python
import functools
import math

import jax
import jax.numpy as jnp
from jax import lax
from jax.experimental import pallas as pl
from jax.experimental.pallas import tpu as pltpu
from jax.sharding import PartitionSpec as P

epsilon = 1e-06
dead_mark = 1e30
dead_limit = 1e15
mib = 1 << 20
f32 = jnp.float32
bf16 = jnp.bfloat16
params = pltpu.CompilerParams(vmem_limit_bytes=60 * mib)


def cost(flops, bytes_accessed, exps=0):
    return pl.CostEstimate(
        flops=int(flops), bytes_accessed=int(bytes_accessed), transcendentals=int(exps)
    )


def flip(values, axis, mask):
    size = lax.axis_size(axis)
    return lax.ppermute(values, axis, [(i, i ^ mask) for i in range(size)])


def place_half(width):
    head_shards = lax.axis_size("head")
    out_width = width // head_shards
    return out_width // 2 if splits(out_width, head_shards) else out_width


def splits(out_width, head_shards):
    return head_shards == 2 and out_width % 256 == 0


def chain(values, *earlier):
    return lax.optimization_barrier((values, earlier))[0]


def layer_norm(values, gain):
    center = values - jnp.mean(values, axis=-1, keepdims=True)
    spread = jnp.mean(center * center, axis=-1, keepdims=True)
    return center * lax.rsqrt(spread + epsilon) * gain


def prepare(survive_ref, tokens_ref, gain_ref, normed_ref, chosen_ref, back_ref, count_ref):
    positions = tokens_ref.shape[0]
    first = lax.broadcasted_iota(jnp.int32, (positions, positions), 0)
    second = lax.broadcasted_iota(jnp.int32, (positions, positions), 1)
    live = jnp.broadcast_to(survive_ref[...].reshape(1, positions), (8, positions)).astype(f32)
    upper = (first <= second).astype(f32).astype(bf16)
    rank = jnp.dot(live.astype(bf16), upper, preferred_element_type=f32)
    target = jnp.where(live > 0.5, rank - 1.0, -1.0)
    chosen_ref[...] = (first == target[:1].astype(jnp.int32)).astype(f32).astype(bf16)
    home = jnp.transpose(target)[:, :1].astype(jnp.int32)
    back_ref[...] = (second == home).astype(f32).astype(bf16)
    count_ref[0, 0] = jnp.max(rank).astype(jnp.int32)
    gain = gain_ref[...].reshape(1, gain_ref.shape[0])
    rows = 128 if positions % 128 == 0 else positions
    for low in range(0, positions, rows):
        part = tokens_ref[low : low + rows, :].astype(f32)
        normed_ref[low : low + rows, :] = layer_norm(part, gain).astype(bf16)


def project_body(place_ref, *refs, kinds, chunks, groups, first, streams):
    refs = list(refs)
    result_ref = refs.pop()
    weight_refs, gain_ref = refs[:streams], refs[streams]
    refs = refs[streams + 1 :]
    outs = refs[3 + first : 3 + first + groups * len(chunks)]
    plane = place_ref[0]
    if first:
        survive_ref, tokens_ref, norm_gain_ref, source_ref = refs[:4]
        normed_ref, chosen_ref, back_ref, count_ref, slice_ref, copy_sem = refs[4 + len(outs) :]
        half = slice_ref.shape[1]
        start = pl.multiple_of(place_ref[3] * half, half)
        copy = pltpu.make_async_copy(source_ref.at[:, pl.ds(start, half)], slice_ref, copy_sem)

        @pl.when(pl.program_id(1) == 0)
        def _():
            copy.start()
            prepare(
                survive_ref, tokens_ref, norm_gain_ref, normed_ref, chosen_ref, back_ref, count_ref
            )

    else:
        count_ref, normed_ref, chosen_ref = refs[:3]
    rows, width = normed_ref.shape
    size = gain_ref.shape[2]
    depth = width // streams
    for step in range(len(chunks) * len(kinds)):
        chunk, kind = chunks[step // len(kinds)], kinds[step % len(kinds)]
        low = step % len(kinds) * size
        targets = outs[step // len(kinds) * groups :][:groups]

        @pl.when(pl.program_id(0) * len(kinds) + pl.program_id(1) == step)
        def _():
            result = sum(
                jnp.dot(
                    normed_ref[:, i * depth : (i + 1) * depth],
                    weight_ref[0],
                    preferred_element_type=f32,
                )
                for i, weight_ref in enumerate(weight_refs)
            )
            for g in range(groups):
                part = result[:, g * size : (g + 1) * size]
                if kind != 2:
                    gain = gain_ref[chunk * groups + g, kind : kind + 1, :]
                    if kind == 0:
                        gain = gain * (1.0 / math.sqrt(size))
                    part = layer_norm(part, gain)
                result_ref[:, g * size : (g + 1) * size] = part.astype(bf16)
            packed = jnp.dot(chosen_ref[...], result_ref[...], preferred_element_type=f32)
            if kind == 1:
                row = lax.broadcasted_iota(jnp.int32, (rows, groups * size), 0)
                packed = jnp.where(row < count_ref[0, 0], packed, dead_mark)
            result_ref[...] = packed.astype(bf16)
            for k in range(groups):
                start = pl.multiple_of(lax.bitwise_xor(plane, k) * size, size)
                targets[k][0, :, low : low + size] = result_ref[:, pl.ds(start, size)]

    if first:

        @pl.when(pl.program_id(1) == len(kinds) - 1)
        def _():
            copy.wait()


def project(place, prepared, weights, gains, kinds, chunks, groups, first=None):
    heads, _, size = gains.shape
    width = weights.shape[1]
    columns = groups * size
    wide = len(kinds) * size
    streams = 4 if width % 512 == 0 else 1
    fixed = lambda c, t, place: (0, 0)
    line = lambda c, t, place: (0,)
    smem = pl.BlockSpec(memory_space=pltpu.SMEM)
    anywhere = pl.BlockSpec(memory_space=pl.ANY)
    rows = (first or prepared)[1].shape[0]
    square = pl.BlockSpec((rows, rows), fixed)
    whole = pl.BlockSpec((rows, width), fixed)

    def weight_index(part, c, t, place):
        kind = 0
        for step, value in enumerate(kinds):
            kind = jnp.where(t == step, value, kind)
        return (kind, part, chunks[0] + c)

    count = groups * len(chunks)
    out_specs = [pl.BlockSpec((1, rows, wide), lambda c, t, place: (0, 0, 0))] * count
    out_shape = [jax.ShapeDtypeStruct((1, rows, wide), bf16)] * count
    scratch = [pltpu.VMEM((rows, columns), bf16)]
    if first:
        half = place_half(first[3].shape[1])
        in_specs = [pl.BlockSpec((rows,), line), whole, pl.BlockSpec((width,), line), anywhere]
        out_specs += [whole, square, square, smem, anywhere]
        out_shape += [
            jax.ShapeDtypeStruct((rows, width), bf16),
            jax.ShapeDtypeStruct((rows, rows), bf16),
            jax.ShapeDtypeStruct((rows, rows), bf16),
            jax.ShapeDtypeStruct((1, 1), jnp.int32),
            jax.ShapeDtypeStruct((first[3].shape[0], half), bf16),
        ]
        scratch = [pltpu.SemaphoreType.DMA(())] + scratch
    else:
        in_specs = [smem, whole, square]
    return pl.pallas_call(
        functools.partial(
            project_body,
            kinds=kinds,
            chunks=chunks,
            groups=groups,
            first=first is not None,
            streams=streams,
        ),
        grid_spec=pltpu.PrefetchScalarGridSpec(
            num_scalar_prefetch=1,
            grid=(len(chunks), len(kinds)),
            in_specs=[
                pl.BlockSpec((1, width // streams, columns), functools.partial(weight_index, part))
                for part in range(streams)
            ]
            + [pl.BlockSpec(gains.shape, lambda c, t, place: (0, 0, 0))]
            + in_specs,
            out_specs=out_specs,
            scratch_shapes=scratch,
        ),
        out_shape=out_shape,
        compiler_params=params,
        cost_estimate=cost(
            2 * rows * width * len(kinds) * len(chunks) * columns,
            2 * width * len(kinds) * len(chunks) * columns + 2 * rows * width,
        ),
        name="project",
    )(place, *[weights] * streams, gains, *(first or prepared))


def attend_body(place_ref, *refs, groups, low_lane, key_room, query_rows, key_cols):
    query_refs, sources = refs[:groups], refs[groups:-5]
    out_ref, keys, values, queries, results = refs[-5:]
    rows, size = out_ref.shape[1:]
    plane = place_ref[0]
    blocks = [(source, k) for source in sources for k in range(groups)]
    piece = 128 if rows % 128 == 0 else rows
    align = lambda count: pl.multiple_of((count + 15) // 16 * 16, 16)
    line = lax.broadcasted_iota(jnp.int32, (piece, size), 0)

    found = []
    for source, block in blocks:
        live = (source[block, :, :size].astype(f32) < dead_limit).astype(f32)
        found.append(jnp.max(jnp.sum(live, axis=0, keepdims=True)).astype(jnp.int32))

    offset = jnp.int32(0)
    for (source, block), count in zip(blocks, found):
        for part in range(rows // piece):

            @pl.when(part * piece < count)
            def _():
                here = pl.ds(pl.multiple_of(offset + part * piece, 16), piece)
                there = pl.ds(part * piece, piece)
                live = line + part * piece < count
                key = jnp.where(live, source[block, there, :size].astype(f32), 0.0)
                keys[here, :] = key.astype(bf16)
                values[here, :size] = source[block, there, size:]
                values[here, size:] = live.astype(f32).astype(bf16)

        offset = pl.multiple_of(offset + align(count), 16)

    def clear(step, carry):
        here = pl.ds(pl.multiple_of(offset + step * 16, 16), 16)
        keys[here, :] = jnp.zeros((16, size), bf16)
        values[here, :] = jnp.zeros((16, 2 * size), bf16)
        return carry

    lax.fori_loop(0, (key_room - offset) // 16, clear, 0)

    mine = found[:groups]
    starts = []
    start = jnp.int32(0)
    for k in range(groups):
        starts.append(start)
        for part in range(rows // piece):

            @pl.when(part * piece < mine[k])
            def _():
                here = pl.ds(pl.multiple_of(start + part * piece, 16), piece)
                there = pl.ds(part * piece, piece)
                queries[here, :] = query_refs[k][0, there, low_lane : low_lane + size]

        start = pl.multiple_of(start + align(mine[k]), 16)

    def one_tile(tile, carry):
        here = pl.ds(pl.multiple_of(tile * query_rows, query_rows), query_rows)
        query = queries[here, :]
        total = jnp.zeros((query_rows, 2 * size), f32)
        for low in range(0, key_room, key_cols):
            high = min(low + key_cols, key_room)
            scores = lax.dot_general(
                query, keys[low:high, :], (((1,), (1,)), ((), ())), preferred_element_type=f32
            )
            weights = jnp.exp(scores).astype(bf16)
            total += jnp.dot(weights, values[low:high, :], preferred_element_type=f32)
        results[here, :] = (total[:, :size] / total[:, size:]).astype(bf16)
        return carry

    lax.fori_loop(0, (start + query_rows - 1) // query_rows, one_tile, 0)

    for k in range(groups):
        for part in range(rows // piece):
            here = pl.ds(pl.multiple_of(starts[k] + part * piece, 16), piece)
            live = line + part * piece < mine[k]
            out_ref[lax.bitwise_xor(plane, k), part * piece : (part + 1) * piece, :] = jnp.where(
                live, results[here, :].astype(f32), 0.0
            ).astype(bf16)


def attend(place, queries, low_lane, keyvals, shards):
    groups = len(queries)
    rows = keyvals[0].shape[1]
    size = keyvals[0].shape[2] // 2
    running = shards * rows // 2
    key_room = -(-(running + 16 * shards) // 256) * 256
    query_rows = 256
    query_room = -(-groups * rows // query_rows) * query_rows + rows
    query_block = (1,) + queries[0].shape[1:]
    return pl.pallas_call(
        functools.partial(
            attend_body,
            groups=groups,
            low_lane=low_lane,
            key_room=key_room,
            query_rows=query_rows,
            key_cols=256,
        ),
        grid_spec=pltpu.PrefetchScalarGridSpec(
            num_scalar_prefetch=1,
            grid=(1,),
            in_specs=[pl.BlockSpec(query_block, lambda i, place: (0, 0, 0))] * groups
            + [pl.BlockSpec(keyvals[0].shape, lambda i, place: (0, 0, 0))] * len(keyvals),
            out_specs=pl.BlockSpec((groups, rows, size), lambda i, place: (0, 0, 0)),
            scratch_shapes=[
                pltpu.VMEM((key_room + rows, size), bf16),
                pltpu.VMEM((key_room + rows, 2 * size), bf16),
                pltpu.VMEM((query_room, size), bf16),
                pltpu.VMEM((query_room, size), bf16),
            ],
        ),
        out_shape=jax.ShapeDtypeStruct((groups, rows, size), bf16),
        compiler_params=params,
        cost_estimate=cost(
            8 * groups * rows // 2 * running * size,
            4 * shards * rows * size,
            groups * rows // 2 * running,
        ),
        name="attend",
    )(place, *queries, *keyvals)


def finish_body(place_ref, *refs, chunks, others, has_sum, last):
    refs = list(refs)
    out_ref = refs.pop()
    total = refs.pop(0)[...] if has_sum else None
    for m in range(1 + others):
        attended_refs, weight_ref = refs[:chunks], refs[chunks]
        refs = refs[chunks + 1 :]
        wide = jnp.concatenate(
            [ref[g] for ref in attended_refs for g in range(ref.shape[0])], axis=-1
        )
        weight = weight_ref[0, 0] if m else weight_ref[...]
        term = jnp.dot(wide, weight, preferred_element_type=f32)
        total = term if total is None else total + term
    if last:
        rounded = total.astype(bf16)
        out_ref[...] = jnp.dot(refs[0][...], rounded, preferred_element_type=f32).astype(bf16)
    else:
        out_ref[...] = total


def finish(place, total, attended, w_out, other_weights, back, first_chunk):
    groups, rows, size = attended[0][0].shape
    split, head_shards, _, half = other_weights.shape
    chunks = len(attended)
    out_width = split * half
    depth = chunks * groups * size
    block = first_chunk // chunks
    mine = lambda i, place: (0, i)
    own = lambda i, place: (block, split * place[2] + i)
    block_a = pl.BlockSpec((groups, rows, size), lambda i, place: (0, 0, 0))
    specs, operands = [], []
    if total is not None:
        specs.append(pl.BlockSpec((rows, half), mine))
        operands.append(total)
    for mask in range(head_shards):
        specs += [block_a] * chunks
        operands += [found[mask] for found in attended]
        if mask == 0:
            specs.append(pl.BlockSpec((depth, half), own))
            operands.append(w_out)
        else:
            specs.append(
                pl.BlockSpec(
                    (1, 1, depth, half),
                    lambda i, place, mask=mask: (i, lax.bitwise_xor(place[2], mask), block, 0),
                )
            )
            operands.append(other_weights)
    last = back is not None
    if last:
        specs.append(pl.BlockSpec(back.shape, lambda i, place: (0, 0)))
        operands.append(back)
    return pl.pallas_call(
        functools.partial(
            finish_body,
            chunks=chunks,
            others=head_shards - 1,
            has_sum=total is not None,
            last=last,
        ),
        grid_spec=pltpu.PrefetchScalarGridSpec(
            num_scalar_prefetch=1,
            grid=(split,),
            in_specs=specs,
            out_specs=pl.BlockSpec((rows, half), mine),
        ),
        out_shape=jax.ShapeDtypeStruct((rows, out_width), bf16 if last else f32),
        compiler_params=pltpu.CompilerParams(vmem_limit_bytes=32 * mib),
        cost_estimate=cost(
            2 * rows * depth * head_shards * out_width,
            2 * depth * head_shards * out_width + 8 * rows * out_width,
        ),
        name="finish",
    )(place, *operands)


def fetch_weights(w_out, part, head_shards):
    depth, width = w_out.shape
    out_width = width // head_shards
    if not splits(out_width, head_shards):
        blocks = jnp.transpose(w_out.reshape(depth, head_shards, out_width), (1, 0, 2))
        return lax.all_to_all(blocks, "head", split_axis=0, concat_axis=0, tiled=True)[None]
    pairs = [[i, i + 1] for i in range(0, lax.axis_size("seq"), 2)]
    found = lax.all_gather(part, "head")
    return lax.all_gather(found, "seq", axis_index_groups=pairs)


def per_device(tokens, survive, norm_gain, w_qkv, qk_gain, w_out):
    heads, size = qk_gain.shape[1:]
    shards, head_shards = lax.axis_size("seq"), lax.axis_size("head")
    groups = math.gcd(heads & -heads, shards & -shards)
    ring = shards // groups
    chunks = heads // groups
    me, side = lax.axis_index("seq"), lax.axis_index("head")
    planes = [[i + ring * g for g in range(groups)] for i in range(ring)]
    split = 2 if splits(w_out.shape[1] // head_shards, head_shards) else 1
    piece = (1 - side) * split + me % split if split == 2 else side
    place = jnp.stack([me // ring, me % ring, side, piece]).astype(jnp.int32)

    def swap(blocks):
        return [blocks[0]] + [flip(blocks[k], "seq", k * ring) for k in range(1, groups)]

    def everywhere(blocks):
        stacked = jnp.concatenate([block[:, :, : 2 * size] for block in blocks])
        found = {0: stacked}
        mask = ring // 2
        while mask:
            for known in list(found):
                found[known | mask] = flip(found[known], "seq", mask)
            mask //= 2
        return [found[mask] for mask in range(ring)]

    def send_back(blocks):
        if groups == 1:
            return blocks
        return lax.all_to_all(
            blocks, "seq", split_axis=0, concat_axis=0, axis_index_groups=planes, tiled=True
        )

    def across(blocks):
        return [blocks] + [flip(blocks, "head", mask) for mask in range(1, head_shards)]

    weights = jnp.transpose(w_qkv, (1, 0, 2))
    gains = jnp.transpose(qk_gain, (1, 0, 2))

    plan = [((1, 2, 0), (0,))]
    plan += [((1, 2), (chunk,)) for chunk in range(1, chunks)]
    plan += [((0,), tuple(range(1, chunks)))] if chunks > 1 else []
    keyvals, queries = {}, {}
    waiting = None
    for kinds, which in plan:
        if not queries:
            operands = (survive, tokens, norm_gain, w_out)
            found = project(place, None, weights, gains, kinds, which, groups, operands)
            normed, chosen, back, count, part = found[groups:]
            other_weights = fetch_weights(w_out, part, head_shards)
        else:
            source = chain(normed, blocks[1]) if groups > 1 else normed
            found = project(place, (count, source, chosen), weights, gains, kinds, which, groups)
        if waiting is not None:
            ready, owner = waiting
            keyvals[owner] = everywhere(list(chain(tuple(ready), found[0])))
        for i, chunk in enumerate(which):
            blocks = swap(found[i * groups : (i + 1) * groups])
            if 0 in kinds:
                queries[chunk] = (blocks, (len(kinds) - 1) * size)
        waiting = (blocks, which[0]) if 1 in kinds else None
    if waiting is not None:
        keyvals[waiting[1]] = everywhere(waiting[0])

    attended = []
    for chunk in range(chunks):
        query, low_lane = queries[chunk]
        attended.append(send_back(attend(place, query, low_lane, keyvals[chunk], shards)))
    total = None
    if chunks > 1:
        early = [across(found) for found in attended[:-1]]
        total = finish(place, None, early, w_out, other_weights, None, 0)
    final = across(attended[-1] if total is None else chain(attended[-1], total))
    return finish(place, total, [final], w_out, other_weights, back, chunks - 1)


def solution(mesh):
    placed = (
        P("seq", None),
        P("seq"),
        P(),
        P(None, None, "head"),
        P(None, "head", None),
        P("head", None),
    )
    return jax.shard_map(
        per_device, mesh=mesh, in_specs=placed, out_specs=P("seq", "head"), check_vma=False
    )
```

```python
import functools
import math

import jax
import jax.numpy as jnp
from jax import lax
from jax.experimental import pallas as pl
from jax.experimental.pallas import tpu as pltpu
from jax.sharding import PartitionSpec as P

epsilon = 1e-06
dead_mark = 1e30
dead_limit = 1e15
mib = 1 << 20
f32 = jnp.float32
bf16 = jnp.bfloat16
params = pltpu.CompilerParams(vmem_limit_bytes=60 * mib)


def cost(flops, bytes_accessed, exps=0):
    return pl.CostEstimate(
        flops=int(flops), bytes_accessed=int(bytes_accessed), transcendentals=int(exps)
    )


def flip(values, axis, mask):
    size = lax.axis_size(axis)
    return lax.ppermute(values, axis, [(i, i ^ mask) for i in range(size)])


def chain(values, *earlier):
    return lax.optimization_barrier((values, earlier))[0]


def layer_norm(values, gain):
    center = values - jnp.mean(values, axis=-1, keepdims=True)
    spread = jnp.mean(center * center, axis=-1, keepdims=True)
    return center * lax.rsqrt(spread + epsilon) * gain


def prepare(survive_ref, tokens_ref, gain_ref, normed_ref, chosen_ref, back_ref, count_ref):
    positions = tokens_ref.shape[0]
    first = lax.broadcasted_iota(jnp.int32, (positions, positions), 0)
    second = lax.broadcasted_iota(jnp.int32, (positions, positions), 1)
    live = jnp.broadcast_to(survive_ref[...].reshape(1, positions), (8, positions)).astype(f32)
    upper = (first <= second).astype(f32).astype(bf16)
    rank = jnp.dot(live.astype(bf16), upper, preferred_element_type=f32)
    target = jnp.where(live > 0.5, rank - 1.0, -1.0)
    chosen_ref[...] = (first == target[:1].astype(jnp.int32)).astype(f32).astype(bf16)
    home = jnp.transpose(target)[:, :1].astype(jnp.int32)
    back_ref[...] = (second == home).astype(f32).astype(bf16)
    count_ref[0, 0] = jnp.max(rank).astype(jnp.int32)
    gain = gain_ref[...].reshape(1, gain_ref.shape[0])
    rows = 128 if positions % 128 == 0 else positions
    for low in range(0, positions, rows):
        part = tokens_ref[low : low + rows, :].astype(f32)
        normed_ref[low : low + rows, :] = layer_norm(part, gain).astype(bf16)


def project_body(place_ref, *refs, steps, groups, first):
    refs = list(refs)
    result_ref = refs.pop()
    weight_ref, gain_ref = refs[:2]
    if first:
        survive_ref, tokens_ref, norm_gain_ref = refs[2:5]
        outs, (normed_ref, chosen_ref, back_ref, count_ref) = refs[5:-4], refs[-4:]

        @pl.when(pl.program_id(0) == 0)
        def _():
            prepare(
                survive_ref, tokens_ref, norm_gain_ref, normed_ref, chosen_ref, back_ref, count_ref
            )

    else:
        (count_ref, normed_ref, chosen_ref), outs = refs[2:5], refs[5:]
    rows = normed_ref.shape[0]
    size = gain_ref.shape[2]
    plane = place_ref[0]
    for step, (kind, chunk, target, low) in enumerate(steps):

        @pl.when(pl.program_id(0) == step)
        def _():
            result = jnp.dot(normed_ref[...], weight_ref[0], preferred_element_type=f32)
            for g in range(groups):
                part = result[:, g * size : (g + 1) * size]
                if kind != 2:
                    gain = gain_ref[chunk * groups + g, kind : kind + 1, :]
                    if kind == 0:
                        gain = gain * (1.0 / math.sqrt(size))
                    part = layer_norm(part, gain)
                result_ref[:, g * size : (g + 1) * size] = part.astype(bf16)
            packed = jnp.dot(chosen_ref[...], result_ref[...], preferred_element_type=f32)
            if kind == 1:
                row = lax.broadcasted_iota(jnp.int32, (rows, groups * size), 0)
                packed = jnp.where(row < count_ref[0, 0], packed, dead_mark)
            result_ref[...] = packed.astype(bf16)
            for k in range(groups):
                start = pl.multiple_of(lax.bitwise_xor(plane, k) * size, size)
                found = result_ref[:, pl.ds(start, size)]
                outs[target * groups + k][0, :, low : low + size] = found


def project(place, prepared, weights, gains, sets, groups, first=None):
    size = gains.shape[2]
    width = weights.shape[1]
    columns = groups * size
    fixed = lambda t, place: (0, 0)
    line = lambda t, place: (0,)
    smem = pl.BlockSpec(memory_space=pltpu.SMEM)
    rows = (first or prepared)[1].shape[0]
    square = pl.BlockSpec((rows, rows), fixed)
    whole = pl.BlockSpec((rows, width), fixed)
    steps = [
        (kind, chunk, target, i * size)
        for target, (kinds, chunk) in enumerate(sets)
        for i, kind in enumerate(kinds)
    ]

    def weight_index(t, place):
        kind, chunk = steps[0][:2]
        for step, found in enumerate(steps):
            kind = jnp.where(t == step, found[0], kind)
            chunk = jnp.where(t == step, found[1], chunk)
        return (kind, 0, chunk)

    widths = [len(kinds) * size for kinds, _ in sets for _ in range(groups)]
    out_specs = [pl.BlockSpec((1, rows, wide), lambda t, place: (0, 0, 0)) for wide in widths]
    out_shape = [jax.ShapeDtypeStruct((1, rows, wide), bf16) for wide in widths]
    if first:
        in_specs = [pl.BlockSpec((rows,), line), whole, pl.BlockSpec((width,), line)]
        out_specs += [whole, square, square, smem]
        out_shape += [
            jax.ShapeDtypeStruct((rows, width), bf16),
            jax.ShapeDtypeStruct((rows, rows), bf16),
            jax.ShapeDtypeStruct((rows, rows), bf16),
            jax.ShapeDtypeStruct((1, 1), jnp.int32),
        ]
    else:
        in_specs = [smem, whole, square]
    found = pl.pallas_call(
        functools.partial(project_body, steps=steps, groups=groups, first=first is not None),
        grid_spec=pltpu.PrefetchScalarGridSpec(
            num_scalar_prefetch=1,
            grid=(len(steps),),
            in_specs=[
                pl.BlockSpec((1, width, columns), weight_index),
                pl.BlockSpec(gains.shape, lambda t, place: (0, 0, 0)),
            ]
            + in_specs,
            out_specs=out_specs,
            scratch_shapes=[pltpu.VMEM((rows, columns), bf16)],
        ),
        out_shape=out_shape,
        compiler_params=params,
        cost_estimate=cost(
            2 * rows * width * len(steps) * columns,
            2 * width * len(steps) * columns + 2 * rows * width,
        ),
        name="project",
    )(place, weights, gains, *(first or prepared))
    blocks = [found[i * groups : (i + 1) * groups] for i in range(len(sets))]
    return blocks, found[len(sets) * groups :]


def attend_body(place_ref, *refs, groups, low_lane, key_room, query_rows, key_cols):
    query_refs, sources = refs[:groups], refs[groups:-5]
    out_ref, keys, values, queries, results = refs[-5:]
    rows, size = out_ref.shape[1:]
    plane = place_ref[0]
    blocks = [(source, k) for source in sources for k in range(groups)]
    piece = 128 if rows % 128 == 0 else rows
    align = lambda count: pl.multiple_of((count + 15) // 16 * 16, 16)
    line = lax.broadcasted_iota(jnp.int32, (piece, size), 0)

    found = []
    for source, block in blocks:
        live = (source[block, :, :size].astype(f32) < dead_limit).astype(f32)
        found.append(jnp.max(jnp.sum(live, axis=0, keepdims=True)).astype(jnp.int32))

    offset = jnp.int32(0)
    for (source, block), count in zip(blocks, found):
        for part in range(rows // piece):

            @pl.when(part * piece < count)
            def _():
                here = pl.ds(pl.multiple_of(offset + part * piece, 16), piece)
                there = pl.ds(part * piece, piece)
                live = line + part * piece < count
                key = jnp.where(live, source[block, there, :size].astype(f32), 0.0)
                keys[here, :] = key.astype(bf16)
                values[here, :size] = source[block, there, size:]
                values[here, size:] = live.astype(f32).astype(bf16)

        offset = pl.multiple_of(offset + align(count), 16)

    def clear(step, carry):
        here = pl.ds(pl.multiple_of(offset + step * 16, 16), 16)
        keys[here, :] = jnp.zeros((16, size), bf16)
        values[here, :] = jnp.zeros((16, 2 * size), bf16)
        return carry

    lax.fori_loop(0, (key_room - offset) // 16, clear, 0)

    mine = found[:groups]
    starts = []
    start = jnp.int32(0)
    for k in range(groups):
        starts.append(start)
        for part in range(rows // piece):

            @pl.when(part * piece < mine[k])
            def _():
                here = pl.ds(pl.multiple_of(start + part * piece, 16), piece)
                there = pl.ds(part * piece, piece)
                queries[here, :] = query_refs[k][0, there, low_lane : low_lane + size]

        start = pl.multiple_of(start + align(mine[k]), 16)

    def one_tile(tile, carry):
        here = pl.ds(pl.multiple_of(tile * query_rows, query_rows), query_rows)
        query = queries[here, :]
        total = jnp.zeros((query_rows, 2 * size), f32)
        for low in range(0, key_room, key_cols):
            high = min(low + key_cols, key_room)
            scores = lax.dot_general(
                query, keys[low:high, :], (((1,), (1,)), ((), ())), preferred_element_type=f32
            )
            weights = jnp.exp(scores).astype(bf16)
            total += jnp.dot(weights, values[low:high, :], preferred_element_type=f32)
        results[here, :] = (total[:, :size] / total[:, size:]).astype(bf16)
        return carry

    lax.fori_loop(0, (start + query_rows - 1) // query_rows, one_tile, 0)

    for k in range(groups):
        for part in range(rows // piece):
            here = pl.ds(pl.multiple_of(starts[k] + part * piece, 16), piece)
            live = line + part * piece < mine[k]
            out_ref[lax.bitwise_xor(plane, k), part * piece : (part + 1) * piece, :] = jnp.where(
                live, results[here, :].astype(f32), 0.0
            ).astype(bf16)


def attend(place, queries, low_lane, keyvals, shards):
    groups = len(queries)
    rows = keyvals[0].shape[1]
    size = keyvals[0].shape[2] // 2
    running = shards * rows // 2
    key_room = -(-(running + 16 * shards) // 256) * 256
    query_rows = 256
    query_room = -(-groups * rows // query_rows) * query_rows + rows
    query_block = (1,) + queries[0].shape[1:]
    return pl.pallas_call(
        functools.partial(
            attend_body,
            groups=groups,
            low_lane=low_lane,
            key_room=key_room,
            query_rows=query_rows,
            key_cols=256,
        ),
        grid_spec=pltpu.PrefetchScalarGridSpec(
            num_scalar_prefetch=1,
            grid=(1,),
            in_specs=[pl.BlockSpec(query_block, lambda i, place: (0, 0, 0))] * groups
            + [pl.BlockSpec(keyvals[0].shape, lambda i, place: (0, 0, 0))] * len(keyvals),
            out_specs=pl.BlockSpec((groups, rows, size), lambda i, place: (0, 0, 0)),
            scratch_shapes=[
                pltpu.VMEM((key_room + rows, size), bf16),
                pltpu.VMEM((key_room + rows, 2 * size), bf16),
                pltpu.VMEM((query_room, size), bf16),
                pltpu.VMEM((query_room, size), bf16),
            ],
        ),
        out_shape=jax.ShapeDtypeStruct((groups, rows, size), bf16),
        compiler_params=params,
        cost_estimate=cost(
            8 * groups * rows // 2 * running * size,
            4 * shards * rows * size,
            groups * rows // 2 * running,
        ),
        name="attend",
    )(place, *queries, *keyvals)


def finish_body(place_ref, *refs, chunks, others, has_sum, last):
    refs = list(refs)
    out_ref = refs.pop()
    total = refs.pop(0)[...] if has_sum else None
    for m in range(1 + others):
        attended_refs, weight_ref = refs[:chunks], refs[chunks]
        refs = refs[chunks + 1 :]
        wide = jnp.concatenate(
            [ref[g] for ref in attended_refs for g in range(ref.shape[0])], axis=-1
        )
        weight = weight_ref[0, 0] if m else weight_ref[...]
        term = jnp.dot(wide, weight, preferred_element_type=f32)
        total = term if total is None else total + term
    if last:
        rounded = total.astype(bf16)
        out_ref[...] = jnp.dot(refs[0][...], rounded, preferred_element_type=f32).astype(bf16)
    else:
        out_ref[...] = total


def finish(place, total, attended, w_out, other_weights, back, first_chunk):
    groups, rows, size = attended[0][0].shape
    split, head_shards, _, half = other_weights.shape
    chunks = len(attended)
    out_width = split * half
    depth = chunks * groups * size
    block = first_chunk // chunks
    mine = lambda i, place: (0, i)
    own = lambda i, place: (block, split * place[2] + i)
    block_a = pl.BlockSpec((groups, rows, size), lambda i, place: (0, 0, 0))
    specs, operands = [], []
    if total is not None:
        specs.append(pl.BlockSpec((rows, half), mine))
        operands.append(total)
    for mask in range(head_shards):
        specs += [block_a] * chunks
        operands += [found[mask] for found in attended]
        if mask == 0:
            specs.append(pl.BlockSpec((depth, half), own))
            operands.append(w_out)
        else:
            specs.append(
                pl.BlockSpec(
                    (1, 1, depth, half),
                    lambda i, place, mask=mask: (i, lax.bitwise_xor(place[2], mask), block, 0),
                )
            )
            operands.append(other_weights)
    last = back is not None
    if last:
        specs.append(pl.BlockSpec(back.shape, lambda i, place: (0, 0)))
        operands.append(back)
    return pl.pallas_call(
        functools.partial(
            finish_body,
            chunks=chunks,
            others=head_shards - 1,
            has_sum=total is not None,
            last=last,
        ),
        grid_spec=pltpu.PrefetchScalarGridSpec(
            num_scalar_prefetch=1,
            grid=(split,),
            in_specs=specs,
            out_specs=pl.BlockSpec((rows, half), mine),
        ),
        out_shape=jax.ShapeDtypeStruct((rows, out_width), bf16 if last else f32),
        compiler_params=params,
        cost_estimate=cost(
            2 * rows * depth * head_shards * out_width,
            2 * depth * head_shards * out_width + 8 * rows * out_width,
        ),
        name="finish",
    )(place, *operands)


def splits(out_width, head_shards):
    return head_shards == 2 and out_width % 256 == 0


def fetch_weights(w_out, me, side, head_shards):
    depth, width = w_out.shape
    out_width = width // head_shards
    if not splits(out_width, head_shards):
        blocks = jnp.transpose(w_out.reshape(depth, head_shards, out_width), (1, 0, 2))
        return lax.all_to_all(blocks, "head", split_axis=0, concat_axis=0, tiled=True)
    half = out_width // 2
    column = (1 - side) * out_width + (me % 2) * half
    return lax.all_gather(lax.dynamic_slice(w_out, (0, column), (depth, half)), "head")


def share_weights(found, out_width, head_shards):
    if not splits(out_width, head_shards):
        return found[None]
    pairs = [[i, i + 1] for i in range(0, lax.axis_size("seq"), 2)]
    return lax.all_gather(found, "seq", axis_index_groups=pairs)


def per_device(tokens, survive, norm_gain, w_qkv, qk_gain, w_out):
    heads, size = qk_gain.shape[1:]
    shards, head_shards = lax.axis_size("seq"), lax.axis_size("head")
    groups = math.gcd(heads & -heads, shards & -shards)
    ring = shards // groups
    chunks = heads // groups
    me, side = lax.axis_index("seq"), lax.axis_index("head")
    place = jnp.stack([me // ring, me % ring, side]).astype(jnp.int32)
    planes = [[i + ring * g for g in range(groups)] for i in range(ring)]

    def swap(blocks):
        return [blocks[0]] + [flip(blocks[k], "seq", k * ring) for k in range(1, groups)]

    def stack(blocks):
        return jnp.concatenate([block[:, :, : 2 * size] for block in blocks])

    def everywhere(stacked, gate):
        found = {0: stacked}
        mask = ring // 2
        while mask:
            for known in list(found):
                source = found[known]
                if gate is not None and mask < ring // 2:
                    source = chain(source, gate)
                found[known | mask] = flip(source, "seq", mask)
            mask //= 2
        return [found[mask] for mask in range(ring)]

    def send_back(blocks):
        if groups == 1:
            return blocks
        return lax.all_to_all(
            blocks, "seq", split_axis=0, concat_axis=0, axis_index_groups=planes, tiled=True
        )

    def across(blocks):
        return [blocks] + [flip(blocks, "head", mask) for mask in range(1, head_shards)]

    weights = jnp.transpose(w_qkv, (1, 0, 2))
    gains = jnp.transpose(qk_gain, (1, 0, 2))

    plan = [[((1, 2, 0), 0)]]
    plan += [[((1, 2), chunk)] for chunk in range(1, chunks)]
    if chunks > 1:
        plan[1] += [((0,), chunk) for chunk in range(1, chunks)]
    arrived, stacks, later, fetched, gate = [], [], [], None, None
    for i, sets in enumerate(plan):
        if i == 0:
            operands = (survive, tokens, norm_gain)
            blocks, rest = project(place, None, weights, gains, sets, groups, operands)
            normed, chosen, back, count = rest
        else:
            source = chain(normed, stacks[i - 2]) if i > 1 else normed
            prepared = (count, source, chosen)
            blocks, _ = project(place, prepared, weights, gains, sets, groups)
            stacks.append(stack(list(chain(tuple(arrived[i - 1]), blocks[0][0]))))
        if i == min(1, chunks - 1):
            later = blocks[1:]
            fetched = fetch_weights(chain(w_out, blocks[0][0]), me, side, head_shards)
        arrived.append(swap(blocks[0]))
        gate = blocks[0][0]

    attended = []
    query, low_lane = arrived[0], 2 * size
    for chunk in range(chunks):
        if chunk == chunks - 1:
            stacks.append(stack(list(chain(tuple(arrived[-1]), *attended[:1]))))
        upcoming = None
        if chunk < chunks - 1:
            upcoming = swap(list(chain(tuple(later[chunk]), stacks[min(chunk + 1, len(stacks) - 1)])))
        keyvals = everywhere(stacks[chunk], gate)
        before = (stacks[-1],) + tuple(attended[-1:])
        query = [chain(query[0], *before)] + list(query[1:])
        attended.append(attend(place, query, low_lane, keyvals, shards))
        query, low_lane = upcoming, 0
        gate = tuple(upcoming[1:]) if upcoming else None
    out_width = w_out.shape[1] // head_shards
    other_weights = share_weights(chain(fetched, attended[-1]), out_width, head_shards)
    attended = [send_back(found) for found in attended]
    total = None
    if chunks > 1:
        sooner = [across(found) for found in attended[:-1]]
        total = finish(place, None, sooner, w_out, other_weights, None, 0)
    final = across(attended[-1] if total is None else chain(attended[-1], total))
    return finish(place, total, [final], w_out, other_weights, back, chunks - 1)


def solution(mesh):
    placed = (
        P("seq", None),
        P("seq"),
        P(),
        P(None, None, "head"),
        P(None, "head", None),
        P("head", None),
    )
    return jax.shard_map(
        per_device, mesh=mesh, in_specs=placed, out_specs=P("seq", "head"), check_vma=False
    )
```

```python
import functools
import math

import jax
import jax.numpy as jnp
from jax import lax
from jax.experimental import pallas as pl
from jax.experimental.pallas import tpu as pltpu
from jax.sharding import PartitionSpec as P

epsilon = 1e-06
dead_mark = 1e30
dead_limit = 1e15
mib = 1 << 20
f32 = jnp.float32
bf16 = jnp.bfloat16
params = pltpu.CompilerParams(vmem_limit_bytes=60 * mib)


def cost(flops, bytes_accessed, exps=0):
    return pl.CostEstimate(
        flops=int(flops), bytes_accessed=int(bytes_accessed), transcendentals=int(exps)
    )


def flip(values, axis, mask):
    size = lax.axis_size(axis)
    return lax.ppermute(values, axis, [(i, i ^ mask) for i in range(size)])


def chain(values, *earlier):
    return lax.optimization_barrier((values, earlier))[0]


def layer_norm(values, gain):
    center = values - jnp.mean(values, axis=-1, keepdims=True)
    spread = jnp.mean(center * center, axis=-1, keepdims=True)
    return center * lax.rsqrt(spread + epsilon) * gain


def prepare(survive_ref, tokens_ref, gain_ref, normed_ref, chosen_ref, back_ref, count_ref):
    positions = tokens_ref.shape[0]
    first = lax.broadcasted_iota(jnp.int32, (positions, positions), 0)
    second = lax.broadcasted_iota(jnp.int32, (positions, positions), 1)
    live = jnp.broadcast_to(survive_ref[...].reshape(1, positions), (8, positions)).astype(f32)
    upper = (first <= second).astype(f32).astype(bf16)
    rank = jnp.dot(live.astype(bf16), upper, preferred_element_type=f32)
    target = jnp.where(live > 0.5, rank - 1.0, -1.0)
    chosen_ref[...] = (first == target[:1].astype(jnp.int32)).astype(f32).astype(bf16)
    home = jnp.transpose(target)[:, :1].astype(jnp.int32)
    back_ref[...] = (second == home).astype(f32).astype(bf16)
    count_ref[0, 0] = jnp.max(rank).astype(jnp.int32)
    gain = gain_ref[...].reshape(1, gain_ref.shape[0])
    rows = 128 if positions % 128 == 0 else positions
    for low in range(0, positions, rows):
        part = tokens_ref[low : low + rows, :].astype(f32)
        normed_ref[low : low + rows, :] = layer_norm(part, gain).astype(bf16)


def project_body(place_ref, *refs, steps, groups, first):
    refs = list(refs)
    result_ref = refs.pop()
    weight_ref, gain_ref = refs[:2]
    if first:
        survive_ref, tokens_ref, norm_gain_ref = refs[2:5]
        outs, (normed_ref, chosen_ref, back_ref, count_ref) = refs[5:-4], refs[-4:]

        @pl.when(pl.program_id(0) == 0)
        def _():
            prepare(
                survive_ref, tokens_ref, norm_gain_ref, normed_ref, chosen_ref, back_ref, count_ref
            )

    else:
        (count_ref, normed_ref, chosen_ref), outs = refs[2:5], refs[5:]
    rows = normed_ref.shape[0]
    size = gain_ref.shape[2]
    plane = place_ref[0]
    for step, (kind, chunk, target, low) in enumerate(steps):

        @pl.when(pl.program_id(0) == step)
        def _():
            result = jnp.dot(normed_ref[...], weight_ref[0], preferred_element_type=f32)
            for g in range(groups):
                part = result[:, g * size : (g + 1) * size]
                if kind != 2:
                    gain = gain_ref[chunk * groups + g, kind : kind + 1, :]
                    if kind == 0:
                        gain = gain * (1.0 / math.sqrt(size))
                    part = layer_norm(part, gain)
                result_ref[:, g * size : (g + 1) * size] = part.astype(bf16)
            packed = jnp.dot(chosen_ref[...], result_ref[...], preferred_element_type=f32)
            if kind == 1:
                row = lax.broadcasted_iota(jnp.int32, (rows, groups * size), 0)
                packed = jnp.where(row < count_ref[0, 0], packed, dead_mark)
            result_ref[...] = packed.astype(bf16)
            for k in range(groups):
                start = pl.multiple_of(lax.bitwise_xor(plane, k) * size, size)
                found = result_ref[:, pl.ds(start, size)]
                outs[target * groups + k][0, :, low : low + size] = found


def project(place, prepared, weights, gains, sets, groups, first=None):
    size = gains.shape[2]
    width = weights.shape[1]
    columns = groups * size
    fixed = lambda t, place: (0, 0)
    line = lambda t, place: (0,)
    smem = pl.BlockSpec(memory_space=pltpu.SMEM)
    rows = (first or prepared)[1].shape[0]
    square = pl.BlockSpec((rows, rows), fixed)
    whole = pl.BlockSpec((rows, width), fixed)
    steps = [
        (kind, chunk, target, i * size)
        for target, (kinds, chunk) in enumerate(sets)
        for i, kind in enumerate(kinds)
    ]

    def weight_index(t, place):
        kind, chunk = steps[0][:2]
        for step, found in enumerate(steps):
            kind = jnp.where(t == step, found[0], kind)
            chunk = jnp.where(t == step, found[1], chunk)
        return (kind, 0, chunk)

    widths = [len(kinds) * size for kinds, _ in sets for _ in range(groups)]
    out_specs = [pl.BlockSpec((1, rows, wide), lambda t, place: (0, 0, 0)) for wide in widths]
    out_shape = [jax.ShapeDtypeStruct((1, rows, wide), bf16) for wide in widths]
    if first:
        in_specs = [pl.BlockSpec((rows,), line), whole, pl.BlockSpec((width,), line)]
        out_specs += [whole, square, square, smem]
        out_shape += [
            jax.ShapeDtypeStruct((rows, width), bf16),
            jax.ShapeDtypeStruct((rows, rows), bf16),
            jax.ShapeDtypeStruct((rows, rows), bf16),
            jax.ShapeDtypeStruct((1, 1), jnp.int32),
        ]
    else:
        in_specs = [smem, whole, square]
    found = pl.pallas_call(
        functools.partial(project_body, steps=steps, groups=groups, first=first is not None),
        grid_spec=pltpu.PrefetchScalarGridSpec(
            num_scalar_prefetch=1,
            grid=(len(steps),),
            in_specs=[
                pl.BlockSpec((1, width, columns), weight_index),
                pl.BlockSpec(gains.shape, lambda t, place: (0, 0, 0)),
            ]
            + in_specs,
            out_specs=out_specs,
            scratch_shapes=[pltpu.VMEM((rows, columns), bf16)],
        ),
        out_shape=out_shape,
        compiler_params=params,
        cost_estimate=cost(
            2 * rows * width * len(steps) * columns,
            2 * width * len(steps) * columns + 2 * rows * width,
        ),
        name="project",
    )(place, weights, gains, *(first or prepared))
    blocks = [found[i * groups : (i + 1) * groups] for i in range(len(sets))]
    return blocks, found[len(sets) * groups :]


def attend_body(place_ref, *refs, groups, ordered, low_lane, key_room, query_rows, key_cols):
    outs = 1 if ordered else groups
    query_refs, sources, out_refs = refs[:groups], refs[groups : -4 - outs], refs[-4 - outs : -4]
    keys, values, queries, results = refs[-4:]
    rows, size = out_refs[0].shape[1:]
    plane = place_ref[0]
    blocks = [(source, k) for source in sources for k in range(groups)]
    piece = 128 if rows % 128 == 0 else rows
    align = lambda count: pl.multiple_of((count + 15) // 16 * 16, 16)
    line = lax.broadcasted_iota(jnp.int32, (piece, size), 0)

    found = []
    for source, block in blocks:
        live = (source[block, :, :size].astype(f32) < dead_limit).astype(f32)
        found.append(jnp.max(jnp.sum(live, axis=0, keepdims=True)).astype(jnp.int32))

    offset = jnp.int32(0)
    for (source, block), count in zip(blocks, found):
        for part in range(rows // piece):

            @pl.when(part * piece < count)
            def _():
                here = pl.ds(pl.multiple_of(offset + part * piece, 16), piece)
                there = pl.ds(part * piece, piece)
                live = line + part * piece < count
                key = jnp.where(live, source[block, there, :size].astype(f32), 0.0)
                keys[here, :] = key.astype(bf16)
                values[here, :size] = source[block, there, size:]
                values[here, size:] = live.astype(f32).astype(bf16)

        offset = pl.multiple_of(offset + align(count), 16)

    def clear(step, carry):
        here = pl.ds(pl.multiple_of(offset + step * 16, 16), 16)
        keys[here, :] = jnp.zeros((16, size), bf16)
        values[here, :] = jnp.zeros((16, 2 * size), bf16)
        return carry

    lax.fori_loop(0, (key_room - offset) // 16, clear, 0)

    mine = found[:groups]
    starts = []
    start = jnp.int32(0)
    for k in range(groups):
        starts.append(start)
        for part in range(rows // piece):

            @pl.when(part * piece < mine[k])
            def _():
                here = pl.ds(pl.multiple_of(start + part * piece, 16), piece)
                there = pl.ds(part * piece, piece)
                queries[here, :] = query_refs[k][0, there, low_lane : low_lane + size]

        start = pl.multiple_of(start + align(mine[k]), 16)

    def one_tile(tile, carry):
        here = pl.ds(pl.multiple_of(tile * query_rows, query_rows), query_rows)
        query = queries[here, :]
        total = jnp.zeros((query_rows, 2 * size), f32)
        for low in range(0, key_room, key_cols):
            high = min(low + key_cols, key_room)
            scores = lax.dot_general(
                query, keys[low:high, :], (((1,), (1,)), ((), ())), preferred_element_type=f32
            )
            weights = jnp.exp(scores).astype(bf16)
            total += jnp.dot(weights, values[low:high, :], preferred_element_type=f32)
        results[here, :] = (total[:, :size] / total[:, size:]).astype(bf16)
        return carry

    lax.fori_loop(0, (start + query_rows - 1) // query_rows, one_tile, 0)

    for k in range(groups):
        for part in range(rows // piece):
            here = pl.ds(pl.multiple_of(starts[k] + part * piece, 16), piece)
            live = line + part * piece < mine[k]
            kept = jnp.where(live, results[here, :].astype(f32), 0.0).astype(bf16)
            block = lax.bitwise_xor(plane, k) if ordered else 0
            out_refs[0 if ordered else k][block, part * piece : (part + 1) * piece, :] = kept


def attend(place, queries, low_lane, keyvals, shards, ordered):
    groups = len(queries)
    rows = keyvals[0].shape[1]
    size = keyvals[0].shape[2] // 2
    running = shards * rows // 2
    key_room = -(-(running + 16 * shards) // 256) * 256
    query_rows = 256
    query_room = -(-groups * rows // query_rows) * query_rows + rows
    query_block = (1,) + queries[0].shape[1:]
    outs, wide = (1, groups) if ordered else (groups, 1)
    return pl.pallas_call(
        functools.partial(
            attend_body,
            groups=groups,
            ordered=ordered,
            low_lane=low_lane,
            key_room=key_room,
            query_rows=query_rows,
            key_cols=256,
        ),
        grid_spec=pltpu.PrefetchScalarGridSpec(
            num_scalar_prefetch=1,
            grid=(1,),
            in_specs=[pl.BlockSpec(query_block, lambda i, place: (0, 0, 0))] * groups
            + [pl.BlockSpec(keyvals[0].shape, lambda i, place: (0, 0, 0))] * len(keyvals),
            out_specs=[pl.BlockSpec((wide, rows, size), lambda i, place: (0, 0, 0))] * outs,
            scratch_shapes=[
                pltpu.VMEM((key_room + rows, size), bf16),
                pltpu.VMEM((key_room + rows, 2 * size), bf16),
                pltpu.VMEM((query_room, size), bf16),
                pltpu.VMEM((query_room, size), bf16),
            ],
        ),
        out_shape=[jax.ShapeDtypeStruct((wide, rows, size), bf16)] * outs,
        compiler_params=params,
        cost_estimate=cost(
            8 * groups * rows // 2 * running * size,
            4 * shards * rows * size,
            groups * rows // 2 * running,
        ),
        name="attend",
    )(place, *queries, *keyvals)


def finish_body(place_ref, *refs, chunks, others, has_sum, last, ordered):
    refs = list(refs)
    wide_ref = refs.pop()
    out_ref = refs.pop()
    total = refs.pop(0)[...] if has_sum else None
    for m in range(1 + others):
        attended_refs, weight_ref = refs[:chunks], refs[chunks]
        refs = refs[chunks + 1 :]
        for i, ref in enumerate(attended_refs):
            groups, _, size = ref.shape
            for g in range(groups):
                head = i * groups + (g if ordered else lax.bitwise_xor(place_ref[0], g))
                start = head * size if ordered else pl.multiple_of(head * size, size)
                wide_ref[:, pl.ds(start, size)] = ref[g]
        wide = wide_ref[...]
        weight = weight_ref[0, 0] if m else weight_ref[...]
        term = jnp.dot(wide, weight, preferred_element_type=f32)
        total = term if total is None else total + term
    if last:
        rounded = total.astype(bf16)
        out_ref[...] = jnp.dot(refs[0][...], rounded, preferred_element_type=f32).astype(bf16)
    else:
        out_ref[...] = total


def finish(place, total, attended, w_out, other_weights, back, first_chunk, ordered):
    groups, rows, size = attended[0][0].shape
    split, head_shards, _, half = other_weights.shape
    chunks = len(attended)
    out_width = split * half
    depth = chunks * groups * size
    block = first_chunk // chunks
    mine = lambda i, place: (0, i)
    own = lambda i, place: (block, split * place[2] + i)
    block_a = pl.BlockSpec((groups, rows, size), lambda i, place: (0, 0, 0))
    specs, operands = [], []
    if total is not None:
        specs.append(pl.BlockSpec((rows, half), mine))
        operands.append(total)
    for mask in range(head_shards):
        specs += [block_a] * chunks
        operands += [found[mask] for found in attended]
        if mask == 0:
            specs.append(pl.BlockSpec((depth, half), own))
            operands.append(w_out)
        else:
            specs.append(
                pl.BlockSpec(
                    (1, 1, depth, half),
                    lambda i, place, mask=mask: (i, lax.bitwise_xor(place[2], mask), block, 0),
                )
            )
            operands.append(other_weights)
    last = back is not None
    if last:
        specs.append(pl.BlockSpec(back.shape, lambda i, place: (0, 0)))
        operands.append(back)
    return pl.pallas_call(
        functools.partial(
            finish_body,
            chunks=chunks,
            others=head_shards - 1,
            has_sum=total is not None,
            last=last,
            ordered=ordered,
        ),
        grid_spec=pltpu.PrefetchScalarGridSpec(
            num_scalar_prefetch=1,
            grid=(split,),
            in_specs=specs,
            out_specs=pl.BlockSpec((rows, half), mine),
            scratch_shapes=[pltpu.VMEM((rows, depth), bf16)],
        ),
        out_shape=jax.ShapeDtypeStruct((rows, out_width), bf16 if last else f32),
        compiler_params=params,
        cost_estimate=cost(
            2 * rows * depth * head_shards * out_width,
            2 * depth * head_shards * out_width + 8 * rows * out_width,
        ),
        name="finish",
    )(place, *operands)


def splits(out_width, head_shards):
    return head_shards == 2 and out_width % 256 == 0


def fetch_weights(w_out, me, side, head_shards):
    depth, width = w_out.shape
    out_width = width // head_shards
    if not splits(out_width, head_shards):
        blocks = jnp.transpose(w_out.reshape(depth, head_shards, out_width), (1, 0, 2))
        return lax.all_to_all(blocks, "head", split_axis=0, concat_axis=0, tiled=True)
    half = out_width // 2
    column = (1 - side) * out_width + (me % 2) * half
    return lax.all_gather(lax.dynamic_slice(w_out, (0, column), (depth, half)), "head")


def share_weights(found, out_width, head_shards):
    if not splits(out_width, head_shards):
        return found[None]
    pairs = [[i, i + 1] for i in range(0, lax.axis_size("seq"), 2)]
    return lax.all_gather(found, "seq", axis_index_groups=pairs)


def per_device(tokens, survive, norm_gain, w_qkv, qk_gain, w_out):
    heads, size = qk_gain.shape[1:]
    shards, head_shards = lax.axis_size("seq"), lax.axis_size("head")
    groups = math.gcd(heads & -heads, shards & -shards)
    ring = shards // groups
    chunks = heads // groups
    me, side = lax.axis_index("seq"), lax.axis_index("head")
    place = jnp.stack([me // ring, me % ring, side]).astype(jnp.int32)
    planes = [[i + ring * g for g in range(groups)] for i in range(ring)]

    def swap(blocks):
        return [blocks[0]] + [flip(blocks[k], "seq", k * ring) for k in range(1, groups)]

    def stack(blocks):
        return jnp.concatenate([block[:, :, : 2 * size] for block in blocks])

    def everywhere(stacked, gate):
        found = {0: stacked}
        mask = ring // 2
        while mask:
            for known in list(found):
                source = found[known]
                if gate is not None and mask < ring // 2:
                    source = chain(source, gate)
                found[known | mask] = flip(source, "seq", mask)
            mask //= 2
        return [found[mask] for mask in range(ring)]

    def send_back(blocks):
        if groups == 1:
            return blocks
        return lax.all_to_all(
            blocks, "seq", split_axis=0, concat_axis=0, axis_index_groups=planes, tiled=True
        )

    def across(blocks):
        return [blocks] + [flip(blocks, "head", mask) for mask in range(1, head_shards)]

    weights = jnp.transpose(w_qkv, (1, 0, 2))
    gains = jnp.transpose(qk_gain, (1, 0, 2))

    def later(values, *earlier):
        return jnp.maximum(chain(values, *earlier), 0)

    def first(blocks):
        return blocks[min(1, groups - 1)]

    def send(blocks, *earlier):
        return swap(list(chain(tuple(blocks), *earlier)) if earlier else blocks)

    operands = (survive, tokens, norm_gain)
    sets = [((1, 2, 0), 0)]
    (blocks,), rest = project(place, None, weights, gains, sets, groups, operands)
    normed, chosen, back, count = rest
    arrived = [swap(blocks)]
    fetched = fetch_weights(chain(w_out, later(count)), me, side, head_shards)

    rest, asked = range(1, chunks), []
    if chunks > 1:
        prepared = (count, chain(normed, first(arrived[0])), chosen)
        sets = [((1, 2), chunk) for chunk in rest]
        made, _ = project(place, prepared, weights, gains, sets, groups)
        stacks = [stack(list(chain(tuple(arrived[0]), made[0][0])))]
        arrived.append(send(made[0]))
        for blocks in made[1:]:
            arrived.append(send(blocks, first(arrived[-1])))
        hop = flip(stacks[0], "seq", ring // 2) if ring > 1 else stacks[0]
        stacks.append(stack(arrived[1]))
        ready = later(count, hop, stacks[1])
        sets = [((0,), chunk) for chunk in rest]
        made, _ = project(place, (ready, normed, chosen), weights, gains, sets, groups)
        gate = made[0][0]
        stacks += [stack(blocks) for blocks in arrived[2:]]
        for blocks in made:
            asked.append(send(blocks, first(asked[-1]) if asked else stacks[-1]))
    else:
        gate, stacks = None, [stack(arrived[0])]

    attended, returned = [], []
    query, low_lane = arrived[0], 2 * size
    for chunk in range(chunks):
        final = chunk == chunks - 1
        keyvals = everywhere(stacks[chunk], gate)
        before = (stacks[-1],) + tuple(attended[-1:]) + tuple(returned[:1] if final else [])
        ready = later(place, *query[1:], *before)
        found = attend(ready, query, low_lane, keyvals, shards, not final)
        attended.append(found[0])
        if chunk == max(chunks - 2, 0):
            out_width = w_out.shape[1] // head_shards
            other_weights = share_weights(chain(fetched, found[0]), out_width, head_shards)
        if final:
            returned.append(jnp.concatenate(swap(found)))
        else:
            returned.append(send_back(found[0]))
            query, low_lane = asked[chunk], 0
            gate = tuple(query)
    total = None
    if chunks > 1:
        sooner = [across(found) for found in returned[:-1]]
        total = finish(place, None, sooner, w_out, other_weights, None, 0, True)
    last = across(returned[-1] if total is None else chain(returned[-1], total))
    return finish(place, total, [last], w_out, other_weights, back, chunks - 1, False)


def solution(mesh):
    placed = (
        P("seq", None),
        P("seq"),
        P(),
        P(None, None, "head"),
        P(None, "head", None),
        P("head", None),
    )
    return jax.shard_map(
        per_device, mesh=mesh, in_specs=placed, out_specs=P("seq", "head"), check_vma=False
    )
```

```python
import functools
import math

import jax
import jax.numpy as jnp
from jax import lax
from jax.experimental import pallas as pl
from jax.experimental.pallas import tpu as pltpu
from jax.sharding import PartitionSpec as P

epsilon = 1e-06
dead_mark = 1e30
dead_limit = 1e15
mib = 1 << 20
f32 = jnp.float32
bf16 = jnp.bfloat16
params = pltpu.CompilerParams(vmem_limit_bytes=60 * mib)


def cost(flops, bytes_accessed, exps=0):
    return pl.CostEstimate(
        flops=int(flops), bytes_accessed=int(bytes_accessed), transcendentals=int(exps)
    )


def flip(values, axis, mask):
    size = lax.axis_size(axis)
    return lax.ppermute(values, axis, [(i, i ^ mask) for i in range(size)])


def chain(values, *earlier):
    return lax.optimization_barrier((values, earlier))[0]


def layer_norm(values, gain):
    center = values - jnp.mean(values, axis=-1, keepdims=True)
    spread = jnp.mean(center * center, axis=-1, keepdims=True)
    return center * lax.rsqrt(spread + epsilon) * gain


def prepare(survive_ref, tokens_ref, gain_ref, normed_ref, chosen_ref, back_ref, count_ref):
    positions = tokens_ref.shape[0]
    first = lax.broadcasted_iota(jnp.int32, (positions, positions), 0)
    second = lax.broadcasted_iota(jnp.int32, (positions, positions), 1)
    live = jnp.broadcast_to(survive_ref[...].reshape(1, positions), (8, positions)).astype(f32)
    upper = (first <= second).astype(f32).astype(bf16)
    rank = jnp.dot(live.astype(bf16), upper, preferred_element_type=f32)
    target = jnp.where(live > 0.5, rank - 1.0, -1.0)
    chosen_ref[...] = (first == target[:1].astype(jnp.int32)).astype(f32).astype(bf16)
    home = jnp.transpose(target)[:, :1].astype(jnp.int32)
    back_ref[...] = (second == home).astype(f32).astype(bf16)
    count_ref[0, 0] = jnp.max(rank).astype(jnp.int32)
    gain = gain_ref[...].reshape(1, gain_ref.shape[0])
    rows = 128 if positions % 128 == 0 else positions
    for low in range(0, positions, rows):
        part = tokens_ref[low : low + rows, :].astype(f32)
        normed_ref[low : low + rows, :] = layer_norm(part, gain).astype(bf16)


def project_body(place_ref, *refs, steps, groups, first):
    refs = list(refs)
    result_ref = refs.pop()
    weight_ref, gain_ref = refs[:2]
    if first:
        survive_ref, tokens_ref, norm_gain_ref = refs[2:5]
        outs, (normed_ref, chosen_ref, back_ref, count_ref) = refs[5:-4], refs[-4:]

        @pl.when(pl.program_id(0) == 0)
        def _():
            prepare(
                survive_ref, tokens_ref, norm_gain_ref, normed_ref, chosen_ref, back_ref, count_ref
            )

    else:
        (count_ref, normed_ref, chosen_ref), outs = refs[2:5], refs[5:]
    rows = normed_ref.shape[0]
    size = gain_ref.shape[2]
    plane = place_ref[0]
    for step, (kind, chunk, target, row, low) in enumerate(steps):

        @pl.when(pl.program_id(0) == step)
        def _():
            result = jnp.dot(normed_ref[...], weight_ref[0], preferred_element_type=f32)
            for g in range(groups):
                part = result[:, g * size : (g + 1) * size]
                if kind != 2:
                    gain = gain_ref[chunk * groups + g, kind : kind + 1, :]
                    if kind == 0:
                        gain = gain * (1.0 / math.sqrt(size))
                    part = layer_norm(part, gain)
                result_ref[:, g * size : (g + 1) * size] = part.astype(bf16)
            packed = jnp.dot(chosen_ref[...], result_ref[...], preferred_element_type=f32)
            if kind == 1:
                line = lax.broadcasted_iota(jnp.int32, (rows, groups * size), 0)
                packed = jnp.where(line < count_ref[0, 0], packed, dead_mark)
            result_ref[...] = packed.astype(bf16)
            for k in range(groups):
                start = pl.multiple_of(lax.bitwise_xor(plane, k) * size, size)
                found = result_ref[:, pl.ds(start, size)]
                outs[target * groups + k][row, :, low : low + size] = found


def project(place, prepared, weights, gains, sets, groups, first=None):
    size = gains.shape[2]
    width = weights.shape[1]
    columns = groups * size
    fixed = lambda t, place: (0, 0)
    line = lambda t, place: (0,)
    smem = pl.BlockSpec(memory_space=pltpu.SMEM)
    rows = (first or prepared)[1].shape[0]
    square = pl.BlockSpec((rows, rows), fixed)
    whole = pl.BlockSpec((rows, width), fixed)
    steps = [
        (kind, chunk, target, row, i * size)
        for target, (kinds, which) in enumerate(sets)
        for row, chunk in enumerate(which)
        for i, kind in enumerate(kinds)
    ]

    def weight_index(t, place):
        kind, chunk = steps[0][:2]
        for step, found in enumerate(steps):
            kind = jnp.where(t == step, found[0], kind)
            chunk = jnp.where(t == step, found[1], chunk)
        return (kind, 0, chunk)

    shapes = [
        (len(which), rows, len(kinds) * size) for kinds, which in sets for _ in range(groups)
    ]
    out_specs = [pl.BlockSpec(shape, lambda t, place: (0, 0, 0)) for shape in shapes]
    out_shape = [jax.ShapeDtypeStruct(shape, bf16) for shape in shapes]
    if first:
        in_specs = [pl.BlockSpec((rows,), line), whole, pl.BlockSpec((width,), line)]
        out_specs += [whole, square, square, smem]
        out_shape += [
            jax.ShapeDtypeStruct((rows, width), bf16),
            jax.ShapeDtypeStruct((rows, rows), bf16),
            jax.ShapeDtypeStruct((rows, rows), bf16),
            jax.ShapeDtypeStruct((1, 1), jnp.int32),
        ]
    else:
        in_specs = [smem, whole, square]
    found = pl.pallas_call(
        functools.partial(project_body, steps=steps, groups=groups, first=first is not None),
        grid_spec=pltpu.PrefetchScalarGridSpec(
            num_scalar_prefetch=1,
            grid=(len(steps),),
            in_specs=[
                pl.BlockSpec((1, width, columns), weight_index),
                pl.BlockSpec(gains.shape, lambda t, place: (0, 0, 0)),
            ]
            + in_specs,
            out_specs=out_specs,
            scratch_shapes=[pltpu.VMEM((rows, columns), bf16)],
        ),
        out_shape=out_shape,
        compiler_params=params,
        cost_estimate=cost(
            2 * rows * width * len(steps) * columns,
            2 * width * len(steps) * columns + 2 * rows * width,
        ),
        name="project",
    )(place, weights, gains, *(first or prepared))
    blocks = [found[i * groups : (i + 1) * groups] for i in range(len(sets))]
    return blocks, found[len(sets) * groups :]


def attend_body(place_ref, *refs, groups, ordered, low_lane, key_room, query_rows, key_cols):
    outs = 1 if ordered else groups
    query_refs, sources, out_refs = refs[:groups], refs[groups : -4 - outs], refs[-4 - outs : -4]
    keys, values, queries, results = refs[-4:]
    rows, size = out_refs[0].shape[1:]
    plane = place_ref[0]
    blocks = [(source, k) for source in sources for k in range(groups)]
    piece = 128 if rows % 128 == 0 else rows
    align = lambda count: pl.multiple_of((count + 15) // 16 * 16, 16)
    line = lax.broadcasted_iota(jnp.int32, (piece, size), 0)

    found = []
    for source, block in blocks:
        live = (source[block, :, :size].astype(f32) < dead_limit).astype(f32)
        found.append(jnp.max(jnp.sum(live, axis=0, keepdims=True)).astype(jnp.int32))

    offset = jnp.int32(0)
    for (source, block), count in zip(blocks, found):
        for part in range(rows // piece):

            @pl.when(part * piece < count)
            def _():
                here = pl.ds(pl.multiple_of(offset + part * piece, 16), piece)
                there = pl.ds(part * piece, piece)
                live = line + part * piece < count
                key = jnp.where(live, source[block, there, :size].astype(f32), 0.0)
                keys[here, :] = key.astype(bf16)
                values[here, :size] = source[block, there, size:]
                values[here, size:] = live.astype(f32).astype(bf16)

        offset = pl.multiple_of(offset + align(count), 16)

    def clear(step, carry):
        here = pl.ds(pl.multiple_of(offset + step * 16, 16), 16)
        keys[here, :] = jnp.zeros((16, size), bf16)
        values[here, :] = jnp.zeros((16, 2 * size), bf16)
        return carry

    lax.fori_loop(0, (key_room - offset) // 16, clear, 0)

    mine = found[:groups]
    starts = []
    start = jnp.int32(0)
    for k in range(groups):
        starts.append(start)
        for part in range(rows // piece):

            @pl.when(part * piece < mine[k])
            def _():
                here = pl.ds(pl.multiple_of(start + part * piece, 16), piece)
                there = pl.ds(part * piece, piece)
                queries[here, :] = query_refs[k][0, there, low_lane : low_lane + size]

        start = pl.multiple_of(start + align(mine[k]), 16)

    def one_tile(tile, carry):
        here = pl.ds(pl.multiple_of(tile * query_rows, query_rows), query_rows)
        query = queries[here, :]
        total = jnp.zeros((query_rows, 2 * size), f32)
        for low in range(0, key_room, key_cols):
            high = min(low + key_cols, key_room)
            scores = lax.dot_general(
                query, keys[low:high, :], (((1,), (1,)), ((), ())), preferred_element_type=f32
            )
            weights = jnp.exp(scores).astype(bf16)
            total += jnp.dot(weights, values[low:high, :], preferred_element_type=f32)
        results[here, :] = (total[:, :size] / total[:, size:]).astype(bf16)
        return carry

    lax.fori_loop(0, (start + query_rows - 1) // query_rows, one_tile, 0)

    for k in range(groups):
        for part in range(rows // piece):
            here = pl.ds(pl.multiple_of(starts[k] + part * piece, 16), piece)
            live = line + part * piece < mine[k]
            kept = jnp.where(live, results[here, :].astype(f32), 0.0).astype(bf16)
            block = lax.bitwise_xor(plane, k) if ordered else 0
            out_refs[0 if ordered else k][block, part * piece : (part + 1) * piece, :] = kept


def attend(place, queries, which, low_lane, keyvals, shards, ordered):
    groups = len(queries)
    rows = keyvals[0].shape[1]
    size = keyvals[0].shape[2] // 2
    running = shards * rows // 2
    key_room = -(-(running + 16 * shards) // 256) * 256
    query_rows = 256
    query_room = -(-groups * rows // query_rows) * query_rows + rows
    query_block = (1,) + queries[0].shape[1:]
    outs, wide = (1, groups) if ordered else (groups, 1)
    return pl.pallas_call(
        functools.partial(
            attend_body,
            groups=groups,
            ordered=ordered,
            low_lane=low_lane,
            key_room=key_room,
            query_rows=query_rows,
            key_cols=256,
        ),
        grid_spec=pltpu.PrefetchScalarGridSpec(
            num_scalar_prefetch=1,
            grid=(1,),
            in_specs=[pl.BlockSpec(query_block, lambda i, place: (which, 0, 0))] * groups
            + [pl.BlockSpec(keyvals[0].shape, lambda i, place: (0, 0, 0))] * len(keyvals),
            out_specs=[pl.BlockSpec((wide, rows, size), lambda i, place: (0, 0, 0))] * outs,
            scratch_shapes=[
                pltpu.VMEM((key_room + rows, size), bf16),
                pltpu.VMEM((key_room + rows, 2 * size), bf16),
                pltpu.VMEM((query_room, size), bf16),
                pltpu.VMEM((query_room, size), bf16),
            ],
        ),
        out_shape=[jax.ShapeDtypeStruct((wide, rows, size), bf16)] * outs,
        compiler_params=params,
        cost_estimate=cost(
            8 * groups * rows // 2 * running * size,
            4 * shards * rows * size,
            groups * rows // 2 * running,
        ),
        name="attend",
    )(place, *queries, *keyvals)


def finish_body(place_ref, *refs, chunks, others, has_sum, last, ordered):
    refs = list(refs)
    wide_ref = refs.pop()
    out_ref = refs.pop()
    total = refs.pop(0)[...] if has_sum else None
    for m in range(1 + others):
        attended_refs, weight_ref = refs[:chunks], refs[chunks]
        refs = refs[chunks + 1 :]
        for i, ref in enumerate(attended_refs):
            groups, _, size = ref.shape
            for g in range(groups):
                head = i * groups + (g if ordered else lax.bitwise_xor(place_ref[0], g))
                start = head * size if ordered else pl.multiple_of(head * size, size)
                wide_ref[:, pl.ds(start, size)] = ref[g]
        wide = wide_ref[...]
        weight = weight_ref[0, 0] if m else weight_ref[...]
        term = jnp.dot(wide, weight, preferred_element_type=f32)
        total = term if total is None else total + term
    if last:
        rounded = total.astype(bf16)
        out_ref[...] = jnp.dot(refs[0][...], rounded, preferred_element_type=f32).astype(bf16)
    else:
        out_ref[...] = total


def finish(place, total, attended, w_out, other_weights, back, first_chunk, ordered):
    groups, rows, size = attended[0][0].shape
    split, head_shards, _, half = other_weights.shape
    chunks = len(attended)
    out_width = split * half
    depth = chunks * groups * size
    block = first_chunk // chunks
    mine = lambda i, place: (0, i)
    own = lambda i, place: (block, split * place[2] + i)
    block_a = pl.BlockSpec((groups, rows, size), lambda i, place: (0, 0, 0))
    specs, operands = [], []
    if total is not None:
        specs.append(pl.BlockSpec((rows, half), mine))
        operands.append(total)
    for mask in range(head_shards):
        specs += [block_a] * chunks
        operands += [found[mask] for found in attended]
        if mask == 0:
            specs.append(pl.BlockSpec((depth, half), own))
            operands.append(w_out)
        else:
            specs.append(
                pl.BlockSpec(
                    (1, 1, depth, half),
                    lambda i, place, mask=mask: (i, lax.bitwise_xor(place[2], mask), block, 0),
                )
            )
            operands.append(other_weights)
    last = back is not None
    if last:
        specs.append(pl.BlockSpec(back.shape, lambda i, place: (0, 0)))
        operands.append(back)
    return pl.pallas_call(
        functools.partial(
            finish_body,
            chunks=chunks,
            others=head_shards - 1,
            has_sum=total is not None,
            last=last,
            ordered=ordered,
        ),
        grid_spec=pltpu.PrefetchScalarGridSpec(
            num_scalar_prefetch=1,
            grid=(split,),
            in_specs=specs,
            out_specs=pl.BlockSpec((rows, half), mine),
            scratch_shapes=[pltpu.VMEM((rows, depth), bf16)],
        ),
        out_shape=jax.ShapeDtypeStruct((rows, out_width), bf16 if last else f32),
        compiler_params=pltpu.CompilerParams(vmem_limit_bytes=40 * mib),
        cost_estimate=cost(
            2 * rows * depth * head_shards * out_width,
            2 * depth * head_shards * out_width + 8 * rows * out_width,
        ),
        name="finish",
    )(place, *operands)


def splits(out_width, head_shards):
    return head_shards == 2 and out_width % 256 == 0


def fetch_weights(w_out, me, side, head_shards, arrived):
    depth, width = w_out.shape
    out_width = width // head_shards
    if not splits(out_width, head_shards):
        blocks = jnp.transpose(w_out.reshape(depth, head_shards, out_width), (1, 0, 2))
        return lax.all_to_all(blocks, "head", split_axis=0, concat_axis=0, tiled=True)
    half = out_width // 2
    nothing = jnp.minimum(jnp.abs(arrived[0, 0, 0]).astype(jnp.int32), 0)
    column = (1 - side) * out_width + (me % 2) * half + nothing
    return lax.all_gather(lax.dynamic_slice(w_out, (0, column), (depth, half)), "head")


def share_weights(found, out_width, head_shards):
    if not splits(out_width, head_shards):
        return found[None]
    pairs = [[i, i + 1] for i in range(0, lax.axis_size("seq"), 2)]
    return lax.all_gather(found, "seq", axis_index_groups=pairs)


def per_device(tokens, survive, norm_gain, w_qkv, qk_gain, w_out):
    heads, size = qk_gain.shape[1:]
    shards, head_shards = lax.axis_size("seq"), lax.axis_size("head")
    groups = math.gcd(heads & -heads, shards & -shards)
    ring = shards // groups
    chunks = heads // groups
    me, side = lax.axis_index("seq"), lax.axis_index("head")
    place = jnp.stack([me // ring, me % ring, side]).astype(jnp.int32)
    planes = [[i + ring * g for g in range(groups)] for i in range(ring)]

    def swap(blocks):
        return [blocks[0]] + [flip(blocks[k], "seq", k * ring) for k in range(1, groups)]

    def stack(blocks):
        return jnp.concatenate([block[:, :, : 2 * size] for block in blocks])

    def everywhere(stacked, gate):
        found = {0: stacked}
        mask = ring // 2
        while mask:
            for known in list(found):
                source = found[known]
                if gate is not None and mask < ring // 2:
                    source = chain(source, gate)
                found[known | mask] = flip(source, "seq", mask)
            mask //= 2
        return [found[mask] for mask in range(ring)]

    def send_back(blocks):
        if groups == 1:
            return blocks
        return lax.all_to_all(
            blocks, "seq", split_axis=0, concat_axis=0, axis_index_groups=planes, tiled=True
        )

    def across(blocks):
        return [blocks] + [flip(blocks, "head", mask) for mask in range(1, head_shards)]

    weights = jnp.transpose(w_qkv, (1, 0, 2))
    gains = jnp.transpose(qk_gain, (1, 0, 2))

    def later(values, *earlier):
        return jnp.maximum(chain(values, *earlier), 0)

    def first(blocks):
        return blocks[min(1, groups - 1)]

    def send(blocks, *earlier):
        return swap(list(chain(tuple(blocks), *earlier)) if earlier else blocks)

    operands = (survive, tokens, norm_gain)
    sets = [((1, 2, 0), (0,))]
    (blocks,), rest = project(place, None, weights, gains, sets, groups, operands)
    normed, chosen, back, count = rest
    arrived = [swap(blocks)]
    fetched = fetch_weights(w_out, me, side, head_shards, first(arrived[0]))

    rest, asked, hops = range(1, chunks), None, []
    if chunks > 1:
        prepared = (count, chain(normed, first(arrived[0])), chosen)
        sets = [((1, 2), (chunk,)) for chunk in rest]
        made, _ = project(place, prepared, weights, gains, sets, groups)
        stacks = [stack(list(chain(tuple(arrived[0]), made[0][0])))]
        arrived.append(send(made[0]))
        for blocks in made[1:]:
            arrived.append(send(blocks, first(arrived[-1])))
        hop = flip(stacks[0], "seq", ring // 2) if ring > 1 else stacks[0]
        stacks.append(stack(arrived[1]))
        ready = later(count, hop, stacks[1])
        sets = [((0,), tuple(rest))]
        (made,), _ = project(place, (ready, normed, chosen), weights, gains, sets, groups)
        gate = made[0]
        stacks += [stack(blocks) for blocks in arrived[2:]]
        asked = send(made, stacks[-1])
        hops = [flip(stacks[-1], "seq", ring // 2)] if ring > 1 else []
    else:
        gate, stacks = None, [stack(arrived[0])]

    attended, returned = [], []
    query, low_lane = arrived[0], 2 * size
    for chunk in range(chunks):
        final = chunk == chunks - 1
        keyvals = everywhere(stacks[chunk], gate)
        before = [stacks[-1]] + attended[-1:] + (hops if chunk else []) + (returned[:1] if final else [])
        ready = later(place, *query[1:], *before)
        row = max(chunk - 1, 0)
        found = attend(ready, query, row, low_lane, keyvals, shards, not final)
        attended.append(found[0])
        returned.append(jnp.concatenate(swap(found)) if final else send_back(found[0]))
        if not final:
            query, low_lane = asked, 0
            gate = tuple(asked)
    out_width = w_out.shape[1] // head_shards
    if chunks > 1:
        fetched = chain(fetched, first(asked))
    other_weights = share_weights(fetched, out_width, head_shards)
    total = None
    if chunks > 1:
        sooner = [across(found) for found in returned[:-1]]
        total = finish(place, None, sooner, w_out, other_weights, None, 0, True)
    last = across(returned[-1])
    return finish(place, total, [last], w_out, other_weights, back, chunks - 1, False)


def solution(mesh):
    placed = (
        P("seq", None),
        P("seq"),
        P(),
        P(None, None, "head"),
        P(None, "head", None),
        P("head", None),
    )
    return jax.shard_map(
        per_device, mesh=mesh, in_specs=placed, out_specs=P("seq", "head"), check_vma=False
    )
```

```python
import functools
import math

import jax
import jax.numpy as jnp
from jax import lax
from jax.experimental import pallas as pl
from jax.experimental.pallas import tpu as pltpu
from jax.sharding import PartitionSpec as P

epsilon = 1e-06
dead_mark = 1e30
dead_limit = 1e15
mib = 1 << 20
f32 = jnp.float32
bf16 = jnp.bfloat16
params = pltpu.CompilerParams(vmem_limit_bytes=60 * mib)


def cost(flops, bytes_accessed, exps=0):
    return pl.CostEstimate(
        flops=int(flops), bytes_accessed=int(bytes_accessed), transcendentals=int(exps)
    )


def flip(values, axis, mask):
    size = lax.axis_size(axis)
    return lax.ppermute(values, axis, [(i, i ^ mask) for i in range(size)])


def chain(values, *earlier):
    return lax.optimization_barrier((values, earlier))[0]


def layer_norm(values, gain):
    center = values - jnp.mean(values, axis=-1, keepdims=True)
    spread = jnp.mean(center * center, axis=-1, keepdims=True)
    return center * lax.rsqrt(spread + epsilon) * gain


def prepare(survive_ref, tokens_ref, gain_ref, normed_ref, chosen_ref, back_ref, count_ref):
    positions = tokens_ref.shape[0]
    first = lax.broadcasted_iota(jnp.int32, (positions, positions), 0)
    second = lax.broadcasted_iota(jnp.int32, (positions, positions), 1)
    live = jnp.broadcast_to(survive_ref[...].reshape(1, positions), (8, positions)).astype(f32)
    upper = (first <= second).astype(f32).astype(bf16)
    rank = jnp.dot(live.astype(bf16), upper, preferred_element_type=f32)
    target = jnp.where(live > 0.5, rank - 1.0, -1.0)
    chosen_ref[...] = (first == target[:1].astype(jnp.int32)).astype(f32).astype(bf16)
    home = jnp.transpose(target)[:, :1].astype(jnp.int32)
    back_ref[...] = (second == home).astype(f32).astype(bf16)
    count_ref[0, 0] = jnp.max(rank).astype(jnp.int32)
    gain = gain_ref[...].reshape(1, gain_ref.shape[0])
    rows = 128 if positions % 128 == 0 else positions
    for low in range(0, positions, rows):
        part = tokens_ref[low : low + rows, :].astype(f32)
        normed_ref[low : low + rows, :] = layer_norm(part, gain).astype(bf16)


def project_body(place_ref, *refs, steps, groups, first):
    refs = list(refs)
    result_ref = refs.pop()
    weight_ref, gain_ref = refs[:2]
    if first:
        survive_ref, tokens_ref, norm_gain_ref = refs[2:5]
        outs, (normed_ref, chosen_ref, back_ref, count_ref) = refs[5:-4], refs[-4:]

        @pl.when(pl.program_id(0) == 0)
        def _():
            prepare(
                survive_ref, tokens_ref, norm_gain_ref, normed_ref, chosen_ref, back_ref, count_ref
            )

    else:
        (count_ref, normed_ref, chosen_ref), outs = refs[2:5], refs[5:]
    rows = normed_ref.shape[0]
    size = gain_ref.shape[2]
    plane = place_ref[0]
    for step, (kind, chunk, target, row, low) in enumerate(steps):

        @pl.when(pl.program_id(0) == step)
        def _():
            result = jnp.dot(normed_ref[...], weight_ref[0], preferred_element_type=f32)
            for g in range(groups):
                part = result[:, g * size : (g + 1) * size]
                if kind != 2:
                    gain = gain_ref[chunk * groups + g, kind : kind + 1, :]
                    if kind == 0:
                        gain = gain * (1.0 / math.sqrt(size))
                    part = layer_norm(part, gain)
                result_ref[:, g * size : (g + 1) * size] = part.astype(bf16)
            packed = jnp.dot(chosen_ref[...], result_ref[...], preferred_element_type=f32)
            if kind == 1:
                line = lax.broadcasted_iota(jnp.int32, (rows, groups * size), 0)
                packed = jnp.where(line < count_ref[0, 0], packed, dead_mark)
            result_ref[...] = packed.astype(bf16)
            for k in range(groups):
                start = pl.multiple_of(lax.bitwise_xor(plane, k) * size, size)
                found = result_ref[:, pl.ds(start, size)]
                outs[target * groups + k][row, :, low : low + size] = found


def project(place, prepared, weights, gains, sets, groups, first=None):
    size = gains.shape[2]
    width = weights.shape[1]
    columns = groups * size
    fixed = lambda t, place: (0, 0)
    line = lambda t, place: (0,)
    smem = pl.BlockSpec(memory_space=pltpu.SMEM)
    rows = (first or prepared)[1].shape[0]
    square = pl.BlockSpec((rows, rows), fixed)
    whole = pl.BlockSpec((rows, width), fixed)
    steps = [
        (kind, chunk, target, row, i * size)
        for target, (kinds, which) in enumerate(sets)
        for row, chunk in enumerate(which)
        for i, kind in enumerate(kinds)
    ]

    def weight_index(t, place):
        kind, chunk = steps[0][:2]
        for step, found in enumerate(steps):
            kind = jnp.where(t == step, found[0], kind)
            chunk = jnp.where(t == step, found[1], chunk)
        return (kind, 0, chunk)

    shapes = [
        (len(which), rows, len(kinds) * size) for kinds, which in sets for _ in range(groups)
    ]
    out_specs = [pl.BlockSpec(shape, lambda t, place: (0, 0, 0)) for shape in shapes]
    out_shape = [jax.ShapeDtypeStruct(shape, bf16) for shape in shapes]
    if first:
        in_specs = [pl.BlockSpec((rows,), line), whole, pl.BlockSpec((width,), line)]
        out_specs += [whole, square, square, smem]
        out_shape += [
            jax.ShapeDtypeStruct((rows, width), bf16),
            jax.ShapeDtypeStruct((rows, rows), bf16),
            jax.ShapeDtypeStruct((rows, rows), bf16),
            jax.ShapeDtypeStruct((1, 1), jnp.int32),
        ]
    else:
        in_specs = [smem, whole, square]
    found = pl.pallas_call(
        functools.partial(project_body, steps=steps, groups=groups, first=first is not None),
        grid_spec=pltpu.PrefetchScalarGridSpec(
            num_scalar_prefetch=1,
            grid=(len(steps),),
            in_specs=[
                pl.BlockSpec((1, width, columns), weight_index),
                pl.BlockSpec(gains.shape, lambda t, place: (0, 0, 0)),
            ]
            + in_specs,
            out_specs=out_specs,
            scratch_shapes=[pltpu.VMEM((rows, columns), bf16)],
        ),
        out_shape=out_shape,
        compiler_params=params,
        cost_estimate=cost(
            2 * rows * width * len(steps) * columns,
            2 * width * len(steps) * columns + 2 * rows * width,
        ),
        name="project",
    )(place, weights, gains, *(first or prepared))
    blocks = [found[i * groups : (i + 1) * groups] for i in range(len(sets))]
    return blocks, found[len(sets) * groups :]


def attend_body(place_ref, *refs, groups, ordered, low_lane, key_room, query_rows, key_cols):
    outs = 1 if ordered else groups
    query_refs, sources, out_refs = refs[:groups], refs[groups : -4 - outs], refs[-4 - outs : -4]
    keys, values, queries, results = refs[-4:]
    rows, size = out_refs[0].shape[1:]
    plane = place_ref[0]
    blocks = [(source, k) for source in sources for k in range(groups)]
    piece = 128 if rows % 128 == 0 else rows
    align = lambda count: pl.multiple_of((count + 15) // 16 * 16, 16)
    line = lax.broadcasted_iota(jnp.int32, (piece, size), 0)

    found = []
    for source, block in blocks:
        live = (source[block, :, :size].astype(f32) < dead_limit).astype(f32)
        found.append(jnp.max(jnp.sum(live, axis=0, keepdims=True)).astype(jnp.int32))

    offset = jnp.int32(0)
    for (source, block), count in zip(blocks, found):
        for part in range(rows // piece):

            @pl.when(part * piece < count)
            def _():
                here = pl.ds(pl.multiple_of(offset + part * piece, 16), piece)
                there = pl.ds(part * piece, piece)
                live = line + part * piece < count
                key = jnp.where(live, source[block, there, :size].astype(f32), 0.0)
                keys[here, :] = key.astype(bf16)
                values[here, :size] = source[block, there, size:]
                values[here, size:] = live.astype(f32).astype(bf16)

        offset = pl.multiple_of(offset + align(count), 16)

    def clear(step, carry):
        here = pl.ds(pl.multiple_of(offset + step * 16, 16), 16)
        keys[here, :] = jnp.zeros((16, size), bf16)
        values[here, :] = jnp.zeros((16, 2 * size), bf16)
        return carry

    lax.fori_loop(0, (key_room - offset) // 16, clear, 0)

    mine = found[:groups]
    starts = []
    start = jnp.int32(0)
    for k in range(groups):
        starts.append(start)
        for part in range(rows // piece):

            @pl.when(part * piece < mine[k])
            def _():
                here = pl.ds(pl.multiple_of(start + part * piece, 16), piece)
                there = pl.ds(part * piece, piece)
                queries[here, :] = query_refs[k][0, there, low_lane : low_lane + size]

        start = pl.multiple_of(start + align(mine[k]), 16)

    def one_tile(tile, carry):
        here = pl.ds(pl.multiple_of(tile * query_rows, query_rows), query_rows)
        query = queries[here, :]
        total = jnp.zeros((query_rows, 2 * size), f32)
        for low in range(0, key_room, key_cols):
            high = min(low + key_cols, key_room)
            scores = lax.dot_general(
                query, keys[low:high, :], (((1,), (1,)), ((), ())), preferred_element_type=f32
            )
            weights = jnp.exp(scores).astype(bf16)
            total += jnp.dot(weights, values[low:high, :], preferred_element_type=f32)
        results[here, :] = (total[:, :size] / total[:, size:]).astype(bf16)
        return carry

    lax.fori_loop(0, (start + query_rows - 1) // query_rows, one_tile, 0)

    for k in range(groups):
        for part in range(rows // piece):
            here = pl.ds(pl.multiple_of(starts[k] + part * piece, 16), piece)
            live = line + part * piece < mine[k]
            kept = jnp.where(live, results[here, :].astype(f32), 0.0).astype(bf16)
            block = lax.bitwise_xor(plane, k) if ordered else 0
            out_refs[0 if ordered else k][block, part * piece : (part + 1) * piece, :] = kept


def attend(place, queries, which, low_lane, keyvals, shards, ordered):
    groups = len(queries)
    rows = keyvals[0].shape[1]
    size = keyvals[0].shape[2] // 2
    running = shards * rows // 2
    key_room = -(-(running + 16 * shards) // 256) * 256
    query_rows = 256
    query_room = -(-groups * rows // query_rows) * query_rows + rows
    query_block = (1,) + queries[0].shape[1:]
    outs, wide = (1, groups) if ordered else (groups, 1)
    return pl.pallas_call(
        functools.partial(
            attend_body,
            groups=groups,
            ordered=ordered,
            low_lane=low_lane,
            key_room=key_room,
            query_rows=query_rows,
            key_cols=256,
        ),
        grid_spec=pltpu.PrefetchScalarGridSpec(
            num_scalar_prefetch=1,
            grid=(1,),
            in_specs=[pl.BlockSpec(query_block, lambda i, place: (which, 0, 0))] * groups
            + [pl.BlockSpec(keyvals[0].shape, lambda i, place: (0, 0, 0))] * len(keyvals),
            out_specs=[pl.BlockSpec((wide, rows, size), lambda i, place: (0, 0, 0))] * outs,
            scratch_shapes=[
                pltpu.VMEM((key_room + rows, size), bf16),
                pltpu.VMEM((key_room + rows, 2 * size), bf16),
                pltpu.VMEM((query_room, size), bf16),
                pltpu.VMEM((query_room, size), bf16),
            ],
        ),
        out_shape=[jax.ShapeDtypeStruct((wide, rows, size), bf16)] * outs,
        compiler_params=params,
        cost_estimate=cost(
            8 * groups * rows // 2 * running * size,
            4 * shards * rows * size,
            groups * rows // 2 * running,
        ),
        name="attend",
    )(place, *queries, *keyvals)


def finish_body(place_ref, *refs, chunks, others, has_sum, last, ordered):
    refs = list(refs)
    wide_ref = refs.pop()
    out_ref = refs.pop()
    total = refs.pop(0)[...] if has_sum else None
    for m in range(1 + others):
        attended_refs, weight_ref = refs[:chunks], refs[chunks]
        refs = refs[chunks + 1 :]
        for i, ref in enumerate(attended_refs):
            groups, _, size = ref.shape
            for g in range(groups):
                head = i * groups + (g if ordered else lax.bitwise_xor(place_ref[0], g))
                start = head * size if ordered else pl.multiple_of(head * size, size)
                wide_ref[:, pl.ds(start, size)] = ref[g]
        wide = wide_ref[...]
        weight = weight_ref[0, 0] if m else weight_ref[...]
        term = jnp.dot(wide, weight, preferred_element_type=f32)
        total = term if total is None else total + term
    if last:
        rounded = total.astype(bf16)
        out_ref[...] = jnp.dot(refs[0][...], rounded, preferred_element_type=f32).astype(bf16)
    else:
        out_ref[...] = total


def finish(place, total, attended, w_out, other_weights, back, first_chunk, ordered):
    groups, rows, size = attended[0][0].shape
    split, head_shards, _, half = other_weights.shape
    chunks = len(attended)
    out_width = split * half
    depth = chunks * groups * size
    block = first_chunk // chunks
    mine = lambda i, place: (0, i)
    own = lambda i, place: (block, split * place[2] + i)
    block_a = pl.BlockSpec((groups, rows, size), lambda i, place: (0, 0, 0))
    specs, operands = [], []
    if total is not None:
        specs.append(pl.BlockSpec((rows, half), mine))
        operands.append(total)
    for mask in range(head_shards):
        specs += [block_a] * chunks
        operands += [found[mask] for found in attended]
        if mask == 0:
            specs.append(pl.BlockSpec((depth, half), own))
            operands.append(w_out)
        else:
            specs.append(
                pl.BlockSpec(
                    (1, 1, depth, half),
                    lambda i, place, mask=mask: (i, lax.bitwise_xor(place[2], mask), block, 0),
                )
            )
            operands.append(other_weights)
    last = back is not None
    if last:
        specs.append(pl.BlockSpec(back.shape, lambda i, place: (0, 0)))
        operands.append(back)
    return pl.pallas_call(
        functools.partial(
            finish_body,
            chunks=chunks,
            others=head_shards - 1,
            has_sum=total is not None,
            last=last,
            ordered=ordered,
        ),
        grid_spec=pltpu.PrefetchScalarGridSpec(
            num_scalar_prefetch=1,
            grid=(split,),
            in_specs=specs,
            out_specs=pl.BlockSpec((rows, half), mine),
            scratch_shapes=[pltpu.VMEM((rows, depth), bf16)],
        ),
        out_shape=jax.ShapeDtypeStruct((rows, out_width), bf16 if last else f32),
        compiler_params=pltpu.CompilerParams(vmem_limit_bytes=40 * mib),
        cost_estimate=cost(
            2 * rows * depth * head_shards * out_width,
            2 * depth * head_shards * out_width + 8 * rows * out_width,
        ),
        name="finish",
    )(place, *operands)


def splits(out_width, head_shards):
    return head_shards == 2 and out_width % 256 == 0


def fetch_weights(w_out, me, side, head_shards):
    depth, width = w_out.shape
    out_width = width // head_shards
    if not splits(out_width, head_shards):
        blocks = jnp.transpose(w_out.reshape(depth, head_shards, out_width), (1, 0, 2))
        return lax.all_to_all(blocks, "head", split_axis=0, concat_axis=0, tiled=True)
    half = out_width // 2
    column = (1 - side) * out_width + (me % 2) * half
    return lax.all_gather(lax.dynamic_slice(w_out, (0, column), (depth, half)), "head")


def share_weights(found, out_width, head_shards):
    if not splits(out_width, head_shards):
        return found[None]
    pairs = [[i, i + 1] for i in range(0, lax.axis_size("seq"), 2)]
    return lax.all_gather(found, "seq", axis_index_groups=pairs)


def per_device(tokens, survive, norm_gain, w_qkv, qk_gain, w_out):
    heads, size = qk_gain.shape[1:]
    shards, head_shards = lax.axis_size("seq"), lax.axis_size("head")
    groups = math.gcd(heads & -heads, shards & -shards)
    ring = shards // groups
    chunks = heads // groups
    me, side = lax.axis_index("seq"), lax.axis_index("head")
    place = jnp.stack([me // ring, me % ring, side]).astype(jnp.int32)
    planes = [[i + ring * g for g in range(groups)] for i in range(ring)]

    def swap(blocks):
        return [blocks[0]] + [flip(blocks[k], "seq", k * ring) for k in range(1, groups)]

    def stack(blocks):
        return jnp.concatenate([block[:, :, : 2 * size] for block in blocks])

    def everywhere(stacked, gate):
        found = {0: stacked}
        mask = ring // 2
        while mask:
            for known in list(found):
                source = found[known]
                if gate is not None and mask < ring // 2:
                    source = chain(source, gate)
                found[known | mask] = flip(source, "seq", mask)
            mask //= 2
        return [found[mask] for mask in range(ring)]

    def send_back(blocks):
        if groups == 1:
            return blocks
        return lax.all_to_all(
            blocks, "seq", split_axis=0, concat_axis=0, axis_index_groups=planes, tiled=True
        )

    def across(blocks):
        return [blocks] + [flip(blocks, "head", mask) for mask in range(1, head_shards)]

    weights = jnp.transpose(w_qkv, (1, 0, 2))
    gains = jnp.transpose(qk_gain, (1, 0, 2))

    def later(values, *earlier):
        return jnp.maximum(chain(values, *earlier), 0)

    def first(blocks):
        return blocks[min(1, groups - 1)]

    def send(blocks, *earlier):
        return swap(list(chain(tuple(blocks), *earlier)) if earlier else blocks)

    operands = (survive, tokens, norm_gain)
    sets = [((1, 2, 0), (0,))]
    (blocks,), rest = project(place, None, weights, gains, sets, groups, operands)
    normed, chosen, back, count = rest
    arrived = [swap(blocks)]
    fetched = fetch_weights(w_out, me, side, head_shards)

    rest, asked, hops = range(1, chunks), None, []
    gate, stacks = None, []
    for chunk in rest:
        source = chain(normed, first(arrived[-1]), *stacks[-1:])
        sets = [((1, 2), (chunk,))]
        if chunk == chunks - 1:
            sets.append(((0,), tuple(rest)))
        made, _ = project(place, (count, source, chosen), weights, gains, sets, groups)
        gate = made[0][0]
        stacks.append(stack(list(chain(tuple(arrived[-1]), gate))))
        arrived.append(swap(made[0]))
        if chunk == chunks - 1:
            asked = send(made[1], first(arrived[-1]))
    stacks.append(stack(arrived[-1]))
    if chunks > 1 and ring > 1:
        hops = [flip(stacks[-1], "seq", ring // 2)]
    out_width = w_out.shape[1] // head_shards
    other_weights = share_weights(chain(fetched, gate), out_width, head_shards)

    attended, returned = [], []
    query, low_lane = arrived[0], 2 * size
    for chunk in range(chunks):
        final = chunk == chunks - 1
        keyvals = everywhere(stacks[chunk], gate)
        before = [stacks[-1]] + attended[-1:] + (hops if chunk else []) + (returned[:1] if final else [])
        ready = later(place, *query[1:], *before)
        row = max(chunk - 1, 0)
        found = attend(ready, query, row, low_lane, keyvals, shards, not final)
        attended.append(found[0])
        returned.append(jnp.concatenate(swap(found)) if final else send_back(found[0]))
        if not final:
            query, low_lane = asked, 0
            gate = tuple(asked)
    total = None
    if chunks > 1:
        sooner = [across(found) for found in returned[:-1]]
        total = finish(place, None, sooner, w_out, other_weights, None, 0, True)
    last = across(returned[-1])
    return finish(place, total, [last], w_out, other_weights, back, chunks - 1, False)


def solution(mesh):
    placed = (
        P("seq", None),
        P("seq"),
        P(),
        P(None, None, "head"),
        P(None, "head", None),
        P("head", None),
    )
    return jax.shard_map(
        per_device, mesh=mesh, in_specs=placed, out_specs=P("seq", "head"), check_vma=False
    )
```

```python
import functools
import math

import jax
import jax.numpy as jnp
from jax import lax
from jax.experimental import pallas as pl
from jax.experimental.pallas import tpu as pltpu
from jax.sharding import PartitionSpec as P

epsilon = 1e-06
dead_mark = 1e30
dead_limit = 1e15
mib = 1 << 20
f32 = jnp.float32
bf16 = jnp.bfloat16
params = pltpu.CompilerParams(vmem_limit_bytes=60 * mib)


def cost(flops, bytes_accessed, exps=0):
    return pl.CostEstimate(
        flops=int(flops), bytes_accessed=int(bytes_accessed), transcendentals=int(exps)
    )


def flip(values, axis, mask):
    size = lax.axis_size(axis)
    return lax.ppermute(values, axis, [(i, i ^ mask) for i in range(size)])


def chain(values, *earlier):
    return lax.optimization_barrier((values, earlier))[0]


def layer_norm(values, gain):
    center = values - jnp.mean(values, axis=-1, keepdims=True)
    spread = jnp.mean(center * center, axis=-1, keepdims=True)
    return center * lax.rsqrt(spread + epsilon) * gain


def prepare(survive_ref, tokens_ref, gain_ref, normed_ref, chosen_ref, back_ref, count_ref):
    positions = tokens_ref.shape[0]
    first = lax.broadcasted_iota(jnp.int32, (positions, positions), 0)
    second = lax.broadcasted_iota(jnp.int32, (positions, positions), 1)
    live = jnp.broadcast_to(survive_ref[...].reshape(1, positions), (8, positions)).astype(f32)
    upper = (first <= second).astype(f32).astype(bf16)
    rank = jnp.dot(live.astype(bf16), upper, preferred_element_type=f32)
    target = jnp.where(live > 0.5, rank - 1.0, -1.0)
    chosen_ref[...] = (first == target[:1].astype(jnp.int32)).astype(f32).astype(bf16)
    home = jnp.transpose(target)[:, :1].astype(jnp.int32)
    back_ref[...] = (second == home).astype(f32).astype(bf16)
    count_ref[0, 0] = jnp.max(rank).astype(jnp.int32)
    gain = gain_ref[...].reshape(1, gain_ref.shape[0])
    rows = 128 if positions % 128 == 0 else positions
    for low in range(0, positions, rows):
        part = tokens_ref[low : low + rows, :].astype(f32)
        normed_ref[low : low + rows, :] = layer_norm(part, gain).astype(bf16)


def project_body(place_ref, *refs, steps, groups, first):
    refs = list(refs)
    result_ref = refs.pop()
    weight_ref, gain_ref = refs[:2]
    if first:
        survive_ref, tokens_ref, norm_gain_ref = refs[2:5]
        outs, (normed_ref, chosen_ref, back_ref, count_ref) = refs[5:-4], refs[-4:]

        @pl.when(pl.program_id(0) == 0)
        def _():
            prepare(
                survive_ref, tokens_ref, norm_gain_ref, normed_ref, chosen_ref, back_ref, count_ref
            )

    else:
        (count_ref, normed_ref, chosen_ref), outs = refs[2:5], refs[5:]
    rows = normed_ref.shape[0]
    size = gain_ref.shape[2]
    plane = place_ref[0]
    for step, (kind, chunk, target, row, low) in enumerate(steps):

        @pl.when(pl.program_id(0) == step)
        def _():
            result = jnp.dot(normed_ref[...], weight_ref[0], preferred_element_type=f32)
            for g in range(groups):
                part = result[:, g * size : (g + 1) * size]
                if kind != 2:
                    gain = gain_ref[chunk * groups + g, kind : kind + 1, :]
                    if kind == 0:
                        gain = gain * (1.0 / math.sqrt(size))
                    part = layer_norm(part, gain)
                result_ref[:, g * size : (g + 1) * size] = part.astype(bf16)
            packed = jnp.dot(chosen_ref[...], result_ref[...], preferred_element_type=f32)
            if kind == 1:
                line = lax.broadcasted_iota(jnp.int32, (rows, groups * size), 0)
                packed = jnp.where(line < count_ref[0, 0], packed, dead_mark)
            result_ref[...] = packed.astype(bf16)
            for k in range(groups):
                start = pl.multiple_of(lax.bitwise_xor(plane, k) * size, size)
                found = result_ref[:, pl.ds(start, size)]
                outs[target * groups + k][row, :, low : low + size] = found


def project(place, prepared, weights, gains, sets, groups, first=None):
    size = gains.shape[2]
    width = weights.shape[1]
    columns = groups * size
    fixed = lambda t, place: (0, 0)
    line = lambda t, place: (0,)
    smem = pl.BlockSpec(memory_space=pltpu.SMEM)
    rows = (first or prepared)[1].shape[0]
    square = pl.BlockSpec((rows, rows), fixed)
    whole = pl.BlockSpec((rows, width), fixed)
    steps = [
        (kind, chunk, target, row, i * size)
        for target, (kinds, which) in enumerate(sets)
        for row, chunk in enumerate(which)
        for i, kind in enumerate(kinds)
    ]

    def weight_index(t, place):
        kind, chunk = steps[0][:2]
        for step, found in enumerate(steps):
            kind = jnp.where(t == step, found[0], kind)
            chunk = jnp.where(t == step, found[1], chunk)
        return (kind, 0, chunk)

    shapes = [
        (len(which), rows, len(kinds) * size) for kinds, which in sets for _ in range(groups)
    ]
    out_specs = [pl.BlockSpec(shape, lambda t, place: (0, 0, 0)) for shape in shapes]
    out_shape = [jax.ShapeDtypeStruct(shape, bf16) for shape in shapes]
    if first:
        in_specs = [pl.BlockSpec((rows,), line), whole, pl.BlockSpec((width,), line)]
        out_specs += [whole, square, square, smem]
        out_shape += [
            jax.ShapeDtypeStruct((rows, width), bf16),
            jax.ShapeDtypeStruct((rows, rows), bf16),
            jax.ShapeDtypeStruct((rows, rows), bf16),
            jax.ShapeDtypeStruct((1, 1), jnp.int32),
        ]
    else:
        in_specs = [smem, whole, square]
    found = pl.pallas_call(
        functools.partial(project_body, steps=steps, groups=groups, first=first is not None),
        grid_spec=pltpu.PrefetchScalarGridSpec(
            num_scalar_prefetch=1,
            grid=(len(steps),),
            in_specs=[
                pl.BlockSpec((1, width, columns), weight_index),
                pl.BlockSpec(gains.shape, lambda t, place: (0, 0, 0)),
            ]
            + in_specs,
            out_specs=out_specs,
            scratch_shapes=[pltpu.VMEM((rows, columns), bf16)],
        ),
        out_shape=out_shape,
        compiler_params=params,
        cost_estimate=cost(
            2 * rows * width * len(steps) * columns,
            2 * width * len(steps) * columns + 2 * rows * width,
        ),
        name="project",
    )(place, weights, gains, *(first or prepared))
    blocks = [found[i * groups : (i + 1) * groups] for i in range(len(sets))]
    return blocks, found[len(sets) * groups :]


def attend_body(place_ref, *refs, groups, ordered, low_lane, key_room, query_rows, key_cols):
    outs = 1 if ordered else groups
    query_refs, sources, out_refs = refs[:groups], refs[groups : -4 - outs], refs[-4 - outs : -4]
    keys, values, queries, results = refs[-4:]
    rows, size = out_refs[0].shape[1:]
    plane = place_ref[0]
    blocks = [(source, k) for source in sources for k in range(groups)]
    piece = 128 if rows % 128 == 0 else rows
    align = lambda count: pl.multiple_of((count + 15) // 16 * 16, 16)
    line = lax.broadcasted_iota(jnp.int32, (piece, size), 0)

    found = []
    for source, block in blocks:
        live = (source[block, :, :size].astype(f32) < dead_limit).astype(f32)
        found.append(jnp.max(jnp.sum(live, axis=0, keepdims=True)).astype(jnp.int32))

    offset = jnp.int32(0)
    for (source, block), count in zip(blocks, found):
        for part in range(rows // piece):

            @pl.when(part * piece < count)
            def _():
                here = pl.ds(pl.multiple_of(offset + part * piece, 16), piece)
                there = pl.ds(part * piece, piece)
                live = line + part * piece < count
                key = jnp.where(live, source[block, there, :size].astype(f32), 0.0)
                keys[here, :] = key.astype(bf16)
                values[here, :size] = source[block, there, size:]
                values[here, size:] = live.astype(f32).astype(bf16)

        offset = pl.multiple_of(offset + align(count), 16)

    def clear(step, carry):
        here = pl.ds(pl.multiple_of(offset + step * 16, 16), 16)
        keys[here, :] = jnp.zeros((16, size), bf16)
        values[here, :] = jnp.zeros((16, 2 * size), bf16)
        return carry

    lax.fori_loop(0, (key_room - offset) // 16, clear, 0)

    mine = found[:groups]
    starts = []
    start = jnp.int32(0)
    for k in range(groups):
        starts.append(start)
        for part in range(rows // piece):

            @pl.when(part * piece < mine[k])
            def _():
                here = pl.ds(pl.multiple_of(start + part * piece, 16), piece)
                there = pl.ds(part * piece, piece)
                queries[here, :] = query_refs[k][0, there, low_lane : low_lane + size]

        start = pl.multiple_of(start + align(mine[k]), 16)

    def one_tile(tile, carry):
        here = pl.ds(pl.multiple_of(tile * query_rows, query_rows), query_rows)
        query = queries[here, :]
        total = jnp.zeros((query_rows, 2 * size), f32)
        for low in range(0, key_room, key_cols):
            high = min(low + key_cols, key_room)
            scores = lax.dot_general(
                query, keys[low:high, :], (((1,), (1,)), ((), ())), preferred_element_type=f32
            )
            weights = jnp.exp(scores).astype(bf16)
            total += jnp.dot(weights, values[low:high, :], preferred_element_type=f32)
        results[here, :] = (total[:, :size] / total[:, size:]).astype(bf16)
        return carry

    lax.fori_loop(0, (start + query_rows - 1) // query_rows, one_tile, 0)

    for k in range(groups):
        for part in range(rows // piece):
            here = pl.ds(pl.multiple_of(starts[k] + part * piece, 16), piece)
            live = line + part * piece < mine[k]
            kept = jnp.where(live, results[here, :].astype(f32), 0.0).astype(bf16)
            block = lax.bitwise_xor(plane, k) if ordered else 0
            out_refs[0 if ordered else k][block, part * piece : (part + 1) * piece, :] = kept


def attend(place, queries, which, low_lane, keyvals, shards, ordered):
    groups = len(queries)
    rows = keyvals[0].shape[1]
    size = keyvals[0].shape[2] // 2
    running = shards * rows // 2
    key_room = -(-(running + 16 * shards) // 256) * 256
    query_rows = 256
    query_room = -(-groups * rows // query_rows) * query_rows + rows
    query_block = (1,) + queries[0].shape[1:]
    outs, wide = (1, groups) if ordered else (groups, 1)
    return pl.pallas_call(
        functools.partial(
            attend_body,
            groups=groups,
            ordered=ordered,
            low_lane=low_lane,
            key_room=key_room,
            query_rows=query_rows,
            key_cols=256,
        ),
        grid_spec=pltpu.PrefetchScalarGridSpec(
            num_scalar_prefetch=1,
            grid=(1,),
            in_specs=[pl.BlockSpec(query_block, lambda i, place: (which, 0, 0))] * groups
            + [pl.BlockSpec(keyvals[0].shape, lambda i, place: (0, 0, 0))] * len(keyvals),
            out_specs=[pl.BlockSpec((wide, rows, size), lambda i, place: (0, 0, 0))] * outs,
            scratch_shapes=[
                pltpu.VMEM((key_room + rows, size), bf16),
                pltpu.VMEM((key_room + rows, 2 * size), bf16),
                pltpu.VMEM((query_room, size), bf16),
                pltpu.VMEM((query_room, size), bf16),
            ],
        ),
        out_shape=[jax.ShapeDtypeStruct((wide, rows, size), bf16)] * outs,
        compiler_params=params,
        cost_estimate=cost(
            8 * groups * rows // 2 * running * size,
            4 * shards * rows * size,
            groups * rows // 2 * running,
        ),
        name="attend",
    )(place, *queries, *keyvals)


def finish_body(place_ref, *refs, chunks, has_sum, ordered):
    attended_refs, weight_ref = refs[:chunks], refs[chunks]
    out_ref, wide_ref = refs[-2:]

    @pl.when(pl.program_id(0) == 0)
    def _():
        for i, ref in enumerate(attended_refs):
            groups, _, size = ref.shape
            for g in range(groups):
                head = i * groups + (g if ordered else lax.bitwise_xor(place_ref[0], g))
                start = head * size if ordered else pl.multiple_of(head * size, size)
                wide_ref[:, pl.ds(start, size)] = ref[g]

    total = jnp.dot(wide_ref[...], weight_ref[...], preferred_element_type=f32)
    if has_sum:
        total += refs[chunks + 1][...]
    out_ref[...] = total.astype(out_ref.dtype)


def finish(place, attended, w_out, first_chunk, ordered, total=None, mask=None, kind=f32):
    groups, rows, size = attended[0].shape
    head_shards = lax.axis_size("head")
    out_width = w_out.shape[1] // head_shards
    chunks = len(attended)
    depth = chunks * groups * size
    block = first_chunk // chunks
    parts = 2 if out_width % 256 == 0 else 1
    tile = out_width // parts
    count = parts * (head_shards if mask is None else 1)

    def column(i, place):
        return i if mask is None else lax.bitwise_xor(place[2], mask) * parts + i

    specs = [pl.BlockSpec((groups, rows, size), lambda i, place: (0, 0, 0))] * chunks
    specs.append(pl.BlockSpec((depth, tile), lambda i, place: (block, column(i, place))))
    operands = [*attended, w_out]
    if total is not None:
        specs.append(pl.BlockSpec((rows, tile), lambda i, place: (0, column(i, place))))
        operands.append(total)
    return pl.pallas_call(
        functools.partial(
            finish_body, chunks=chunks, has_sum=total is not None, ordered=ordered
        ),
        grid_spec=pltpu.PrefetchScalarGridSpec(
            num_scalar_prefetch=1,
            grid=(count,),
            in_specs=specs,
            out_specs=pl.BlockSpec((rows, tile), lambda i, place: (0, i)),
            scratch_shapes=[pltpu.VMEM((rows, depth), bf16)],
        ),
        out_shape=jax.ShapeDtypeStruct((rows, tile * count), kind),
        compiler_params=params,
        cost_estimate=cost(
            2 * rows * depth * tile * count, 2 * depth * tile * count + 8 * rows * tile * count
        ),
        name="finish",
    )(place, *operands)


def close_body(back_ref, mine_ref, *refs):
    out_ref = refs[-1]
    total = mine_ref[...]
    for ref in refs[:-1]:
        total += ref[...].astype(f32)
    rounded = total.astype(bf16)
    out_ref[...] = jnp.dot(back_ref[...], rounded, preferred_element_type=f32).astype(bf16)


def close(back, mine, others):
    rows, width = mine.shape
    parts = 4 if width % 512 == 0 else 1
    tile = pl.BlockSpec((rows, width // parts), lambda i: (0, i))
    return pl.pallas_call(
        close_body,
        grid=(parts,),
        in_specs=[pl.BlockSpec((rows, rows), lambda i: (0, 0))] + [tile] * (1 + len(others)),
        out_specs=tile,
        out_shape=jax.ShapeDtypeStruct((rows, width), bf16),
        compiler_params=params,
        cost_estimate=cost(2 * rows * rows * width, 10 * rows * width),
        name="close",
    )(back, mine, *others)


def per_device(tokens, survive, norm_gain, w_qkv, qk_gain, w_out):
    heads, size = qk_gain.shape[1:]
    shards, head_shards = lax.axis_size("seq"), lax.axis_size("head")
    groups = math.gcd(heads & -heads, shards & -shards)
    ring = shards // groups
    chunks = heads // groups
    me, side = lax.axis_index("seq"), lax.axis_index("head")
    place = jnp.stack([me // ring, me % ring, side]).astype(jnp.int32)
    planes = [[i + ring * g for g in range(groups)] for i in range(ring)]

    def swap(blocks):
        return [blocks[0]] + [flip(blocks[k], "seq", k * ring) for k in range(1, groups)]

    def stack(blocks):
        return jnp.concatenate([block[:, :, : 2 * size] for block in blocks])

    def everywhere(stacked, gate):
        found = {0: stacked}
        mask = ring // 2
        while mask:
            for known in list(found):
                source = found[known]
                if gate is not None and mask < ring // 2:
                    source = chain(source, gate)
                found[known | mask] = flip(source, "seq", mask)
            mask //= 2
        return [found[mask] for mask in range(ring)]

    def send_back(blocks):
        if groups == 1:
            return blocks
        return lax.all_to_all(
            blocks, "seq", split_axis=0, concat_axis=0, axis_index_groups=planes, tiled=True
        )

    weights = jnp.transpose(w_qkv, (1, 0, 2))
    gains = jnp.transpose(qk_gain, (1, 0, 2))

    def later(values, *earlier):
        return jnp.maximum(chain(values, *earlier), 0)

    def first(blocks):
        return blocks[min(1, groups - 1)]

    def send(blocks, *earlier):
        return swap(list(chain(tuple(blocks), *earlier)) if earlier else blocks)

    operands = (survive, tokens, norm_gain)
    sets = [((1, 2, 0), (0,))]
    (blocks,), rest = project(place, None, weights, gains, sets, groups, operands)
    normed, chosen, back, count = rest
    arrived = [swap(blocks)]

    rest, asked, hops = range(1, chunks), None, []
    if chunks > 1:
        prepared = (count, chain(normed, first(arrived[0])), chosen)
        sets = [((1, 2), (chunk,)) for chunk in rest]
        made, _ = project(place, prepared, weights, gains, sets, groups)
        stacks = [stack(list(chain(tuple(arrived[0]), made[0][0])))]
        arrived.append(send(made[0]))
        for blocks in made[1:]:
            arrived.append(send(blocks, first(arrived[-1])))
        hop = flip(stacks[0], "seq", ring // 2) if ring > 1 else stacks[0]
        stacks.append(stack(arrived[1]))
        ready = later(count, hop, stacks[1])
        sets = [((0,), tuple(rest))]
        (made,), _ = project(place, (ready, normed, chosen), weights, gains, sets, groups)
        gate = made[0]
        stacks += [stack(blocks) for blocks in arrived[2:]]
        asked = send(made, stacks[-1])
        hops = [flip(stacks[-1], "seq", ring // 2)] if ring > 1 else []
    else:
        gate, stacks = None, [stack(arrived[0])]

    attended, returned = [], []
    query, low_lane = arrived[0], 2 * size
    for chunk in range(chunks):
        final = chunk == chunks - 1
        keyvals = everywhere(stacks[chunk], gate)
        before = [stacks[-1]] + attended[-1:] + (hops if chunk else []) + (returned[:1] if final else [])
        ready = later(place, *query[1:], *before)
        row = max(chunk - 1, 0)
        found = attend(ready, query, row, low_lane, keyvals, shards, not final)
        attended.append(found[0])
        returned.append(jnp.concatenate(swap(found)) if final else send_back(found[0]))
        if not final:
            query, low_lane, gate = asked, 0, None
    total = finish(place, returned[:-1], w_out, 0, True) if chunks > 1 else None
    final = functools.partial(finish, place, returned[-1:], w_out, chunks - 1, False)
    sent = [final(total=total, mask=mask, kind=bf16) for mask in range(1, head_shards)]
    others = [flip(part, "head", mask) for mask, part in enumerate(sent, 1)]
    mine = final(total=chain(total, *sent) if chunks > 1 else None, mask=0)
    return close(back, mine, others)


def solution(mesh):
    placed = (
        P("seq", None),
        P("seq"),
        P(),
        P(None, None, "head"),
        P(None, "head", None),
        P("head", None),
    )
    return jax.shard_map(
        per_device, mesh=mesh, in_specs=placed, out_specs=P("seq", "head"), check_vma=False
    )
```

```python
import functools
import math

import jax
import jax.numpy as jnp
from jax import lax
from jax.experimental import pallas as pl
from jax.experimental.pallas import tpu as pltpu
from jax.sharding import PartitionSpec as P

epsilon = 1e-06
dead_mark = 1e30
dead_limit = 1e15
mib = 1 << 20
f32 = jnp.float32
bf16 = jnp.bfloat16
params = pltpu.CompilerParams(vmem_limit_bytes=60 * mib)


def cost(flops, bytes_accessed, exps=0):
    return pl.CostEstimate(
        flops=int(flops), bytes_accessed=int(bytes_accessed), transcendentals=int(exps)
    )


def flip(values, axis, mask):
    size = lax.axis_size(axis)
    return lax.ppermute(values, axis, [(i, i ^ mask) for i in range(size)])


def chain(values, *earlier):
    return lax.optimization_barrier((values, earlier))[0]


def layer_norm(values, gain):
    center = values - jnp.mean(values, axis=-1, keepdims=True)
    spread = jnp.mean(center * center, axis=-1, keepdims=True)
    return center * lax.rsqrt(spread + epsilon) * gain


def prepare(survive_ref, tokens_ref, gain_ref, normed_ref, chosen_ref, back_ref, count_ref):
    positions = tokens_ref.shape[0]
    first = lax.broadcasted_iota(jnp.int32, (positions, positions), 0)
    second = lax.broadcasted_iota(jnp.int32, (positions, positions), 1)
    live = jnp.broadcast_to(survive_ref[...].reshape(1, positions), (8, positions)).astype(f32)
    upper = (first <= second).astype(f32).astype(bf16)
    rank = jnp.dot(live.astype(bf16), upper, preferred_element_type=f32)
    target = jnp.where(live > 0.5, rank - 1.0, -1.0)
    chosen_ref[...] = (first == target[:1].astype(jnp.int32)).astype(f32).astype(bf16)
    home = jnp.transpose(target)[:, :1].astype(jnp.int32)
    back_ref[...] = (second == home).astype(f32).astype(bf16)
    count_ref[0, 0] = jnp.max(rank).astype(jnp.int32)
    gain = gain_ref[...].reshape(1, gain_ref.shape[0])
    rows = 128 if positions % 128 == 0 else positions
    for low in range(0, positions, rows):
        part = tokens_ref[low : low + rows, :].astype(f32)
        normed_ref[low : low + rows, :] = layer_norm(part, gain).astype(bf16)


def project_body(place_ref, *refs, steps, groups, first):
    refs = list(refs)
    result_ref = refs.pop()
    weight_ref, gain_ref = refs[:2]
    if first:
        survive_ref, tokens_ref, norm_gain_ref = refs[2:5]
        outs, (normed_ref, chosen_ref, back_ref, count_ref) = refs[5:-4], refs[-4:]

        @pl.when(pl.program_id(0) == 0)
        def _():
            prepare(
                survive_ref, tokens_ref, norm_gain_ref, normed_ref, chosen_ref, back_ref, count_ref
            )

    else:
        (count_ref, normed_ref, chosen_ref), outs = refs[2:5], refs[5:]
    rows = normed_ref.shape[0]
    size = gain_ref.shape[2]
    plane = place_ref[0]
    for step, (kind, chunk, target, row, low) in enumerate(steps):

        @pl.when(pl.program_id(0) == step)
        def _():
            result = jnp.dot(normed_ref[...], weight_ref[0], preferred_element_type=f32)
            for g in range(groups):
                part = result[:, g * size : (g + 1) * size]
                if kind != 2:
                    gain = gain_ref[chunk * groups + g, kind : kind + 1, :]
                    if kind == 0:
                        gain = gain * (1.0 / math.sqrt(size))
                    part = layer_norm(part, gain)
                result_ref[:, g * size : (g + 1) * size] = part.astype(bf16)
            packed = jnp.dot(chosen_ref[...], result_ref[...], preferred_element_type=f32)
            if kind == 1:
                line = lax.broadcasted_iota(jnp.int32, (rows, groups * size), 0)
                packed = jnp.where(line < count_ref[0, 0], packed, dead_mark)
            result_ref[...] = packed.astype(bf16)
            for k in range(groups):
                start = pl.multiple_of(lax.bitwise_xor(plane, k) * size, size)
                found = result_ref[:, pl.ds(start, size)]
                outs[target * groups + k][row, :, low : low + size] = found


def project(place, prepared, weights, gains, sets, groups, first=None):
    size = gains.shape[2]
    width = weights.shape[1]
    columns = groups * size
    fixed = lambda t, place: (0, 0)
    line = lambda t, place: (0,)
    smem = pl.BlockSpec(memory_space=pltpu.SMEM)
    rows = (first or prepared)[1].shape[0]
    square = pl.BlockSpec((rows, rows), fixed)
    whole = pl.BlockSpec((rows, width), fixed)
    steps = [
        (kind, chunk, target, row, i * size)
        for target, (kinds, which) in enumerate(sets)
        for row, chunk in enumerate(which)
        for i, kind in enumerate(kinds)
    ]

    def weight_index(t, place):
        kind, chunk = steps[0][:2]
        for step, found in enumerate(steps):
            kind = jnp.where(t == step, found[0], kind)
            chunk = jnp.where(t == step, found[1], chunk)
        return (kind, 0, chunk)

    shapes = [
        (len(which), rows, len(kinds) * size) for kinds, which in sets for _ in range(groups)
    ]
    out_specs = [pl.BlockSpec(shape, lambda t, place: (0, 0, 0)) for shape in shapes]
    out_shape = [jax.ShapeDtypeStruct(shape, bf16) for shape in shapes]
    if first:
        in_specs = [pl.BlockSpec((rows,), line), whole, pl.BlockSpec((width,), line)]
        out_specs += [whole, square, square, smem]
        out_shape += [
            jax.ShapeDtypeStruct((rows, width), bf16),
            jax.ShapeDtypeStruct((rows, rows), bf16),
            jax.ShapeDtypeStruct((rows, rows), bf16),
            jax.ShapeDtypeStruct((1, 1), jnp.int32),
        ]
    else:
        in_specs = [smem, whole, square]
    found = pl.pallas_call(
        functools.partial(project_body, steps=steps, groups=groups, first=first is not None),
        grid_spec=pltpu.PrefetchScalarGridSpec(
            num_scalar_prefetch=1,
            grid=(len(steps),),
            in_specs=[
                pl.BlockSpec((1, width, columns), weight_index),
                pl.BlockSpec(gains.shape, lambda t, place: (0, 0, 0)),
            ]
            + in_specs,
            out_specs=out_specs,
            scratch_shapes=[pltpu.VMEM((rows, columns), bf16)],
        ),
        out_shape=out_shape,
        compiler_params=params,
        cost_estimate=cost(
            2 * rows * width * len(steps) * columns,
            2 * width * len(steps) * columns + 2 * rows * width,
        ),
        name="project",
    )(place, weights, gains, *(first or prepared))
    blocks = [found[i * groups : (i + 1) * groups] for i in range(len(sets))]
    return blocks, found[len(sets) * groups :]


def attend_body(place_ref, *refs, groups, ordered, low_lane, key_room, query_rows, key_cols):
    outs = 1 if ordered else groups
    query_refs, sources, out_refs = refs[:groups], refs[groups : -4 - outs], refs[-4 - outs : -4]
    keys, values, queries, results = refs[-4:]
    rows, size = out_refs[0].shape[1:]
    plane = place_ref[0]
    blocks = [(source, k) for source in sources for k in range(groups)]
    piece = 128 if rows % 128 == 0 else rows
    align = lambda count: pl.multiple_of((count + 15) // 16 * 16, 16)
    line = lax.broadcasted_iota(jnp.int32, (piece, size), 0)

    found = []
    for source, block in blocks:
        live = (source[block, :, :size].astype(f32) < dead_limit).astype(f32)
        found.append(jnp.max(jnp.sum(live, axis=0, keepdims=True)).astype(jnp.int32))

    offset = jnp.int32(0)
    for (source, block), count in zip(blocks, found):
        for part in range(rows // piece):

            @pl.when(part * piece < count)
            def _():
                here = pl.ds(pl.multiple_of(offset + part * piece, 16), piece)
                there = pl.ds(part * piece, piece)
                live = line + part * piece < count
                key = jnp.where(live, source[block, there, :size].astype(f32), 0.0)
                keys[here, :] = key.astype(bf16)
                values[here, :size] = source[block, there, size:]
                values[here, size:] = live.astype(f32).astype(bf16)

        offset = pl.multiple_of(offset + align(count), 16)

    def clear(step, carry):
        here = pl.ds(pl.multiple_of(offset + step * 16, 16), 16)
        keys[here, :] = jnp.zeros((16, size), bf16)
        values[here, :] = jnp.zeros((16, 2 * size), bf16)
        return carry

    lax.fori_loop(0, (key_room - offset) // 16, clear, 0)

    mine = found[:groups]
    starts = []
    start = jnp.int32(0)
    for k in range(groups):
        starts.append(start)
        for part in range(rows // piece):

            @pl.when(part * piece < mine[k])
            def _():
                here = pl.ds(pl.multiple_of(start + part * piece, 16), piece)
                there = pl.ds(part * piece, piece)
                queries[here, :] = query_refs[k][0, there, low_lane : low_lane + size]

        start = pl.multiple_of(start + align(mine[k]), 16)

    def one_tile(tile, carry):
        here = pl.ds(pl.multiple_of(tile * query_rows, query_rows), query_rows)
        query = queries[here, :]
        total = jnp.zeros((query_rows, 2 * size), f32)
        for low in range(0, key_room, key_cols):
            high = min(low + key_cols, key_room)
            scores = lax.dot_general(
                query, keys[low:high, :], (((1,), (1,)), ((), ())), preferred_element_type=f32
            )
            weights = jnp.exp(scores).astype(bf16)
            total += jnp.dot(weights, values[low:high, :], preferred_element_type=f32)
        results[here, :] = (total[:, :size] / total[:, size:]).astype(bf16)
        return carry

    lax.fori_loop(0, (start + query_rows - 1) // query_rows, one_tile, 0)

    for k in range(groups):
        for part in range(rows // piece):
            here = pl.ds(pl.multiple_of(starts[k] + part * piece, 16), piece)
            live = line + part * piece < mine[k]
            kept = jnp.where(live, results[here, :].astype(f32), 0.0).astype(bf16)
            block = lax.bitwise_xor(plane, k) if ordered else 0
            out_refs[0 if ordered else k][block, part * piece : (part + 1) * piece, :] = kept


def attend(place, queries, which, low_lane, keyvals, shards, ordered):
    groups = len(queries)
    rows = keyvals[0].shape[1]
    size = keyvals[0].shape[2] // 2
    running = shards * rows // 2
    key_room = -(-(running + 16 * shards) // 256) * 256
    query_rows = 256
    query_room = -(-groups * rows // query_rows) * query_rows + rows
    query_block = (1,) + queries[0].shape[1:]
    outs, wide = (1, groups) if ordered else (groups, 1)
    return pl.pallas_call(
        functools.partial(
            attend_body,
            groups=groups,
            ordered=ordered,
            low_lane=low_lane,
            key_room=key_room,
            query_rows=query_rows,
            key_cols=256,
        ),
        grid_spec=pltpu.PrefetchScalarGridSpec(
            num_scalar_prefetch=1,
            grid=(1,),
            in_specs=[pl.BlockSpec(query_block, lambda i, place: (which, 0, 0))] * groups
            + [pl.BlockSpec(keyvals[0].shape, lambda i, place: (0, 0, 0))] * len(keyvals),
            out_specs=[pl.BlockSpec((wide, rows, size), lambda i, place: (0, 0, 0))] * outs,
            scratch_shapes=[
                pltpu.VMEM((key_room + rows, size), bf16),
                pltpu.VMEM((key_room + rows, 2 * size), bf16),
                pltpu.VMEM((query_room, size), bf16),
                pltpu.VMEM((query_room, size), bf16),
            ],
        ),
        out_shape=[jax.ShapeDtypeStruct((wide, rows, size), bf16)] * outs,
        compiler_params=params,
        cost_estimate=cost(
            8 * groups * rows // 2 * running * size,
            4 * shards * rows * size,
            groups * rows // 2 * running,
        ),
        name="attend",
    )(place, *queries, *keyvals)


def pieces_of(width):
    return 2 if width % 256 == 0 else 1


def finish_body(place_ref, *refs, chunks, has_sum, ordered):
    attended_refs, weight_ref = refs[:chunks], refs[chunks]
    out_ref, wide_ref = refs[-2:]

    @pl.when(pl.program_id(0) == 0)
    def _():
        for i, ref in enumerate(attended_refs):
            groups, _, size = ref.shape
            for g in range(groups):
                head = i * groups + (g if ordered else lax.bitwise_xor(place_ref[0], g))
                start = head * size if ordered else pl.multiple_of(head * size, size)
                wide_ref[:, pl.ds(start, size)] = ref[g]

    total = jnp.dot(wide_ref[...], weight_ref[...], preferred_element_type=f32)
    if has_sum:
        total += refs[chunks + 1][...]
    out_ref[...] = total.astype(out_ref.dtype)


def finish(place, attended, w_out, first_chunk, ordered, total=None, mask=None, piece=None, kind=f32):
    groups, rows, size = attended[0].shape
    head_shards = lax.axis_size("head")
    out_width = w_out.shape[1] // head_shards
    chunks = len(attended)
    depth = chunks * groups * size
    block = first_chunk // chunks
    parts = pieces_of(out_width)
    tile = out_width // parts
    count = parts * head_shards if mask is None else parts if piece is None else 1

    def column(i, place):
        return i if mask is None else lax.bitwise_xor(place[2], mask) * parts + i + (piece or 0)

    specs = [pl.BlockSpec((groups, rows, size), lambda i, place: (0, 0, 0))] * chunks
    specs.append(pl.BlockSpec((depth, tile), lambda i, place: (block, column(i, place))))
    operands = [*attended, w_out]
    if total is not None:
        specs.append(pl.BlockSpec((rows, tile), lambda i, place: (0, column(i, place))))
        operands.append(total)
    return pl.pallas_call(
        functools.partial(
            finish_body, chunks=chunks, has_sum=total is not None, ordered=ordered
        ),
        grid_spec=pltpu.PrefetchScalarGridSpec(
            num_scalar_prefetch=1,
            grid=(count,),
            in_specs=specs,
            out_specs=pl.BlockSpec((rows, tile), lambda i, place: (0, i)),
            scratch_shapes=[pltpu.VMEM((rows, depth), bf16)],
        ),
        out_shape=jax.ShapeDtypeStruct((rows, tile * count), kind),
        compiler_params=params,
        cost_estimate=cost(
            2 * rows * depth * tile * count, 2 * depth * tile * count + 8 * rows * tile * count
        ),
        name="finish",
    )(place, *operands)


def close_body(back_ref, mine_ref, *refs, pieces, sub):
    out_ref = refs[-1]
    total = mine_ref[...]
    for low in range(0, len(refs) - 1, pieces):
        found = refs[low][...]
        for piece in range(1, pieces):
            found = jnp.where(pl.program_id(0) >= piece * sub, refs[low + piece][...], found)
        total += found.astype(f32)
    rounded = total.astype(bf16)
    out_ref[...] = jnp.dot(back_ref[...], rounded, preferred_element_type=f32).astype(bf16)


def close(back, mine, others):
    rows, width = mine.shape
    pieces = len(others[0])
    sub = pieces_of(width // pieces)
    shape = (rows, width // pieces // sub)
    tile = pl.BlockSpec(shape, lambda i: (0, i))
    came = [
        pl.BlockSpec(shape, lambda i, low=piece * sub: (0, jnp.clip(i - low, 0, sub - 1)))
        for piece in range(pieces)
    ]
    return pl.pallas_call(
        functools.partial(close_body, pieces=pieces, sub=sub),
        grid=(pieces * sub,),
        in_specs=[pl.BlockSpec((rows, rows), lambda i: (0, 0)), tile] + came * len(others),
        out_specs=tile,
        out_shape=jax.ShapeDtypeStruct((rows, width), bf16),
        compiler_params=params,
        cost_estimate=cost(2 * rows * rows * width, 10 * rows * width),
        name="close",
    )(back, mine, *[part for parts in others for part in parts])


def per_device(tokens, survive, norm_gain, w_qkv, qk_gain, w_out):
    heads, size = qk_gain.shape[1:]
    shards, head_shards = lax.axis_size("seq"), lax.axis_size("head")
    groups = math.gcd(heads & -heads, shards & -shards)
    ring = shards // groups
    chunks = heads // groups
    me, side = lax.axis_index("seq"), lax.axis_index("head")
    place = jnp.stack([me // ring, me % ring, side]).astype(jnp.int32)
    planes = [[i + ring * g for g in range(groups)] for i in range(ring)]

    def swap(blocks):
        return [blocks[0]] + [flip(blocks[k], "seq", k * ring) for k in range(1, groups)]

    def stack(blocks):
        return jnp.concatenate([block[:, :, : 2 * size] for block in blocks])

    def everywhere(stacked):
        found = {0: stacked}
        mask = ring // 2
        while mask:
            for known in list(found):
                found[known | mask] = flip(found[known], "seq", mask)
            mask //= 2
        return [found[mask] for mask in range(ring)]

    def send_back(blocks):
        if groups == 1:
            return blocks
        return lax.all_to_all(
            blocks, "seq", split_axis=0, concat_axis=0, axis_index_groups=planes, tiled=True
        )

    weights = jnp.transpose(w_qkv, (1, 0, 2))
    gains = jnp.transpose(qk_gain, (1, 0, 2))

    def later(values, *earlier):
        return jnp.maximum(chain(values, *earlier), 0)

    def first(blocks):
        return blocks[min(1, groups - 1)]

    def send(blocks, *earlier):
        return swap(list(chain(tuple(blocks), *earlier)) if earlier else blocks)

    operands = (survive, tokens, norm_gain)
    sets = [((1, 2, 0), (0,))]
    (blocks,), rest = project(place, None, weights, gains, sets, groups, operands)
    normed, chosen, back, count = rest
    arrived = [swap(blocks)]

    rest, asked, hops = range(1, chunks), None, []
    stacks = []
    for chunk in rest:
        source = chain(normed, stacks[-1] if stacks else first(arrived[0]))
        sets = [((1, 2), (chunk,))]
        (made,), _ = project(place, (count, source, chosen), weights, gains, sets, groups)
        if chunk == 1:
            stacks.append(stack(list(chain(tuple(arrived[0]), made[0]))))
            arrived.append(send(made))
        else:
            arrived.append(send(made, first(arrived[-1])))
            stacks.append(stack(arrived[chunk - 1]))
    if chunks > 1:
        hop = flip(stacks[0], "seq", ring // 2) if ring > 1 else stacks[0]
        ready = later(count, hop, stacks[-1])
        sets = [((0,), tuple(rest))]
        (made,), _ = project(place, (ready, normed, chosen), weights, gains, sets, groups)
    stacks.append(stack(arrived[-1]))
    if chunks > 1:
        asked = send(made, stacks[-1])
        hops = [flip(stacks[-1], "seq", ring // 2)] if ring > 1 else []

    attended, returned = [], []
    query, low_lane = arrived[0], 2 * size
    for chunk in range(chunks):
        final = chunk == chunks - 1
        keyvals = everywhere(stacks[chunk])
        before = [stacks[-1]] + attended[-1:] + (hops if chunk else []) + (returned[:1] if final else [])
        ready = later(place, *query[1:], *before)
        row = max(chunk - 1, 0)
        found = attend(ready, query, row, low_lane, keyvals, shards, not final)
        attended.append(found[0])
        if final:
            came = swap(found)
            returned.append(jnp.concatenate(came))
        else:
            returned.append(send_back(found[0]))
            query, low_lane = asked, 0
    total = None
    if chunks > 1:
        sooner = list(chain(tuple(returned[:-1]), first(came)))
        total = finish(place, sooner, w_out, 0, True)
    final = functools.partial(finish, place, returned[-1:], w_out, chunks - 1, False)
    pieces = range(pieces_of(w_out.shape[1] // head_shards))
    sent = [
        [final(total=total, mask=mask, piece=piece, kind=bf16) for piece in pieces]
        for mask in range(1, head_shards)
    ]
    others = [[flip(part, "head", mask) for part in parts] for mask, parts in enumerate(sent, 1)]
    last = [part for parts in sent for part in parts]
    mine = final(total=chain(total, *last) if chunks > 1 else None, mask=0)
    return close(back, mine, others)


def solution(mesh):
    placed = (
        P("seq", None),
        P("seq"),
        P(),
        P(None, None, "head"),
        P(None, "head", None),
        P("head", None),
    )
    return jax.shard_map(
        per_device, mesh=mesh, in_specs=placed, out_specs=P("seq", "head"), check_vma=False
    )
```

```python
import functools
import math

import jax
import jax.numpy as jnp
from jax import lax
from jax.experimental import pallas as pl
from jax.experimental.pallas import tpu as pltpu
from jax.sharding import PartitionSpec as P

epsilon = 1e-06
dead_mark = 1e30
dead_limit = 1e15
mib = 1 << 20
f32 = jnp.float32
bf16 = jnp.bfloat16
params = pltpu.CompilerParams(vmem_limit_bytes=60 * mib)


def cost(flops, bytes_accessed, exps=0):
    return pl.CostEstimate(
        flops=int(flops), bytes_accessed=int(bytes_accessed), transcendentals=int(exps)
    )


def flip(values, axis, mask):
    size = lax.axis_size(axis)
    return lax.ppermute(values, axis, [(i, i ^ mask) for i in range(size)])


def chain(values, *earlier):
    return lax.optimization_barrier((values, earlier))[0]


def layer_norm(values, gain):
    center = values - jnp.mean(values, axis=-1, keepdims=True)
    spread = jnp.mean(center * center, axis=-1, keepdims=True)
    return center * lax.rsqrt(spread + epsilon) * gain


def prepare(survive_ref, tokens_ref, gain_ref, normed_ref, chosen_ref, back_ref, count_ref):
    positions = tokens_ref.shape[0]
    first = lax.broadcasted_iota(jnp.int32, (positions, positions), 0)
    second = lax.broadcasted_iota(jnp.int32, (positions, positions), 1)
    live = jnp.broadcast_to(survive_ref[...].reshape(1, positions), (8, positions)).astype(f32)
    upper = (first <= second).astype(f32).astype(bf16)
    rank = jnp.dot(live.astype(bf16), upper, preferred_element_type=f32)
    target = jnp.where(live > 0.5, rank - 1.0, -1.0)
    chosen_ref[...] = (first == target[:1].astype(jnp.int32)).astype(f32).astype(bf16)
    home = jnp.transpose(target)[:, :1].astype(jnp.int32)
    back_ref[...] = (second == home).astype(f32).astype(bf16)
    count_ref[0, 0] = jnp.max(rank).astype(jnp.int32)
    gain = gain_ref[...].reshape(1, gain_ref.shape[0])
    rows = 128 if positions % 128 == 0 else positions
    for low in range(0, positions, rows):
        part = tokens_ref[low : low + rows, :].astype(f32)
        normed_ref[low : low + rows, :] = layer_norm(part, gain).astype(bf16)


def project_body(place_ref, *refs, steps, groups, first):
    refs = list(refs)
    result_ref = refs.pop()
    weight_ref, gain_ref = refs[:2]
    if first:
        survive_ref, tokens_ref, norm_gain_ref = refs[2:5]
        outs, (normed_ref, chosen_ref, back_ref, count_ref) = refs[5:-4], refs[-4:]

        @pl.when(pl.program_id(0) == 0)
        def _():
            prepare(
                survive_ref, tokens_ref, norm_gain_ref, normed_ref, chosen_ref, back_ref, count_ref
            )

    else:
        (count_ref, normed_ref, chosen_ref), outs = refs[2:5], refs[5:]
    rows = normed_ref.shape[0]
    size = gain_ref.shape[2]
    plane = place_ref[0]
    for step, (kind, chunk, target, row, low) in enumerate(steps):

        @pl.when(pl.program_id(0) == step)
        def _():
            result = jnp.dot(normed_ref[...], weight_ref[0], preferred_element_type=f32)
            for g in range(groups):
                part = result[:, g * size : (g + 1) * size]
                if kind != 2:
                    gain = gain_ref[chunk * groups + g, kind : kind + 1, :]
                    if kind == 0:
                        gain = gain * (1.0 / math.sqrt(size))
                    part = layer_norm(part, gain)
                result_ref[:, g * size : (g + 1) * size] = part.astype(bf16)
            packed = jnp.dot(chosen_ref[...], result_ref[...], preferred_element_type=f32)
            if kind == 1:
                line = lax.broadcasted_iota(jnp.int32, (rows, groups * size), 0)
                packed = jnp.where(line < count_ref[0, 0], packed, dead_mark)
            result_ref[...] = packed.astype(bf16)
            for k in range(groups):
                start = pl.multiple_of(lax.bitwise_xor(plane, k) * size, size)
                found = result_ref[:, pl.ds(start, size)]
                outs[target * groups + k][row, :, low : low + size] = found


def project(place, prepared, weights, gains, sets, groups, first=None):
    size = gains.shape[2]
    width = weights.shape[1]
    columns = groups * size
    fixed = lambda t, place: (0, 0)
    line = lambda t, place: (0,)
    smem = pl.BlockSpec(memory_space=pltpu.SMEM)
    rows = (first or prepared)[1].shape[0]
    square = pl.BlockSpec((rows, rows), fixed)
    whole = pl.BlockSpec((rows, width), fixed)
    steps = [
        (kind, chunk, target, row, i * size)
        for target, (kinds, which) in enumerate(sets)
        for row, chunk in enumerate(which)
        for i, kind in enumerate(kinds)
    ]

    def weight_index(t, place):
        kind, chunk = steps[0][:2]
        for step, found in enumerate(steps):
            kind = jnp.where(t == step, found[0], kind)
            chunk = jnp.where(t == step, found[1], chunk)
        return (kind, 0, chunk)

    shapes = [
        (len(which), rows, len(kinds) * size) for kinds, which in sets for _ in range(groups)
    ]
    out_specs = [pl.BlockSpec(shape, lambda t, place: (0, 0, 0)) for shape in shapes]
    out_shape = [jax.ShapeDtypeStruct(shape, bf16) for shape in shapes]
    if first:
        in_specs = [pl.BlockSpec((rows,), line), whole, pl.BlockSpec((width,), line)]
        out_specs += [whole, square, square, smem]
        out_shape += [
            jax.ShapeDtypeStruct((rows, width), bf16),
            jax.ShapeDtypeStruct((rows, rows), bf16),
            jax.ShapeDtypeStruct((rows, rows), bf16),
            jax.ShapeDtypeStruct((1, 1), jnp.int32),
        ]
    else:
        in_specs = [smem, whole, square]
    found = pl.pallas_call(
        functools.partial(project_body, steps=steps, groups=groups, first=first is not None),
        grid_spec=pltpu.PrefetchScalarGridSpec(
            num_scalar_prefetch=1,
            grid=(len(steps),),
            in_specs=[
                pl.BlockSpec((1, width, columns), weight_index),
                pl.BlockSpec(gains.shape, lambda t, place: (0, 0, 0)),
            ]
            + in_specs,
            out_specs=out_specs,
            scratch_shapes=[pltpu.VMEM((rows, columns), bf16)],
        ),
        out_shape=out_shape,
        compiler_params=params,
        cost_estimate=cost(
            2 * rows * width * len(steps) * columns,
            2 * width * len(steps) * columns + 2 * rows * width,
        ),
        name="project",
    )(place, weights, gains, *(first or prepared))
    blocks = [found[i * groups : (i + 1) * groups] for i in range(len(sets))]
    return blocks, found[len(sets) * groups :]


def attend_body(place_ref, *refs, groups, ordered, low_lane, key_room, query_rows, key_cols):
    outs = 1 if ordered else groups
    query_refs, sources, out_refs = refs[:groups], refs[groups : -4 - outs], refs[-4 - outs : -4]
    keys, values, queries, results = refs[-4:]
    rows, size = out_refs[0].shape[1:]
    plane = place_ref[0]
    blocks = [(source, k) for source in sources for k in range(groups)]
    piece = 128 if rows % 128 == 0 else rows
    align = lambda count: pl.multiple_of((count + 15) // 16 * 16, 16)
    line = lax.broadcasted_iota(jnp.int32, (piece, size), 0)

    found = []
    for source, block in blocks:
        live = (source[block, :, :size].astype(f32) < dead_limit).astype(f32)
        found.append(jnp.max(jnp.sum(live, axis=0, keepdims=True)).astype(jnp.int32))

    offset = jnp.int32(0)
    for (source, block), count in zip(blocks, found):
        for part in range(rows // piece):

            @pl.when(part * piece < count)
            def _():
                here = pl.ds(pl.multiple_of(offset + part * piece, 16), piece)
                there = pl.ds(part * piece, piece)
                live = line + part * piece < count
                key = jnp.where(live, source[block, there, :size].astype(f32), 0.0)
                keys[here, :] = key.astype(bf16)
                values[here, :size] = source[block, there, size:]
                values[here, size:] = live.astype(f32).astype(bf16)

        offset = pl.multiple_of(offset + align(count), 16)

    def clear(step, carry):
        here = pl.ds(pl.multiple_of(offset + step * 16, 16), 16)
        keys[here, :] = jnp.zeros((16, size), bf16)
        values[here, :] = jnp.zeros((16, 2 * size), bf16)
        return carry

    lax.fori_loop(0, (key_room - offset) // 16, clear, 0)

    mine = found[:groups]
    starts = []
    start = jnp.int32(0)
    for k in range(groups):
        starts.append(start)
        for part in range(rows // piece):

            @pl.when(part * piece < mine[k])
            def _():
                here = pl.ds(pl.multiple_of(start + part * piece, 16), piece)
                there = pl.ds(part * piece, piece)
                queries[here, :] = query_refs[k][0, there, low_lane : low_lane + size]

        start = pl.multiple_of(start + align(mine[k]), 16)

    def one_tile(tile, carry):
        here = pl.ds(pl.multiple_of(tile * query_rows, query_rows), query_rows)
        query = queries[here, :]
        total = jnp.zeros((query_rows, 2 * size), f32)
        for low in range(0, key_room, key_cols):
            high = min(low + key_cols, key_room)
            scores = lax.dot_general(
                query, keys[low:high, :], (((1,), (1,)), ((), ())), preferred_element_type=f32
            )
            weights = jnp.exp(scores).astype(bf16)
            total += jnp.dot(weights, values[low:high, :], preferred_element_type=f32)
        results[here, :] = (total[:, :size] / total[:, size:]).astype(bf16)
        return carry

    lax.fori_loop(0, (start + query_rows - 1) // query_rows, one_tile, 0)

    for k in range(groups):
        for part in range(rows // piece):
            here = pl.ds(pl.multiple_of(starts[k] + part * piece, 16), piece)
            live = line + part * piece < mine[k]
            kept = jnp.where(live, results[here, :].astype(f32), 0.0).astype(bf16)
            block = lax.bitwise_xor(plane, k) if ordered else 0
            out_refs[0 if ordered else k][block, part * piece : (part + 1) * piece, :] = kept


def attend(place, queries, which, low_lane, keyvals, shards, ordered):
    groups = len(queries)
    rows = keyvals[0].shape[1]
    size = keyvals[0].shape[2] // 2
    running = shards * rows // 2
    key_room = -(-(running + 16 * shards) // 256) * 256
    query_rows = 256
    query_room = -(-groups * rows // query_rows) * query_rows + rows
    query_block = (1,) + queries[0].shape[1:]
    outs, wide = (1, groups) if ordered else (groups, 1)
    return pl.pallas_call(
        functools.partial(
            attend_body,
            groups=groups,
            ordered=ordered,
            low_lane=low_lane,
            key_room=key_room,
            query_rows=query_rows,
            key_cols=256,
        ),
        grid_spec=pltpu.PrefetchScalarGridSpec(
            num_scalar_prefetch=1,
            grid=(1,),
            in_specs=[pl.BlockSpec(query_block, lambda i, place: (which, 0, 0))] * groups
            + [pl.BlockSpec(keyvals[0].shape, lambda i, place: (0, 0, 0))] * len(keyvals),
            out_specs=[pl.BlockSpec((wide, rows, size), lambda i, place: (0, 0, 0))] * outs,
            scratch_shapes=[
                pltpu.VMEM((key_room + rows, size), bf16),
                pltpu.VMEM((key_room + rows, 2 * size), bf16),
                pltpu.VMEM((query_room, size), bf16),
                pltpu.VMEM((query_room, size), bf16),
            ],
        ),
        out_shape=[jax.ShapeDtypeStruct((wide, rows, size), bf16)] * outs,
        compiler_params=params,
        cost_estimate=cost(
            8 * groups * rows // 2 * running * size,
            4 * shards * rows * size,
            groups * rows // 2 * running,
        ),
        name="attend",
    )(place, *queries, *keyvals)


def finish_body(place_ref, *refs, ordered):
    chunks = len(ordered)
    attended_refs, weight_ref, out_ref, wide_ref = refs[:chunks], *refs[chunks:]

    @pl.when(pl.program_id(0) == 0)
    def _():
        for i, ref in enumerate(attended_refs):
            groups, _, size = ref.shape
            for g in range(groups):
                if ordered[i]:
                    start = (i * groups + g) * size
                else:
                    head = i * groups + lax.bitwise_xor(place_ref[0], g)
                    start = pl.multiple_of(head * size, size)
                wide_ref[:, pl.ds(start, size)] = ref[g]

    total = jnp.dot(wide_ref[...], weight_ref[...], preferred_element_type=f32)
    out_ref[...] = total.astype(out_ref.dtype)


def finish(place, attended, ordered, w_out, mask, kind):
    groups, rows, size = attended[0].shape
    depth = w_out.shape[0]
    out_width = w_out.shape[1] // lax.axis_size("head")
    parts = 4 if out_width % 512 == 0 else 1
    tile = out_width // parts
    column = lambda i, place: (0, lax.bitwise_xor(place[2], mask) * parts + i)
    return pl.pallas_call(
        functools.partial(finish_body, ordered=ordered),
        grid_spec=pltpu.PrefetchScalarGridSpec(
            num_scalar_prefetch=1,
            grid=(parts,),
            in_specs=[pl.BlockSpec((groups, rows, size), lambda i, place: (0, 0, 0))] * len(attended)
            + [pl.BlockSpec((depth, tile), column)],
            out_specs=pl.BlockSpec((rows, tile), lambda i, place: (0, i)),
            scratch_shapes=[pltpu.VMEM((rows, depth), bf16)],
        ),
        out_shape=jax.ShapeDtypeStruct((rows, out_width), kind),
        compiler_params=params,
        cost_estimate=cost(2 * rows * depth * out_width, 2 * depth * out_width + 4 * rows * out_width),
        name="finish",
    )(place, *attended, w_out)


def close_body(back_ref, mine_ref, *refs):
    out_ref = refs[-1]
    total = mine_ref[...]
    for ref in refs[:-1]:
        total += ref[...].astype(f32)
    rounded = total.astype(bf16)
    out_ref[...] = jnp.dot(back_ref[...], rounded, preferred_element_type=f32).astype(bf16)


def close(back, mine, others):
    rows, width = mine.shape
    parts = 4 if width % 512 == 0 else 1
    tile = pl.BlockSpec((rows, width // parts), lambda i: (0, i))
    return pl.pallas_call(
        close_body,
        grid=(parts,),
        in_specs=[pl.BlockSpec((rows, rows), lambda i: (0, 0))] + [tile] * (1 + len(others)),
        out_specs=tile,
        out_shape=jax.ShapeDtypeStruct((rows, width), bf16),
        compiler_params=params,
        cost_estimate=cost(2 * rows * rows * width, 10 * rows * width),
        name="close",
    )(back, mine, *others)


def per_device(tokens, survive, norm_gain, w_qkv, qk_gain, w_out):
    heads, size = qk_gain.shape[1:]
    shards, head_shards = lax.axis_size("seq"), lax.axis_size("head")
    groups = math.gcd(heads & -heads, shards & -shards)
    ring = shards // groups
    chunks = heads // groups
    me, side = lax.axis_index("seq"), lax.axis_index("head")
    place = jnp.stack([me // ring, me % ring, side]).astype(jnp.int32)
    planes = [[i + ring * g for g in range(groups)] for i in range(ring)]

    def swap(blocks):
        return [blocks[0]] + [flip(blocks[k], "seq", k * ring) for k in range(1, groups)]

    def stack(blocks):
        return jnp.concatenate([block[:, :, : 2 * size] for block in blocks])

    def everywhere(stacked, gate):
        found = {0: stacked}
        mask = ring // 2
        while mask:
            for known in list(found):
                source = found[known]
                if gate is not None and mask < ring // 2:
                    source = chain(source, gate)
                found[known | mask] = flip(source, "seq", mask)
            mask //= 2
        return [found[mask] for mask in range(ring)]

    def send_back(blocks):
        if groups == 1:
            return blocks
        return lax.all_to_all(
            blocks, "seq", split_axis=0, concat_axis=0, axis_index_groups=planes, tiled=True
        )

    weights = jnp.transpose(w_qkv, (1, 0, 2))
    gains = jnp.transpose(qk_gain, (1, 0, 2))

    def later(values, *earlier):
        return jnp.maximum(chain(values, *earlier), 0)

    def first(blocks):
        return blocks[min(1, groups - 1)]

    def send(blocks, *earlier):
        return swap(list(chain(tuple(blocks), *earlier)) if earlier else blocks)

    operands = (survive, tokens, norm_gain)
    sets = [((1, 2, 0), (0,))]
    (blocks,), rest = project(place, None, weights, gains, sets, groups, operands)
    normed, chosen, back, count = rest
    arrived = [swap(blocks)]

    rest, asked, hops = range(1, chunks), None, []
    if chunks > 1:
        prepared = (count, chain(normed, first(arrived[0])), chosen)
        sets = [((1, 2), (chunk,)) for chunk in rest]
        made, _ = project(place, prepared, weights, gains, sets, groups)
        stacks = [stack(list(chain(tuple(arrived[0]), made[0][0])))]
        arrived.append(send(made[0]))
        for blocks in made[1:]:
            arrived.append(send(blocks, first(arrived[-1])))
        hop = flip(stacks[0], "seq", ring // 2) if ring > 1 else stacks[0]
        stacks.append(stack(arrived[1]))
        ready = later(count, hop, stacks[1])
        sets = [((0,), tuple(rest))]
        (made,), _ = project(place, (ready, normed, chosen), weights, gains, sets, groups)
        gate = made[0]
        stacks += [stack(blocks) for blocks in arrived[2:]]
        keyvals = everywhere(stacks[0], gate)
        asked = send(made, stacks[-1], *keyvals)
        hops = [flip(stacks[-1], "seq", ring // 2)] if ring > 1 else []
    else:
        stacks = [stack(arrived[0])]
        keyvals = everywhere(stacks[0], None)

    attended, returned = [], []
    query, low_lane = arrived[0], 2 * size
    for chunk in range(chunks):
        final = chunk == chunks - 1
        if chunk:
            keyvals = everywhere(stacks[chunk], None)
        before = [stacks[-1]] + attended[-1:] + (hops if chunk else []) + (returned[:1] if final else [])
        ready = later(place, *query[1:], *before)
        row = max(chunk - 1, 0)
        found = attend(ready, query, row, low_lane, keyvals, shards, not final)
        attended.append(found[0])
        returned.append(jnp.concatenate(swap(found)) if final else send_back(found[0]))
        if not final:
            query, low_lane = asked, 0
    ordered = (True,) * (chunks - 1) + (False,)
    final = functools.partial(finish, place, returned, ordered, w_out)
    sent = [final(mask, bf16) for mask in range(1, head_shards)]
    others = [flip(part, "head", mask) for mask, part in enumerate(sent, 1)]
    returned[0] = chain(returned[0], *sent)
    return close(back, final(0, f32), others)


def solution(mesh):
    placed = (
        P("seq", None),
        P("seq"),
        P(),
        P(None, None, "head"),
        P(None, "head", None),
        P("head", None),
    )
    return jax.shard_map(
        per_device, mesh=mesh, in_specs=placed, out_specs=P("seq", "head"), check_vma=False
    )
```

```python
import functools
import math

import jax
import jax.numpy as jnp
from jax import lax
from jax.experimental import pallas as pl
from jax.experimental.pallas import tpu as pltpu
from jax.sharding import PartitionSpec as P

epsilon = 1e-06
dead_mark = 1e30
dead_limit = 1e15
mib = 1 << 20
f32 = jnp.float32
bf16 = jnp.bfloat16
params = pltpu.CompilerParams(vmem_limit_bytes=60 * mib)


def cost(flops, bytes_accessed, exps=0):
    return pl.CostEstimate(
        flops=int(flops), bytes_accessed=int(bytes_accessed), transcendentals=int(exps)
    )


def flip(values, axis, mask):
    size = lax.axis_size(axis)
    return lax.ppermute(values, axis, [(i, i ^ mask) for i in range(size)])


def chain(values, *earlier):
    return lax.optimization_barrier((values, earlier))[0]


def layer_norm(values, gain):
    center = values - jnp.mean(values, axis=-1, keepdims=True)
    spread = jnp.mean(center * center, axis=-1, keepdims=True)
    return center * lax.rsqrt(spread + epsilon) * gain


def prepare(survive_ref, tokens_ref, gain_ref, normed_ref, chosen_ref, back_ref, count_ref):
    positions = tokens_ref.shape[0]
    first = lax.broadcasted_iota(jnp.int32, (positions, positions), 0)
    second = lax.broadcasted_iota(jnp.int32, (positions, positions), 1)
    live = jnp.broadcast_to(survive_ref[...].reshape(1, positions), (8, positions)).astype(f32)
    upper = (first <= second).astype(f32).astype(bf16)
    rank = jnp.dot(live.astype(bf16), upper, preferred_element_type=f32)
    target = jnp.where(live > 0.5, rank - 1.0, -1.0)
    chosen_ref[...] = (first == target[:1].astype(jnp.int32)).astype(f32).astype(bf16)
    home = jnp.transpose(target)[:, :1].astype(jnp.int32)
    back_ref[...] = (second == home).astype(f32).astype(bf16)
    count_ref[0, 0] = jnp.max(rank).astype(jnp.int32)
    gain = gain_ref[...].reshape(1, gain_ref.shape[0])
    rows = 128 if positions % 128 == 0 else positions
    for low in range(0, positions, rows):
        part = tokens_ref[low : low + rows, :].astype(f32)
        normed_ref[low : low + rows, :] = layer_norm(part, gain).astype(bf16)


def project_body(place_ref, *refs, steps, groups, first):
    refs = list(refs)
    result_ref = refs.pop()
    weight_ref, gain_ref = refs[:2]
    if first:
        survive_ref, tokens_ref, norm_gain_ref = refs[2:5]
        outs, (normed_ref, chosen_ref, back_ref, count_ref) = refs[5:-4], refs[-4:]

        @pl.when(pl.program_id(0) == 0)
        def _():
            prepare(
                survive_ref, tokens_ref, norm_gain_ref, normed_ref, chosen_ref, back_ref, count_ref
            )

    else:
        (count_ref, normed_ref, chosen_ref), outs = refs[2:5], refs[5:]
    rows = normed_ref.shape[0]
    size = gain_ref.shape[2]
    plane = place_ref[0]
    for step, (kind, chunk, target, row, low) in enumerate(steps):

        @pl.when(pl.program_id(0) == step)
        def _():
            result = jnp.dot(normed_ref[...], weight_ref[0], preferred_element_type=f32)
            for g in range(groups):
                part = result[:, g * size : (g + 1) * size]
                if kind != 2:
                    gain = gain_ref[chunk * groups + g, kind : kind + 1, :]
                    if kind == 0:
                        gain = gain * (1.0 / math.sqrt(size))
                    part = layer_norm(part, gain)
                result_ref[:, g * size : (g + 1) * size] = part.astype(bf16)
            packed = jnp.dot(chosen_ref[...], result_ref[...], preferred_element_type=f32)
            if kind == 1:
                line = lax.broadcasted_iota(jnp.int32, (rows, groups * size), 0)
                packed = jnp.where(line < count_ref[0, 0], packed, dead_mark)
            result_ref[...] = packed.astype(bf16)
            for k in range(groups):
                start = pl.multiple_of(lax.bitwise_xor(plane, k) * size, size)
                found = result_ref[:, pl.ds(start, size)]
                outs[target * groups + k][row, :, low : low + size] = found


def project(place, prepared, weights, gains, sets, groups, first=None):
    size = gains.shape[2]
    width = weights.shape[1]
    columns = groups * size
    fixed = lambda t, place: (0, 0)
    line = lambda t, place: (0,)
    smem = pl.BlockSpec(memory_space=pltpu.SMEM)
    rows = (first or prepared)[1].shape[0]
    square = pl.BlockSpec((rows, rows), fixed)
    whole = pl.BlockSpec((rows, width), fixed)
    steps = [
        (kind, chunk, target, row, i * size)
        for target, (kinds, which) in enumerate(sets)
        for row, chunk in enumerate(which)
        for i, kind in enumerate(kinds)
    ]

    def weight_index(t, place):
        kind, chunk = steps[0][:2]
        for step, found in enumerate(steps):
            kind = jnp.where(t == step, found[0], kind)
            chunk = jnp.where(t == step, found[1], chunk)
        return (kind, 0, chunk)

    shapes = [
        (len(which), rows, len(kinds) * size) for kinds, which in sets for _ in range(groups)
    ]
    out_specs = [pl.BlockSpec(shape, lambda t, place: (0, 0, 0)) for shape in shapes]
    out_shape = [jax.ShapeDtypeStruct(shape, bf16) for shape in shapes]
    if first:
        in_specs = [pl.BlockSpec((rows,), line), whole, pl.BlockSpec((width,), line)]
        out_specs += [whole, square, square, smem]
        out_shape += [
            jax.ShapeDtypeStruct((rows, width), bf16),
            jax.ShapeDtypeStruct((rows, rows), bf16),
            jax.ShapeDtypeStruct((rows, rows), bf16),
            jax.ShapeDtypeStruct((1, 1), jnp.int32),
        ]
    else:
        in_specs = [smem, whole, square]
    found = pl.pallas_call(
        functools.partial(project_body, steps=steps, groups=groups, first=first is not None),
        grid_spec=pltpu.PrefetchScalarGridSpec(
            num_scalar_prefetch=1,
            grid=(len(steps),),
            in_specs=[
                pl.BlockSpec((1, width, columns), weight_index),
                pl.BlockSpec(gains.shape, lambda t, place: (0, 0, 0)),
            ]
            + in_specs,
            out_specs=out_specs,
            scratch_shapes=[pltpu.VMEM((rows, columns), bf16)],
        ),
        out_shape=out_shape,
        compiler_params=params,
        cost_estimate=cost(
            2 * rows * width * len(steps) * columns,
            2 * width * len(steps) * columns + 2 * rows * width,
        ),
        name="project",
    )(place, weights, gains, *(first or prepared))
    blocks = [found[i * groups : (i + 1) * groups] for i in range(len(sets))]
    return blocks, found[len(sets) * groups :]


def attend_body(place_ref, *refs, groups, ordered, gathered, low_lane, key_room, query_rows, key_cols):
    outs = 1 if ordered else groups
    query_refs, sources, out_refs = refs[:groups], refs[groups : -5 - outs], refs[-5 - outs : -5]
    keys, values, queries, results, counts = refs[-5:]
    rows, size = out_refs[0].shape[1:]
    plane = place_ref[0]
    blocks = [(source, k) for source in sources for k in range(source.shape[0])]
    piece = 128 if rows % 128 == 0 else rows
    align = lambda count: pl.multiple_of((count + 15) // 16 * 16, 16)
    line = lax.broadcasted_iota(jnp.int32, (piece, size), 0)

    found = []
    for source, block in blocks:
        live = (source[block, :, :size].astype(f32) < dead_limit).astype(f32)
        counts[len(found)] = jnp.max(jnp.sum(live, axis=0, keepdims=True)).astype(jnp.int32)
        found.append(counts[len(found)])

    offset = jnp.int32(0)
    for (source, block), count in zip(blocks, found):
        for part in range(rows // piece):

            @pl.when(part * piece < count)
            def _():
                here = pl.ds(pl.multiple_of(offset + part * piece, 16), piece)
                there = pl.ds(part * piece, piece)
                live = line + part * piece < count
                key = jnp.where(live, source[block, there, :size].astype(f32), 0.0)
                keys[here, :] = key.astype(bf16)
                values[here, :size] = source[block, there, size:]
                values[here, size:] = live.astype(f32).astype(bf16)

        offset = pl.multiple_of(offset + align(count), 16)

    def clear(step, carry):
        here = pl.ds(pl.multiple_of(offset + step * 16, 16), 16)
        keys[here, :] = jnp.zeros((16, size), bf16)
        values[here, :] = jnp.zeros((16, 2 * size), bf16)
        return carry

    lax.fori_loop(0, (key_room - offset) // 16, clear, 0)

    own = place_ref[1] * groups if gathered else 0
    mine = [counts[own + k] for k in range(groups)]
    starts = []
    start = jnp.int32(0)
    for k in range(groups):
        starts.append(start)
        for part in range(rows // piece):

            @pl.when(part * piece < mine[k])
            def _():
                here = pl.ds(pl.multiple_of(start + part * piece, 16), piece)
                there = pl.ds(part * piece, piece)
                queries[here, :] = query_refs[k][0, there, low_lane : low_lane + size]

        start = pl.multiple_of(start + align(mine[k]), 16)

    def one_tile(tile, carry):
        here = pl.ds(pl.multiple_of(tile * query_rows, query_rows), query_rows)
        query = queries[here, :]
        total = jnp.zeros((query_rows, 2 * size), f32)
        for low in range(0, key_room, key_cols):
            high = min(low + key_cols, key_room)
            scores = lax.dot_general(
                query, keys[low:high, :], (((1,), (1,)), ((), ())), preferred_element_type=f32
            )
            weights = jnp.exp(scores).astype(bf16)
            total += jnp.dot(weights, values[low:high, :], preferred_element_type=f32)
        results[here, :] = (total[:, :size] / total[:, size:]).astype(bf16)
        return carry

    lax.fori_loop(0, (start + query_rows - 1) // query_rows, one_tile, 0)

    for k in range(groups):
        for part in range(rows // piece):
            here = pl.ds(pl.multiple_of(starts[k] + part * piece, 16), piece)
            live = line + part * piece < mine[k]
            kept = jnp.where(live, results[here, :].astype(f32), 0.0).astype(bf16)
            block = lax.bitwise_xor(plane, k) if ordered else 0
            out_refs[0 if ordered else k][block, part * piece : (part + 1) * piece, :] = kept


def attend(place, queries, which, low_lane, keyvals, shards, ordered):
    groups = len(queries)
    rows = keyvals[0].shape[1]
    size = keyvals[0].shape[2] // 2
    running = shards * rows // 2
    key_room = -(-(running + 16 * shards) // 256) * 256
    query_rows = 256
    query_room = -(-groups * rows // query_rows) * query_rows + rows
    query_block = (1,) + queries[0].shape[1:]
    outs, wide = (1, groups) if ordered else (groups, 1)
    return pl.pallas_call(
        functools.partial(
            attend_body,
            groups=groups,
            ordered=ordered,
            gathered=len(keyvals) == 1,
            low_lane=low_lane,
            key_room=key_room,
            query_rows=query_rows,
            key_cols=256,
        ),
        grid_spec=pltpu.PrefetchScalarGridSpec(
            num_scalar_prefetch=1,
            grid=(1,),
            in_specs=[pl.BlockSpec(query_block, lambda i, place: (which, 0, 0))] * groups
            + [pl.BlockSpec(keyvals[0].shape, lambda i, place: (0, 0, 0))] * len(keyvals),
            out_specs=[pl.BlockSpec((wide, rows, size), lambda i, place: (0, 0, 0))] * outs,
            scratch_shapes=[
                pltpu.VMEM((key_room + rows, size), bf16),
                pltpu.VMEM((key_room + rows, 2 * size), bf16),
                pltpu.VMEM((query_room, size), bf16),
                pltpu.VMEM((query_room, size), bf16),
                pltpu.SMEM((shards,), jnp.int32),
            ],
        ),
        out_shape=[jax.ShapeDtypeStruct((wide, rows, size), bf16)] * outs,
        compiler_params=params,
        cost_estimate=cost(
            8 * groups * rows // 2 * running * size,
            4 * shards * rows * size,
            groups * rows // 2 * running,
        ),
        name="attend",
    )(place, *queries, *keyvals)


def finish_body(place_ref, *refs, ordered):
    chunks = len(ordered)
    attended_refs, weight_ref, out_ref, wide_ref = refs[:chunks], *refs[chunks:]

    @pl.when(pl.program_id(0) == 0)
    def _():
        for i, ref in enumerate(attended_refs):
            groups, _, size = ref.shape
            for g in range(groups):
                if ordered[i]:
                    start = (i * groups + g) * size
                else:
                    head = i * groups + lax.bitwise_xor(place_ref[0], g)
                    start = pl.multiple_of(head * size, size)
                wide_ref[:, pl.ds(start, size)] = ref[g]

    total = jnp.dot(wide_ref[...], weight_ref[...], preferred_element_type=f32)
    out_ref[...] = total.astype(out_ref.dtype)


def finish(place, attended, ordered, w_out, mask, kind):
    groups, rows, size = attended[0].shape
    depth = w_out.shape[0]
    out_width = w_out.shape[1] // lax.axis_size("head")
    parts = 4 if out_width % 512 == 0 else 1
    tile = out_width // parts
    column = lambda i, place: (0, lax.bitwise_xor(place[2], mask) * parts + i)
    return pl.pallas_call(
        functools.partial(finish_body, ordered=ordered),
        grid_spec=pltpu.PrefetchScalarGridSpec(
            num_scalar_prefetch=1,
            grid=(parts,),
            in_specs=[pl.BlockSpec((groups, rows, size), lambda i, place: (0, 0, 0))] * len(attended)
            + [pl.BlockSpec((depth, tile), column)],
            out_specs=pl.BlockSpec((rows, tile), lambda i, place: (0, i)),
            scratch_shapes=[pltpu.VMEM((rows, depth), bf16)],
        ),
        out_shape=jax.ShapeDtypeStruct((rows, out_width), kind),
        compiler_params=params,
        cost_estimate=cost(2 * rows * depth * out_width, 2 * depth * out_width + 4 * rows * out_width),
        name="finish",
    )(place, *attended, w_out)


def close_body(back_ref, mine_ref, *refs):
    out_ref = refs[-1]
    total = mine_ref[...]
    for ref in refs[:-1]:
        total += ref[...].astype(f32)
    rounded = total.astype(bf16)
    out_ref[...] = jnp.dot(back_ref[...], rounded, preferred_element_type=f32).astype(bf16)


def close(back, mine, others):
    rows, width = mine.shape
    parts = 4 if width % 512 == 0 else 1
    tile = pl.BlockSpec((rows, width // parts), lambda i: (0, i))
    return pl.pallas_call(
        close_body,
        grid=(parts,),
        in_specs=[pl.BlockSpec((rows, rows), lambda i: (0, 0))] + [tile] * (1 + len(others)),
        out_specs=tile,
        out_shape=jax.ShapeDtypeStruct((rows, width), bf16),
        compiler_params=params,
        cost_estimate=cost(2 * rows * rows * width, 10 * rows * width),
        name="close",
    )(back, mine, *others)


def per_device(tokens, survive, norm_gain, w_qkv, qk_gain, w_out):
    heads, size = qk_gain.shape[1:]
    shards, head_shards = lax.axis_size("seq"), lax.axis_size("head")
    groups = math.gcd(heads & -heads, shards & -shards)
    ring = shards // groups
    chunks = heads // groups
    me, side = lax.axis_index("seq"), lax.axis_index("head")
    place = jnp.stack([me // ring, me % ring, side]).astype(jnp.int32)
    planes = [[i + ring * g for g in range(groups)] for i in range(ring)]
    rings = [[i + ring * g for i in range(ring)] for g in range(groups)]

    def swap(blocks):
        return [blocks[0]] + [flip(blocks[k], "seq", k * ring) for k in range(1, groups)]

    def stack(blocks):
        return jnp.concatenate([block[:, :, : 2 * size] for block in blocks])

    def gather(stacked):
        return [lax.all_gather(stacked, "seq", axis=0, tiled=True, axis_index_groups=rings)]

    def everywhere(stacked, hop):
        if hop is None:
            return gather(stacked)
        found, mask = {0: stacked, ring // 2: hop}, ring // 4
        while mask:
            for known in list(found):
                found[known | mask] = flip(found[known], "seq", mask)
            mask //= 2
        return [found[mask] for mask in range(ring)]

    def send_back(blocks):
        if groups == 1:
            return blocks
        return lax.all_to_all(
            blocks, "seq", split_axis=0, concat_axis=0, axis_index_groups=planes, tiled=True
        )

    weights = jnp.transpose(w_qkv, (1, 0, 2))
    gains = jnp.transpose(qk_gain, (1, 0, 2))

    def later(values, *earlier):
        return jnp.maximum(chain(values, *earlier), 0)

    def first(blocks):
        return blocks[min(1, groups - 1)]

    def send(blocks, *earlier):
        return swap(list(chain(tuple(blocks), *earlier)) if earlier else blocks)

    operands = (survive, tokens, norm_gain)
    sets = [((1, 2, 0), (0,))]
    (blocks,), rest = project(place, None, weights, gains, sets, groups, operands)
    normed, chosen, back, count = rest
    arrived = [swap(blocks)]

    rest, asked, hop = range(1, chunks), None, None
    if chunks > 1:
        prepared = (count, chain(normed, first(arrived[0])), chosen)
        sets = [((1, 2), (chunk,)) for chunk in rest]
        made, _ = project(place, prepared, weights, gains, sets, groups)
        stacks = [stack(list(chain(tuple(arrived[0]), made[0][0])))]
        arrived.append(send(made[0]))
        for blocks in made[1:]:
            arrived.append(send(blocks, first(arrived[-1])))
        stacks.append(stack(arrived[1]))
        sets = [((0,), tuple(rest))]
        ready = later(count, stacks[1])
        (made,), _ = project(place, (ready, normed, chosen), weights, gains, sets, groups)
        stacks += [stack(list(chain(tuple(blocks), made[0]))) for blocks in arrived[2:]]
        asked = send(made, stacks[-1])
        if ring > 1 and groups > 1:
            hop = flip(stacks[-1], "seq", ring // 2)
    else:
        stacks = [stack(arrived[0])]

    attended, returned = [], []
    query, low_lane = arrived[0], 2 * size
    for chunk in range(chunks):
        final = chunk == chunks - 1
        keyvals = everywhere(stacks[chunk], hop if final else None)
        before = [stacks[-1]] + attended[-1:]
        if chunk:
            before += [hop] if hop is not None else []
        elif asked is not None:
            before.append(first(asked))
        before += returned[:1] if final else []
        ready = later(place, *query[1:], *before)
        row = max(chunk - 1, 0)
        found = attend(ready, query, row, low_lane, keyvals, shards, not final)
        attended.append(found[0])
        if final:
            returned.append(jnp.concatenate(swap(found)))
        else:
            returned.append(send_back(found[0]))
            query, low_lane = asked, 0
    ordered = (True,) * (chunks - 1) + (False,)
    final = functools.partial(finish, place, returned, ordered, w_out)
    sent = [final(mask, bf16) for mask in range(1, head_shards)]
    others = [flip(part, "head", mask) for mask, part in enumerate(sent, 1)]
    returned[0] = chain(returned[0], *sent)
    return close(back, final(0, f32), others)


def solution(mesh):
    placed = (
        P("seq", None),
        P("seq"),
        P(),
        P(None, None, "head"),
        P(None, "head", None),
        P("head", None),
    )
    return jax.shard_map(
        per_device, mesh=mesh, in_specs=placed, out_specs=P("seq", "head"), check_vma=False
    )
```

```python
import functools
import math

import jax
import jax.numpy as jnp
from jax import lax
from jax.experimental import pallas as pl
from jax.experimental.pallas import tpu as pltpu
from jax.sharding import PartitionSpec as P

epsilon = 1e-06
dead_mark = 1e30
dead_limit = 1e15
mib = 1 << 20
f32 = jnp.float32
bf16 = jnp.bfloat16
params = pltpu.CompilerParams(vmem_limit_bytes=60 * mib)


def cost(flops, bytes_accessed, exps=0):
    return pl.CostEstimate(
        flops=int(flops), bytes_accessed=int(bytes_accessed), transcendentals=int(exps)
    )


def flip(values, axis, mask):
    size = lax.axis_size(axis)
    return lax.ppermute(values, axis, [(i, i ^ mask) for i in range(size)])


def chain(values, *earlier):
    return lax.optimization_barrier((values, earlier))[0]


def layer_norm(values, gain):
    center = values - jnp.mean(values, axis=-1, keepdims=True)
    spread = jnp.mean(center * center, axis=-1, keepdims=True)
    return center * lax.rsqrt(spread + epsilon) * gain


def prepare(survive_ref, tokens_ref, gain_ref, normed_ref, chosen_ref, back_ref, count_ref):
    positions = tokens_ref.shape[0]
    first = lax.broadcasted_iota(jnp.int32, (positions, positions), 0)
    second = lax.broadcasted_iota(jnp.int32, (positions, positions), 1)
    live = jnp.broadcast_to(survive_ref[...].reshape(1, positions), (8, positions)).astype(f32)
    upper = (first <= second).astype(f32).astype(bf16)
    rank = jnp.dot(live.astype(bf16), upper, preferred_element_type=f32)
    target = jnp.where(live > 0.5, rank - 1.0, -1.0)
    chosen_ref[...] = (first == target[:1].astype(jnp.int32)).astype(f32).astype(bf16)
    home = jnp.transpose(target)[:, :1].astype(jnp.int32)
    back_ref[...] = (second == home).astype(f32).astype(bf16)
    count_ref[0, 0] = jnp.max(rank).astype(jnp.int32)
    gain = gain_ref[...].reshape(1, gain_ref.shape[0])
    rows = 128 if positions % 128 == 0 else positions
    for low in range(0, positions, rows):
        part = tokens_ref[low : low + rows, :].astype(f32)
        normed_ref[low : low + rows, :] = layer_norm(part, gain).astype(bf16)


def project_body(place_ref, *refs, steps, groups, first):
    refs = list(refs)
    result_ref = refs.pop()
    weight_ref, gain_ref = refs[:2]
    if first:
        survive_ref, tokens_ref, norm_gain_ref = refs[2:5]
        outs, (normed_ref, chosen_ref, back_ref, count_ref) = refs[5:-4], refs[-4:]

        @pl.when(pl.program_id(0) == 0)
        def _():
            prepare(
                survive_ref, tokens_ref, norm_gain_ref, normed_ref, chosen_ref, back_ref, count_ref
            )

    else:
        (count_ref, normed_ref, chosen_ref), outs = refs[2:5], refs[5:]
    rows = normed_ref.shape[0]
    size = gain_ref.shape[2]
    plane = place_ref[0]
    for step, (kind, chunk, target, row, low) in enumerate(steps):

        @pl.when(pl.program_id(0) == step)
        def _():
            result = jnp.dot(normed_ref[...], weight_ref[0], preferred_element_type=f32)
            for g in range(groups):
                part = result[:, g * size : (g + 1) * size]
                if kind != 2:
                    gain = gain_ref[chunk * groups + g, kind : kind + 1, :]
                    if kind == 0:
                        gain = gain * (1.0 / math.sqrt(size))
                    part = layer_norm(part, gain)
                result_ref[:, g * size : (g + 1) * size] = part.astype(bf16)
            packed = jnp.dot(chosen_ref[...], result_ref[...], preferred_element_type=f32)
            if kind == 1:
                line = lax.broadcasted_iota(jnp.int32, (rows, groups * size), 0)
                packed = jnp.where(line < count_ref[0, 0], packed, dead_mark)
            result_ref[...] = packed.astype(bf16)
            for k in range(groups):
                start = pl.multiple_of(lax.bitwise_xor(plane, k) * size, size)
                found = result_ref[:, pl.ds(start, size)]
                outs[target * groups + k][row, :, low : low + size] = found


def project(place, prepared, weights, gains, sets, groups, first=None):
    size = gains.shape[2]
    width = weights.shape[1]
    columns = groups * size
    fixed = lambda t, place: (0, 0)
    line = lambda t, place: (0,)
    smem = pl.BlockSpec(memory_space=pltpu.SMEM)
    rows = (first or prepared)[1].shape[0]
    square = pl.BlockSpec((rows, rows), fixed)
    whole = pl.BlockSpec((rows, width), fixed)
    steps = [
        (kind, chunk, target, row, i * size)
        for target, (kinds, which) in enumerate(sets)
        for row, chunk in enumerate(which)
        for i, kind in enumerate(kinds)
    ]

    def weight_index(t, place):
        kind, chunk = steps[0][:2]
        for step, found in enumerate(steps):
            kind = jnp.where(t == step, found[0], kind)
            chunk = jnp.where(t == step, found[1], chunk)
        return (kind, 0, chunk)

    shapes = [
        (len(which), rows, len(kinds) * size) for kinds, which in sets for _ in range(groups)
    ]
    out_specs = [pl.BlockSpec(shape, lambda t, place: (0, 0, 0)) for shape in shapes]
    out_shape = [jax.ShapeDtypeStruct(shape, bf16) for shape in shapes]
    if first:
        in_specs = [pl.BlockSpec((rows,), line), whole, pl.BlockSpec((width,), line)]
        out_specs += [whole, square, square, smem]
        out_shape += [
            jax.ShapeDtypeStruct((rows, width), bf16),
            jax.ShapeDtypeStruct((rows, rows), bf16),
            jax.ShapeDtypeStruct((rows, rows), bf16),
            jax.ShapeDtypeStruct((1, 1), jnp.int32),
        ]
    else:
        in_specs = [smem, whole, square]
    found = pl.pallas_call(
        functools.partial(project_body, steps=steps, groups=groups, first=first is not None),
        grid_spec=pltpu.PrefetchScalarGridSpec(
            num_scalar_prefetch=1,
            grid=(len(steps),),
            in_specs=[
                pl.BlockSpec((1, width, columns), weight_index),
                pl.BlockSpec(gains.shape, lambda t, place: (0, 0, 0)),
            ]
            + in_specs,
            out_specs=out_specs,
            scratch_shapes=[pltpu.VMEM((rows, columns), bf16)],
        ),
        out_shape=out_shape,
        compiler_params=params,
        cost_estimate=cost(
            2 * rows * width * len(steps) * columns,
            2 * width * len(steps) * columns + 2 * rows * width,
        ),
        name="project",
    )(place, weights, gains, *(first or prepared))
    blocks = [found[i * groups : (i + 1) * groups] for i in range(len(sets))]
    return blocks, found[len(sets) * groups :]


def attend_body(place_ref, *refs, groups, ordered, gathered, low_lane, key_room, query_rows, key_cols):
    outs = 1 if ordered else groups
    query_refs, sources, out_refs = refs[:groups], refs[groups : -5 - outs], refs[-5 - outs : -5]
    keys, values, queries, results, counts = refs[-5:]
    rows, size = out_refs[0].shape[1:]
    plane = place_ref[0]
    blocks = [(source, k) for source in sources for k in range(source.shape[0])]
    piece = 128 if rows % 128 == 0 else rows
    align = lambda count: pl.multiple_of((count + 15) // 16 * 16, 16)
    line = lax.broadcasted_iota(jnp.int32, (piece, size), 0)

    found = []
    for source, block in blocks:
        live = (source[block, :, :size].astype(f32) < dead_limit).astype(f32)
        counts[len(found)] = jnp.max(jnp.sum(live, axis=0, keepdims=True)).astype(jnp.int32)
        found.append(counts[len(found)])

    offset = jnp.int32(0)
    for (source, block), count in zip(blocks, found):
        for part in range(rows // piece):

            @pl.when(part * piece < count)
            def _():
                here = pl.ds(pl.multiple_of(offset + part * piece, 16), piece)
                there = pl.ds(part * piece, piece)
                live = line + part * piece < count
                key = jnp.where(live, source[block, there, :size].astype(f32), 0.0)
                keys[here, :] = key.astype(bf16)
                values[here, :size] = source[block, there, size:]
                values[here, size:] = live.astype(f32).astype(bf16)

        offset = pl.multiple_of(offset + align(count), 16)

    def clear(step, carry):
        here = pl.ds(pl.multiple_of(offset + step * 16, 16), 16)
        keys[here, :] = jnp.zeros((16, size), bf16)
        values[here, :] = jnp.zeros((16, 2 * size), bf16)
        return carry

    lax.fori_loop(0, (key_room - offset) // 16, clear, 0)

    own = place_ref[1] * groups if gathered else 0
    mine = [counts[own + k] for k in range(groups)]
    starts = []
    start = jnp.int32(0)
    for k in range(groups):
        starts.append(start)
        for part in range(rows // piece):

            @pl.when(part * piece < mine[k])
            def _():
                here = pl.ds(pl.multiple_of(start + part * piece, 16), piece)
                there = pl.ds(part * piece, piece)
                queries[here, :] = query_refs[k][0, there, low_lane : low_lane + size]

        start = pl.multiple_of(start + align(mine[k]), 16)

    def one_tile(tile, carry):
        here = pl.ds(pl.multiple_of(tile * query_rows, query_rows), query_rows)
        query = queries[here, :]
        total = jnp.zeros((query_rows, 2 * size), f32)
        for low in range(0, key_room, key_cols):
            high = min(low + key_cols, key_room)
            scores = lax.dot_general(
                query, keys[low:high, :], (((1,), (1,)), ((), ())), preferred_element_type=f32
            )
            weights = jnp.exp(scores).astype(bf16)
            total += jnp.dot(weights, values[low:high, :], preferred_element_type=f32)
        results[here, :] = (total[:, :size] / total[:, size:]).astype(bf16)
        return carry

    lax.fori_loop(0, (start + query_rows - 1) // query_rows, one_tile, 0)

    for k in range(groups):
        for part in range(rows // piece):
            here = pl.ds(pl.multiple_of(starts[k] + part * piece, 16), piece)
            live = line + part * piece < mine[k]
            kept = jnp.where(live, results[here, :].astype(f32), 0.0).astype(bf16)
            block = lax.bitwise_xor(plane, k) if ordered else 0
            out_refs[0 if ordered else k][block, part * piece : (part + 1) * piece, :] = kept


def attend(place, queries, which, low_lane, keyvals, shards, ordered):
    groups = len(queries)
    rows = keyvals[0].shape[1]
    size = keyvals[0].shape[2] // 2
    running = shards * rows // 2
    key_room = -(-(running + 16 * shards) // 256) * 256
    query_rows = 256
    query_room = -(-groups * rows // query_rows) * query_rows + rows
    query_block = (1,) + queries[0].shape[1:]
    outs, wide = (1, groups) if ordered else (groups, 1)
    return pl.pallas_call(
        functools.partial(
            attend_body,
            groups=groups,
            ordered=ordered,
            gathered=len(keyvals) == 1,
            low_lane=low_lane,
            key_room=key_room,
            query_rows=query_rows,
            key_cols=256,
        ),
        grid_spec=pltpu.PrefetchScalarGridSpec(
            num_scalar_prefetch=1,
            grid=(1,),
            in_specs=[pl.BlockSpec(query_block, lambda i, place: (which, 0, 0))] * groups
            + [pl.BlockSpec(keyvals[0].shape, lambda i, place: (0, 0, 0))] * len(keyvals),
            out_specs=[pl.BlockSpec((wide, rows, size), lambda i, place: (0, 0, 0))] * outs,
            scratch_shapes=[
                pltpu.VMEM((key_room + rows, size), bf16),
                pltpu.VMEM((key_room + rows, 2 * size), bf16),
                pltpu.VMEM((query_room, size), bf16),
                pltpu.VMEM((query_room, size), bf16),
                pltpu.SMEM((shards,), jnp.int32),
            ],
        ),
        out_shape=[jax.ShapeDtypeStruct((wide, rows, size), bf16)] * outs,
        compiler_params=params,
        cost_estimate=cost(
            8 * groups * rows // 2 * running * size,
            4 * shards * rows * size,
            groups * rows // 2 * running,
        ),
        name="attend",
    )(place, *queries, *keyvals)


def finish_body(place_ref, *refs, ordered):
    chunks = len(ordered)
    attended_refs, weight_ref, out_ref, wide_ref = refs[:chunks], *refs[chunks:]

    @pl.when(pl.program_id(0) == 0)
    def _():
        for i, ref in enumerate(attended_refs):
            groups, _, size = ref.shape
            for g in range(groups):
                if ordered[i]:
                    start = (i * groups + g) * size
                else:
                    head = i * groups + lax.bitwise_xor(place_ref[0], g)
                    start = pl.multiple_of(head * size, size)
                wide_ref[:, pl.ds(start, size)] = ref[g]

    total = jnp.dot(wide_ref[...], weight_ref[...], preferred_element_type=f32)
    out_ref[...] = total.astype(out_ref.dtype)


def finish(place, attended, ordered, w_out, mask, kind):
    groups, rows, size = attended[0].shape
    depth = w_out.shape[0]
    out_width = w_out.shape[1] // lax.axis_size("head")
    parts = 4 if out_width % 512 == 0 else 1
    tile = out_width // parts
    column = lambda i, place: (0, lax.bitwise_xor(place[2], mask) * parts + i)
    return pl.pallas_call(
        functools.partial(finish_body, ordered=ordered),
        grid_spec=pltpu.PrefetchScalarGridSpec(
            num_scalar_prefetch=1,
            grid=(parts,),
            in_specs=[pl.BlockSpec((groups, rows, size), lambda i, place: (0, 0, 0))] * len(attended)
            + [pl.BlockSpec((depth, tile), column)],
            out_specs=pl.BlockSpec((rows, tile), lambda i, place: (0, i)),
            scratch_shapes=[pltpu.VMEM((rows, depth), bf16)],
        ),
        out_shape=jax.ShapeDtypeStruct((rows, out_width), kind),
        compiler_params=params,
        cost_estimate=cost(2 * rows * depth * out_width, 2 * depth * out_width + 4 * rows * out_width),
        name="finish",
    )(place, *attended, w_out)


def close_body(back_ref, mine_ref, *refs):
    out_ref = refs[-1]
    total = mine_ref[...]
    for ref in refs[:-1]:
        total += ref[...].astype(f32)
    rounded = total.astype(bf16)
    out_ref[...] = jnp.dot(back_ref[...], rounded, preferred_element_type=f32).astype(bf16)


def close(back, mine, others):
    rows, width = mine.shape
    parts = 4 if width % 512 == 0 else 1
    tile = pl.BlockSpec((rows, width // parts), lambda i: (0, i))
    return pl.pallas_call(
        close_body,
        grid=(parts,),
        in_specs=[pl.BlockSpec((rows, rows), lambda i: (0, 0))] + [tile] * (1 + len(others)),
        out_specs=tile,
        out_shape=jax.ShapeDtypeStruct((rows, width), bf16),
        compiler_params=params,
        cost_estimate=cost(2 * rows * rows * width, 10 * rows * width),
        name="close",
    )(back, mine, *others)


def per_device(tokens, survive, norm_gain, w_qkv, qk_gain, w_out):
    heads, size = qk_gain.shape[1:]
    shards, head_shards = lax.axis_size("seq"), lax.axis_size("head")
    groups = math.gcd(heads & -heads, shards & -shards)
    ring = shards // groups
    chunks = heads // groups
    me, side = lax.axis_index("seq"), lax.axis_index("head")
    place = jnp.stack([me // ring, me % ring, side]).astype(jnp.int32)
    planes = [[i + ring * g for g in range(groups)] for i in range(ring)]
    rings = [[i + ring * g for i in range(ring)] for g in range(groups)]

    def swap(blocks):
        return [blocks[0]] + [flip(blocks[k], "seq", k * ring) for k in range(1, groups)]

    def stack(blocks):
        return jnp.concatenate([block[:, :, : 2 * size] for block in blocks])

    def gather(stacked):
        return [lax.all_gather(stacked, "seq", axis=0, tiled=True, axis_index_groups=rings)]

    def everywhere(stacked, hop, gate):
        if hop is None:
            return gather(stacked)
        found, mask = {0: stacked, ring // 2: hop}, ring // 4
        while mask:
            for known in list(found):
                found[known | mask] = flip(chain(found[known], gate), "seq", mask)
            mask //= 2
        return [found[mask] for mask in range(ring)]

    def hop(stacked):
        return flip(stacked, "seq", ring // 2) if ring > 1 and groups > 1 else None

    def send_back(blocks):
        if groups == 1:
            return blocks
        return lax.all_to_all(
            blocks, "seq", split_axis=0, concat_axis=0, axis_index_groups=planes, tiled=True
        )

    weights = jnp.transpose(w_qkv, (1, 0, 2))
    gains = jnp.transpose(qk_gain, (1, 0, 2))

    def later(values, *earlier):
        return jnp.maximum(chain(values, *earlier), 0)

    def first(blocks):
        return blocks[min(1, groups - 1)]

    def send(blocks, *earlier):
        return swap(list(chain(tuple(blocks), *earlier)) if earlier else blocks)

    operands = (survive, tokens, norm_gain)
    sets = [((1, 2, 0), (0,))]
    (blocks,), rest = project(place, None, weights, gains, sets, groups, operands)
    normed, chosen, back, count = rest
    arrived = [swap(blocks)]

    rest, asked, hops = range(1, chunks), None, [None]
    if chunks > 1:
        prepared = (count, chain(normed, first(arrived[0])), chosen)
        sets = [((1, 2), (chunk,)) for chunk in rest]
        made, _ = project(place, prepared, weights, gains, sets, groups)
        stacks = [stack(list(chain(tuple(arrived[0]), made[0][0])))]
        arrived.append(send(made[0]))
        for blocks in made[1:]:
            arrived.append(send(blocks, first(arrived[-1])))
        stacks.append(stack(arrived[1]))
        hops.append(hop(stacks[1]))
        sets = [((0,), tuple(rest))]
        ready = later(count, stacks[1])
        (made,), _ = project(place, (ready, normed, chosen), weights, gains, sets, groups)
        earlier = [made[0]] + [found for found in hops if found is not None]
        stacks += [stack(list(chain(tuple(blocks), *earlier))) for blocks in arrived[2:]]
        asked = send(made, stacks[-1])
        hops += [hop(stacked) for stacked in stacks[2:]]
    else:
        stacks = [stack(arrived[0])]

    attended, returned = [], []
    query, low_lane = arrived[0], 2 * size
    for chunk in range(chunks):
        final = chunk == chunks - 1
        keyvals = everywhere(stacks[chunk], hops[chunk], tuple(attended[-1:]))
        before = [stacks[-1]] + attended[-1:]
        if chunk:
            before += [hops[-1]] if hops[-1] is not None else []
        elif asked is not None:
            before.append(first(asked))
        before += returned[:1] if final else []
        ready = later(place, *query[1:], *before)
        row = max(chunk - 1, 0)
        found = attend(ready, query, row, low_lane, keyvals, shards, not final)
        attended.append(found[0])
        if final:
            returned.append(jnp.concatenate(swap(found)))
        else:
            returned.append(send_back(found[0]))
            query, low_lane = asked, 0
    ordered = (True,) * (chunks - 1) + (False,)
    final = functools.partial(finish, place, returned, ordered, w_out)
    sent = [final(mask, bf16) for mask in range(1, head_shards)]
    others = [flip(part, "head", mask) for mask, part in enumerate(sent, 1)]
    returned[0] = chain(returned[0], *sent)
    return close(back, final(0, f32), others)


def solution(mesh):
    placed = (
        P("seq", None),
        P("seq"),
        P(),
        P(None, None, "head"),
        P(None, "head", None),
        P("head", None),
    )
    return jax.shard_map(
        per_device, mesh=mesh, in_specs=placed, out_specs=P("seq", "head"), check_vma=False
    )
```

```python
import functools
import math

import jax
import jax.numpy as jnp
from jax import lax
from jax.experimental import pallas as pl
from jax.experimental.pallas import tpu as pltpu
from jax.sharding import PartitionSpec as P

epsilon = 1e-06
dead_mark = 1e30
dead_limit = 1e15
mib = 1 << 20
f32 = jnp.float32
bf16 = jnp.bfloat16
params = pltpu.CompilerParams(vmem_limit_bytes=60 * mib)


def cost(flops, bytes_accessed, exps=0):
    return pl.CostEstimate(
        flops=int(flops), bytes_accessed=int(bytes_accessed), transcendentals=int(exps)
    )


def flip(values, axis, mask):
    size = lax.axis_size(axis)
    return lax.ppermute(values, axis, [(i, i ^ mask) for i in range(size)])


def chain(values, *earlier):
    return lax.optimization_barrier((values, earlier))[0]


def layer_norm(values, gain):
    center = values - jnp.mean(values, axis=-1, keepdims=True)
    spread = jnp.mean(center * center, axis=-1, keepdims=True)
    return center * lax.rsqrt(spread + epsilon) * gain


def prepare(survive_ref, tokens_ref, gain_ref, normed_ref, chosen_ref, back_ref, count_ref):
    positions = tokens_ref.shape[0]
    first = lax.broadcasted_iota(jnp.int32, (positions, positions), 0)
    second = lax.broadcasted_iota(jnp.int32, (positions, positions), 1)
    live = jnp.broadcast_to(survive_ref[...].reshape(1, positions), (8, positions)).astype(f32)
    upper = (first <= second).astype(f32).astype(bf16)
    rank = jnp.dot(live.astype(bf16), upper, preferred_element_type=f32)
    target = jnp.where(live > 0.5, rank - 1.0, -1.0)
    chosen_ref[...] = (first == target[:1].astype(jnp.int32)).astype(f32).astype(bf16)
    home = jnp.transpose(target)[:, :1].astype(jnp.int32)
    back_ref[...] = (second == home).astype(f32).astype(bf16)
    count_ref[0, 0] = jnp.max(rank).astype(jnp.int32)
    gain = gain_ref[...].reshape(1, gain_ref.shape[0])
    rows = 128 if positions % 128 == 0 else positions
    for low in range(0, positions, rows):
        part = tokens_ref[low : low + rows, :].astype(f32)
        normed_ref[low : low + rows, :] = layer_norm(part, gain).astype(bf16)


def project_body(place_ref, *refs, steps, groups, first, joined):
    refs = list(refs)
    result_ref = refs.pop()
    weight_ref, gain_ref = refs[:2]
    if first:
        survive_ref, tokens_ref, norm_gain_ref = refs[2:5]
        outs, (normed_ref, chosen_ref, back_ref, count_ref) = refs[5:-4], refs[-4:]

        @pl.when(pl.program_id(0) == 0)
        def _():
            prepare(
                survive_ref, tokens_ref, norm_gain_ref, normed_ref, chosen_ref, back_ref, count_ref
            )

    else:
        (count_ref, normed_ref, chosen_ref), outs = refs[2:5], refs[5:]
    rows = normed_ref.shape[0]
    size = gain_ref.shape[2]
    plane = place_ref[0]
    for step, (kind, chunk, target, row, low) in enumerate(steps):

        @pl.when(pl.program_id(0) == step)
        def _():
            result = jnp.dot(normed_ref[...], weight_ref[0], preferred_element_type=f32)
            for g in range(groups):
                part = result[:, g * size : (g + 1) * size]
                if kind != 2:
                    gain = gain_ref[chunk * groups + g, kind : kind + 1, :]
                    if kind == 0:
                        gain = gain * (1.0 / math.sqrt(size))
                    part = layer_norm(part, gain)
                result_ref[:, g * size : (g + 1) * size] = part.astype(bf16)
            packed = jnp.dot(chosen_ref[...], result_ref[...], preferred_element_type=f32)
            if kind == 1:
                line = lax.broadcasted_iota(jnp.int32, (rows, groups * size), 0)
                packed = jnp.where(line < count_ref[0, 0], packed, dead_mark)
            result_ref[...] = packed.astype(bf16)
            for k in range(groups):
                if joined:
                    outs[k // groups][k, row] = result_ref[:, k * size : (k + 1) * size]
                else:
                    start = pl.multiple_of(lax.bitwise_xor(plane, k) * size, size)
                    found = result_ref[:, pl.ds(start, size)]
                    outs[target * groups + k][row, :, low : low + size] = found


def project(place, prepared, weights, gains, sets, groups, first=None, joined=False):
    size = gains.shape[2]
    width = weights.shape[1]
    columns = groups * size
    fixed = lambda t, place: (0, 0)
    line = lambda t, place: (0,)
    smem = pl.BlockSpec(memory_space=pltpu.SMEM)
    rows = (first or prepared)[1].shape[0]
    square = pl.BlockSpec((rows, rows), fixed)
    whole = pl.BlockSpec((rows, width), fixed)
    steps = [
        (kind, chunk, target, row, i * size)
        for target, (kinds, which) in enumerate(sets)
        for row, chunk in enumerate(which)
        for i, kind in enumerate(kinds)
    ]

    def weight_index(t, place):
        kind, chunk = steps[0][:2]
        for step, found in enumerate(steps):
            kind = jnp.where(t == step, found[0], kind)
            chunk = jnp.where(t == step, found[1], chunk)
        return (kind, 0, chunk)

    shapes = [
        (len(which), rows, len(kinds) * size) for kinds, which in sets for _ in range(groups)
    ]
    if joined:
        shapes = [(groups, len(sets[0][1]), rows, size)]
    out_specs = [
        pl.BlockSpec(shape, lambda t, place, zeros=(0,) * len(shape): zeros) for shape in shapes
    ]
    out_shape = [jax.ShapeDtypeStruct(shape, bf16) for shape in shapes]
    if first:
        in_specs = [pl.BlockSpec((rows,), line), whole, pl.BlockSpec((width,), line)]
        out_specs += [whole, square, square, smem]
        out_shape += [
            jax.ShapeDtypeStruct((rows, width), bf16),
            jax.ShapeDtypeStruct((rows, rows), bf16),
            jax.ShapeDtypeStruct((rows, rows), bf16),
            jax.ShapeDtypeStruct((1, 1), jnp.int32),
        ]
    else:
        in_specs = [smem, whole, square]
    found = pl.pallas_call(
        functools.partial(
            project_body, steps=steps, groups=groups, first=first is not None, joined=joined
        ),
        grid_spec=pltpu.PrefetchScalarGridSpec(
            num_scalar_prefetch=1,
            grid=(len(steps),),
            in_specs=[
                pl.BlockSpec((1, width, columns), weight_index),
                pl.BlockSpec(gains.shape, lambda t, place: (0, 0, 0)),
            ]
            + in_specs,
            out_specs=out_specs,
            scratch_shapes=[pltpu.VMEM((rows, columns), bf16)],
        ),
        out_shape=out_shape,
        compiler_params=params,
        cost_estimate=cost(
            2 * rows * width * len(steps) * columns,
            2 * width * len(steps) * columns + 2 * rows * width,
        ),
        name="project",
    )(place, weights, gains, *(first or prepared))
    if joined:
        return found[0], []
    blocks = [found[i * groups : (i + 1) * groups] for i in range(len(sets))]
    return blocks, found[len(sets) * groups :]


def attend_body(place_ref, *refs, groups, asked, joined, ordered, low_lane, key_room, query_rows, key_cols):
    outs = 1 if ordered else groups
    query_refs, sources, out_refs = refs[:asked], refs[asked : -4 - outs], refs[-4 - outs : -4]
    keys, values, queries, results = refs[-4:]
    rows, size = out_refs[0].shape[1:]
    plane = place_ref[0]
    blocks = [(source, k) for source in sources for k in range(groups)]
    piece = 128 if rows % 128 == 0 else rows
    align = lambda count: pl.multiple_of((count + 15) // 16 * 16, 16)
    line = lax.broadcasted_iota(jnp.int32, (piece, size), 0)

    found = []
    for source, block in blocks:
        live = (source[block, :, :size].astype(f32) < dead_limit).astype(f32)
        found.append(jnp.max(jnp.sum(live, axis=0, keepdims=True)).astype(jnp.int32))

    offset = jnp.int32(0)
    for (source, block), count in zip(blocks, found):
        for part in range(rows // piece):

            @pl.when(part * piece < count)
            def _():
                here = pl.ds(pl.multiple_of(offset + part * piece, 16), piece)
                there = pl.ds(part * piece, piece)
                live = line + part * piece < count
                key = jnp.where(live, source[block, there, :size].astype(f32), 0.0)
                keys[here, :] = key.astype(bf16)
                values[here, :size] = source[block, there, size:]
                values[here, size:] = live.astype(f32).astype(bf16)

        offset = pl.multiple_of(offset + align(count), 16)

    def clear(step, carry):
        here = pl.ds(pl.multiple_of(offset + step * 16, 16), 16)
        keys[here, :] = jnp.zeros((16, size), bf16)
        values[here, :] = jnp.zeros((16, 2 * size), bf16)
        return carry

    lax.fori_loop(0, (key_room - offset) // 16, clear, 0)

    mine = found[:groups]
    starts = []
    start = jnp.int32(0)
    for k in range(groups):
        starts.append(start)
        for part in range(rows // piece):

            @pl.when(part * piece < mine[k])
            def _():
                here = pl.ds(pl.multiple_of(start + part * piece, 16), piece)
                there = pl.ds(part * piece, piece)
                if joined:
                    found = query_refs[0][lax.bitwise_xor(plane, k), 0, there, :]
                else:
                    found = query_refs[k][0, there, low_lane : low_lane + size]
                queries[here, :] = found

        start = pl.multiple_of(start + align(mine[k]), 16)

    def one_tile(tile, carry):
        here = pl.ds(pl.multiple_of(tile * query_rows, query_rows), query_rows)
        query = queries[here, :]
        total = jnp.zeros((query_rows, 2 * size), f32)
        for low in range(0, key_room, key_cols):
            high = min(low + key_cols, key_room)
            scores = lax.dot_general(
                query, keys[low:high, :], (((1,), (1,)), ((), ())), preferred_element_type=f32
            )
            weights = jnp.exp(scores).astype(bf16)
            total += jnp.dot(weights, values[low:high, :], preferred_element_type=f32)
        results[here, :] = (total[:, :size] / total[:, size:]).astype(bf16)
        return carry

    lax.fori_loop(0, (start + query_rows - 1) // query_rows, one_tile, 0)

    for k in range(groups):
        for part in range(rows // piece):
            here = pl.ds(pl.multiple_of(starts[k] + part * piece, 16), piece)
            live = line + part * piece < mine[k]
            kept = jnp.where(live, results[here, :].astype(f32), 0.0).astype(bf16)
            block = lax.bitwise_xor(plane, k) if ordered else 0
            out_refs[0 if ordered else k][block, part * piece : (part + 1) * piece, :] = kept


def attend(place, queries, which, low_lane, keyvals, shards, ordered):
    groups = keyvals[0].shape[0]
    joined = queries[0].ndim == 4
    rows = keyvals[0].shape[1]
    size = keyvals[0].shape[2] // 2
    running = shards * rows // 2
    key_room = -(-(running + 16 * shards) // 256) * 256
    query_rows = 256
    query_room = -(-groups * rows // query_rows) * query_rows + rows
    if joined:
        query_block = pl.BlockSpec((groups, 1, rows, size), lambda i, place: (0, which, 0, 0))
    else:
        query_block = pl.BlockSpec((1,) + queries[0].shape[1:], lambda i, place: (which, 0, 0))
    outs, wide = (1, groups) if ordered else (groups, 1)
    return pl.pallas_call(
        functools.partial(
            attend_body,
            groups=groups,
            asked=len(queries),
            joined=joined,
            ordered=ordered,
            low_lane=low_lane,
            key_room=key_room,
            query_rows=query_rows,
            key_cols=256,
        ),
        grid_spec=pltpu.PrefetchScalarGridSpec(
            num_scalar_prefetch=1,
            grid=(1,),
            in_specs=[query_block] * len(queries)
            + [pl.BlockSpec(keyvals[0].shape, lambda i, place: (0, 0, 0))] * len(keyvals),
            out_specs=[pl.BlockSpec((wide, rows, size), lambda i, place: (0, 0, 0))] * outs,
            scratch_shapes=[
                pltpu.VMEM((key_room + rows, size), bf16),
                pltpu.VMEM((key_room + rows, 2 * size), bf16),
                pltpu.VMEM((query_room, size), bf16),
                pltpu.VMEM((query_room, size), bf16),
            ],
        ),
        out_shape=[jax.ShapeDtypeStruct((wide, rows, size), bf16)] * outs,
        compiler_params=params,
        cost_estimate=cost(
            8 * groups * rows // 2 * running * size,
            4 * shards * rows * size,
            groups * rows // 2 * running,
        ),
        name="attend",
    )(place, *queries, *keyvals)


def finish_body(place_ref, *refs, ordered):
    chunks = len(ordered)
    attended_refs, weight_ref, out_ref, wide_ref = refs[:chunks], *refs[chunks:]

    @pl.when(pl.program_id(0) == 0)
    def _():
        for i, ref in enumerate(attended_refs):
            groups, _, size = ref.shape
            for g in range(groups):
                if ordered[i]:
                    start = (i * groups + g) * size
                else:
                    head = i * groups + lax.bitwise_xor(place_ref[0], g)
                    start = pl.multiple_of(head * size, size)
                wide_ref[:, pl.ds(start, size)] = ref[g]

    total = jnp.dot(wide_ref[...], weight_ref[...], preferred_element_type=f32)
    out_ref[...] = total.astype(out_ref.dtype)


def finish(place, attended, ordered, w_out, mask, kind):
    groups, rows, size = attended[0].shape
    depth = w_out.shape[0]
    out_width = w_out.shape[1] // lax.axis_size("head")
    parts = 4 if out_width % 512 == 0 else 1
    tile = out_width // parts
    column = lambda i, place: (0, lax.bitwise_xor(place[2], mask) * parts + i)
    return pl.pallas_call(
        functools.partial(finish_body, ordered=ordered),
        grid_spec=pltpu.PrefetchScalarGridSpec(
            num_scalar_prefetch=1,
            grid=(parts,),
            in_specs=[pl.BlockSpec((groups, rows, size), lambda i, place: (0, 0, 0))] * len(attended)
            + [pl.BlockSpec((depth, tile), column)],
            out_specs=pl.BlockSpec((rows, tile), lambda i, place: (0, i)),
            scratch_shapes=[pltpu.VMEM((rows, depth), bf16)],
        ),
        out_shape=jax.ShapeDtypeStruct((rows, out_width), kind),
        compiler_params=params,
        cost_estimate=cost(2 * rows * depth * out_width, 2 * depth * out_width + 4 * rows * out_width),
        name="finish",
    )(place, *attended, w_out)


def close_body(back_ref, mine_ref, *refs):
    out_ref = refs[-1]
    total = mine_ref[...].astype(f32)
    for ref in refs[:-1]:
        total += ref[...].astype(f32)
    rounded = total.astype(bf16)
    out_ref[...] = jnp.dot(back_ref[...], rounded, preferred_element_type=f32).astype(bf16)


def close(back, mine, others):
    rows, width = mine.shape
    parts = 4 if width % 512 == 0 else 1
    tile = pl.BlockSpec((rows, width // parts), lambda i: (0, i))
    return pl.pallas_call(
        close_body,
        grid=(parts,),
        in_specs=[pl.BlockSpec((rows, rows), lambda i: (0, 0))] + [tile] * (1 + len(others)),
        out_specs=tile,
        out_shape=jax.ShapeDtypeStruct((rows, width), bf16),
        compiler_params=params,
        cost_estimate=cost(2 * rows * rows * width, 10 * rows * width),
        name="close",
    )(back, mine, *others)


def per_device(tokens, survive, norm_gain, w_qkv, qk_gain, w_out):
    heads, size = qk_gain.shape[1:]
    shards, head_shards = lax.axis_size("seq"), lax.axis_size("head")
    groups = math.gcd(heads & -heads, shards & -shards)
    ring = shards // groups
    chunks = heads // groups
    me, side = lax.axis_index("seq"), lax.axis_index("head")
    place = jnp.stack([me // ring, me % ring, side]).astype(jnp.int32)
    planes = [[i + ring * g for g in range(groups)] for i in range(ring)]

    def swap(blocks):
        return [blocks[0]] + [flip(blocks[k], "seq", k * ring) for k in range(1, groups)]

    def stack(blocks):
        return jnp.concatenate([block[:, :, : 2 * size] for block in blocks])

    def everywhere(stacked, gate):
        found = {0: stacked}
        mask = ring // 2
        while mask:
            for known in list(found):
                source = found[known]
                if gate is not None and mask < ring // 2:
                    source = chain(source, gate)
                found[known | mask] = flip(source, "seq", mask)
            mask //= 2
        return [found[mask] for mask in range(ring)]

    def send_back(blocks):
        if groups == 1:
            return blocks
        return lax.all_to_all(
            blocks, "seq", split_axis=0, concat_axis=0, axis_index_groups=planes, tiled=True
        )

    weights = jnp.transpose(w_qkv, (1, 0, 2))
    gains = jnp.transpose(qk_gain, (1, 0, 2))

    def later(values, *earlier):
        return jnp.maximum(chain(values, *earlier), 0)

    def first(blocks):
        return blocks[min(1, groups - 1)]

    def send(blocks, *earlier):
        return swap(list(chain(tuple(blocks), *earlier)) if earlier else blocks)

    operands = (survive, tokens, norm_gain)
    sets = [((1, 2, 0), (0,))]
    (blocks,), rest = project(place, None, weights, gains, sets, groups, operands)
    normed, chosen, back, count = rest
    arrived = [swap(blocks)]

    rest, asked, hops = range(1, chunks), None, []
    if chunks > 1:
        prepared = (count, chain(normed, first(arrived[0])), chosen)
        sets = [((1, 2), (chunk,)) for chunk in rest]
        made, _ = project(place, prepared, weights, gains, sets, groups)
        stacks = [stack(list(chain(tuple(arrived[0]), made[0][0])))]
        arrived.append(send(made[0]))
        for blocks in made[1:]:
            arrived.append(send(blocks, first(arrived[-1])))
        hop = flip(stacks[0], "seq", ring // 2) if ring > 1 else stacks[0]
        stacks.append(stack(arrived[1]))
        ready = later(count, hop, stacks[1])
        sets = [((0,), tuple(rest))]
        made, _ = project(
            place, (ready, normed, chosen), weights, gains, sets, groups, joined=True
        )
        gate = made
        stacks += [stack(list(chain(tuple(blocks), made))) for blocks in arrived[2:]]
        asked = [send_back(made)]
        hops = [flip(stacks[-1], "seq", ring // 2)] if ring > 1 else []
    else:
        gate, stacks = None, [stack(arrived[0])]

    attended, returned = [], []
    query, low_lane = arrived[0], 2 * size
    for chunk in range(chunks):
        final = chunk == chunks - 1
        keyvals = everywhere(stacks[chunk], gate)
        before = [stacks[-1]] + attended[-1:] + (hops if chunk else []) + (returned[:1] if final else [])
        ready = later(place, *query[1 if chunk == 0 else 0 :], *before)
        row = max(chunk - 1, 0)
        found = attend(ready, query, row, low_lane, keyvals, shards, not final)
        attended.append(found[0])
        returned.append(jnp.concatenate(swap(found)) if final else send_back(found[0]))
        if not final:
            query, low_lane, gate = asked, 0, None
    ordered = (True,) * (chunks - 1) + (False,)
    final = functools.partial(finish, place, returned, ordered, w_out)
    sent = [final(mask, bf16) for mask in range(1, head_shards)]
    others = [flip(part, "head", mask) for mask, part in enumerate(sent, 1)]
    returned[0] = chain(returned[0], *sent)
    return close(back, final(0, bf16), others)


def solution(mesh):
    placed = (
        P("seq", None),
        P("seq"),
        P(),
        P(None, None, "head"),
        P(None, "head", None),
        P("head", None),
    )
    return jax.shard_map(
        per_device, mesh=mesh, in_specs=placed, out_specs=P("seq", "head"), check_vma=False
    )
```

```python
import functools
import math

import jax
import jax.numpy as jnp
from jax import lax
from jax.experimental import pallas as pl
from jax.experimental.pallas import tpu as pltpu
from jax.sharding import PartitionSpec as P

epsilon = 1e-06
dead_mark = 1e30
dead_limit = 1e15
mib = 1 << 20
f32 = jnp.float32
bf16 = jnp.bfloat16
params = pltpu.CompilerParams(vmem_limit_bytes=60 * mib)


def cost(flops, bytes_accessed, exps=0):
    return pl.CostEstimate(
        flops=int(flops), bytes_accessed=int(bytes_accessed), transcendentals=int(exps)
    )


def flip(values, axis, mask):
    size = lax.axis_size(axis)
    return lax.ppermute(values, axis, [(i, i ^ mask) for i in range(size)])


def chain(values, *earlier):
    return lax.optimization_barrier((values, earlier))[0]


def layer_norm(values, gain):
    center = values - jnp.mean(values, axis=-1, keepdims=True)
    spread = jnp.mean(center * center, axis=-1, keepdims=True)
    return center * lax.rsqrt(spread + epsilon) * gain


def prepare(survive_ref, tokens_ref, gain_ref, normed_ref, chosen_ref, back_ref, count_ref):
    positions = tokens_ref.shape[0]
    first = lax.broadcasted_iota(jnp.int32, (positions, positions), 0)
    second = lax.broadcasted_iota(jnp.int32, (positions, positions), 1)
    live = jnp.broadcast_to(survive_ref[...].reshape(1, positions), (8, positions)).astype(f32)
    upper = (first <= second).astype(f32).astype(bf16)
    rank = jnp.dot(live.astype(bf16), upper, preferred_element_type=f32)
    target = jnp.where(live > 0.5, rank - 1.0, -1.0)
    chosen_ref[...] = (first == target[:1].astype(jnp.int32)).astype(f32).astype(bf16)
    home = jnp.transpose(target)[:, :1].astype(jnp.int32)
    back_ref[...] = (second == home).astype(f32).astype(bf16)
    count_ref[0, 0] = jnp.max(rank).astype(jnp.int32)
    gain = gain_ref[...].reshape(1, gain_ref.shape[0])
    rows = 128 if positions % 128 == 0 else positions
    for low in range(0, positions, rows):
        part = tokens_ref[low : low + rows, :].astype(f32)
        normed_ref[low : low + rows, :] = layer_norm(part, gain).astype(bf16)


def project_body(place_ref, *refs, steps, groups, first, joined):
    refs = list(refs)
    result_ref = refs.pop()
    weight_ref, gain_ref = refs[:2]
    if first:
        survive_ref, tokens_ref, norm_gain_ref = refs[2:5]
        outs, (normed_ref, chosen_ref, back_ref, count_ref) = refs[5:-4], refs[-4:]

        @pl.when(pl.program_id(0) == 0)
        def _():
            prepare(
                survive_ref, tokens_ref, norm_gain_ref, normed_ref, chosen_ref, back_ref, count_ref
            )

    else:
        (count_ref, normed_ref, chosen_ref), outs = refs[2:5], refs[5:]
    rows = normed_ref.shape[0]
    size = gain_ref.shape[2]
    plane = place_ref[0]
    for step, (kind, chunk, target, row, low) in enumerate(steps):

        @pl.when(pl.program_id(0) == step)
        def _():
            result = jnp.dot(normed_ref[...], weight_ref[0], preferred_element_type=f32)
            for g in range(groups):
                part = result[:, g * size : (g + 1) * size]
                if kind != 2:
                    gain = gain_ref[chunk * groups + g, kind : kind + 1, :]
                    if kind == 0:
                        gain = gain * (1.0 / math.sqrt(size))
                    part = layer_norm(part, gain)
                result_ref[:, g * size : (g + 1) * size] = part.astype(bf16)
            packed = jnp.dot(chosen_ref[...], result_ref[...], preferred_element_type=f32)
            if kind == 1:
                line = lax.broadcasted_iota(jnp.int32, (rows, groups * size), 0)
                packed = jnp.where(line < count_ref[0, 0], packed, dead_mark)
            result_ref[...] = packed.astype(bf16)
            for k in range(groups):
                if joined:
                    found = result_ref[:, k * size : (k + 1) * size]
                    outs[target][k, row, :, low : low + size] = found
                else:
                    start = pl.multiple_of(lax.bitwise_xor(plane, k) * size, size)
                    found = result_ref[:, pl.ds(start, size)]
                    outs[target * groups + k][row, :, low : low + size] = found


def project(place, prepared, weights, gains, sets, groups, first=None, joined=False):
    size = gains.shape[2]
    width = weights.shape[1]
    columns = groups * size
    fixed = lambda t, place: (0, 0)
    line = lambda t, place: (0,)
    smem = pl.BlockSpec(memory_space=pltpu.SMEM)
    rows = (first or prepared)[1].shape[0]
    square = pl.BlockSpec((rows, rows), fixed)
    whole = pl.BlockSpec((rows, width), fixed)
    steps = [
        (kind, chunk, target, row, i * size)
        for target, (kinds, which) in enumerate(sets)
        for row, chunk in enumerate(which)
        for i, kind in enumerate(kinds)
    ]

    def weight_index(t, place):
        kind, chunk = steps[0][:2]
        for step, found in enumerate(steps):
            kind = jnp.where(t == step, found[0], kind)
            chunk = jnp.where(t == step, found[1], chunk)
        return (kind, 0, chunk)

    shapes = [
        (len(which), rows, len(kinds) * size) for kinds, which in sets for _ in range(groups)
    ]
    if joined:
        shapes = [(groups, len(which), rows, len(kinds) * size) for kinds, which in sets]
    out_specs = [
        pl.BlockSpec(shape, lambda t, place, zeros=(0,) * len(shape): zeros) for shape in shapes
    ]
    out_shape = [jax.ShapeDtypeStruct(shape, bf16) for shape in shapes]
    if first:
        in_specs = [pl.BlockSpec((rows,), line), whole, pl.BlockSpec((width,), line)]
        out_specs += [whole, square, square, smem]
        out_shape += [
            jax.ShapeDtypeStruct((rows, width), bf16),
            jax.ShapeDtypeStruct((rows, rows), bf16),
            jax.ShapeDtypeStruct((rows, rows), bf16),
            jax.ShapeDtypeStruct((1, 1), jnp.int32),
        ]
    else:
        in_specs = [smem, whole, square]
    found = pl.pallas_call(
        functools.partial(
            project_body, steps=steps, groups=groups, first=first is not None, joined=joined
        ),
        grid_spec=pltpu.PrefetchScalarGridSpec(
            num_scalar_prefetch=1,
            grid=(len(steps),),
            in_specs=[
                pl.BlockSpec((1, width, columns), weight_index),
                pl.BlockSpec(gains.shape, lambda t, place: (0, 0, 0)),
            ]
            + in_specs,
            out_specs=out_specs,
            scratch_shapes=[pltpu.VMEM((rows, columns), bf16)],
        ),
        out_shape=out_shape,
        compiler_params=params,
        cost_estimate=cost(
            2 * rows * width * len(steps) * columns,
            2 * width * len(steps) * columns + 2 * rows * width,
        ),
        name="project",
    )(place, weights, gains, *(first or prepared))
    if joined:
        return found[: len(sets)], []
    blocks = [found[i * groups : (i + 1) * groups] for i in range(len(sets))]
    return blocks, found[len(sets) * groups :]


def attend_body(place_ref, *refs, groups, asked, joined, ordered, low_lane, key_room, query_rows, key_cols):
    outs = 1 if ordered else groups
    query_refs, sources, out_refs = refs[:asked], refs[asked : -5 - outs], refs[-5 - outs : -5]
    keys, values, queries, results, counts = refs[-5:]
    rows, size = out_refs[0].shape[1:]
    plane = place_ref[0]
    blocks = [(source, k) for source in sources for k in range(groups)]
    piece = 128 if rows % 128 == 0 else rows
    align = lambda count: pl.multiple_of((count + 15) // 16 * 16, 16)
    line = lax.broadcasted_iota(jnp.int32, (piece, size), 0)

    found = []
    for source, block in blocks:
        live = (source[block, :, :size].astype(f32) < dead_limit).astype(f32)
        counts[len(found)] = jnp.max(jnp.sum(live, axis=0, keepdims=True)).astype(jnp.int32)
        found.append(counts[len(found)])

    offset = jnp.int32(0)
    for (source, block), count in zip(blocks, found):
        for part in range(rows // piece):

            @pl.when(part * piece < count)
            def _():
                here = pl.ds(pl.multiple_of(offset + part * piece, 16), piece)
                there = pl.ds(part * piece, piece)
                live = line + part * piece < count
                key = jnp.where(live, source[block, there, :size].astype(f32), 0.0)
                keys[here, :] = key.astype(bf16)
                values[here, :size] = source[block, there, size:]
                values[here, size:] = live.astype(f32).astype(bf16)

        offset = pl.multiple_of(offset + align(count), 16)

    def clear(step, carry):
        here = pl.ds(pl.multiple_of(offset + step * 16, 16), 16)
        keys[here, :] = jnp.zeros((16, size), bf16)
        values[here, :] = jnp.zeros((16, 2 * size), bf16)
        return carry

    lax.fori_loop(0, (key_room - offset) // 16, clear, 0)

    mine = [counts[lax.bitwise_xor(plane, k) if joined else k] for k in range(groups)]
    starts = []
    start = jnp.int32(0)
    for k in range(groups):
        starts.append(start)
        for part in range(rows // piece):

            @pl.when(part * piece < mine[k])
            def _():
                here = pl.ds(pl.multiple_of(start + part * piece, 16), piece)
                there = pl.ds(part * piece, piece)
                if joined:
                    found = query_refs[0][lax.bitwise_xor(plane, k), 0, there, :]
                else:
                    found = query_refs[k][0, there, low_lane : low_lane + size]
                queries[here, :] = found

        start = pl.multiple_of(start + align(mine[k]), 16)

    def one_tile(tile, carry):
        here = pl.ds(pl.multiple_of(tile * query_rows, query_rows), query_rows)
        query = queries[here, :]
        total = jnp.zeros((query_rows, 2 * size), f32)
        for low in range(0, key_room, key_cols):
            high = min(low + key_cols, key_room)
            scores = lax.dot_general(
                query, keys[low:high, :], (((1,), (1,)), ((), ())), preferred_element_type=f32
            )
            weights = jnp.exp(scores).astype(bf16)
            total += jnp.dot(weights, values[low:high, :], preferred_element_type=f32)
        results[here, :] = (total[:, :size] / total[:, size:]).astype(bf16)
        return carry

    lax.fori_loop(0, (start + query_rows - 1) // query_rows, one_tile, 0)

    for k in range(groups):
        for part in range(rows // piece):
            here = pl.ds(pl.multiple_of(starts[k] + part * piece, 16), piece)
            live = line + part * piece < mine[k]
            kept = jnp.where(live, results[here, :].astype(f32), 0.0).astype(bf16)
            block = lax.bitwise_xor(plane, k) if ordered else 0
            out_refs[0 if ordered else k][block, part * piece : (part + 1) * piece, :] = kept


def attend(place, queries, which, low_lane, keyvals, shards, ordered):
    groups = keyvals[0].shape[0]
    joined = queries[0].ndim == 4
    rows = keyvals[0].shape[1]
    size = keyvals[0].shape[2] // 2
    running = shards * rows // 2
    key_room = -(-(running + 16 * shards) // 256) * 256
    query_rows = 256
    query_room = -(-groups * rows // query_rows) * query_rows + rows
    if joined:
        query_block = pl.BlockSpec((groups, 1, rows, size), lambda i, place: (0, which, 0, 0))
    else:
        query_block = pl.BlockSpec((1,) + queries[0].shape[1:], lambda i, place: (which, 0, 0))
    outs, wide = (1, groups) if ordered else (groups, 1)
    return pl.pallas_call(
        functools.partial(
            attend_body,
            groups=groups,
            asked=len(queries),
            joined=joined,
            ordered=ordered,
            low_lane=low_lane,
            key_room=key_room,
            query_rows=query_rows,
            key_cols=256,
        ),
        grid_spec=pltpu.PrefetchScalarGridSpec(
            num_scalar_prefetch=1,
            grid=(1,),
            in_specs=[query_block] * len(queries)
            + [pl.BlockSpec(keyvals[0].shape, lambda i, place: (0, 0, 0))] * len(keyvals),
            out_specs=[pl.BlockSpec((wide, rows, size), lambda i, place: (0, 0, 0))] * outs,
            scratch_shapes=[
                pltpu.VMEM((key_room + rows, size), bf16),
                pltpu.VMEM((key_room + rows, 2 * size), bf16),
                pltpu.VMEM((query_room, size), bf16),
                pltpu.VMEM((query_room, size), bf16),
                pltpu.SMEM((shards,), jnp.int32),
            ],
        ),
        out_shape=[jax.ShapeDtypeStruct((wide, rows, size), bf16)] * outs,
        compiler_params=params,
        cost_estimate=cost(
            8 * groups * rows // 2 * running * size,
            4 * shards * rows * size,
            groups * rows // 2 * running,
        ),
        name="attend",
    )(place, *queries, *keyvals)


def finish_body(place_ref, *refs, ordered):
    chunks = len(ordered)
    attended_refs, weight_ref, out_ref, wide_ref = refs[:chunks], *refs[chunks:]

    @pl.when(pl.program_id(0) == 0)
    def _():
        for i, ref in enumerate(attended_refs):
            groups, _, size = ref.shape
            for g in range(groups):
                if ordered[i]:
                    start = (i * groups + g) * size
                else:
                    head = i * groups + lax.bitwise_xor(place_ref[0], g)
                    start = pl.multiple_of(head * size, size)
                wide_ref[:, pl.ds(start, size)] = ref[g]

    total = jnp.dot(wide_ref[...], weight_ref[...], preferred_element_type=f32)
    out_ref[...] = total.astype(out_ref.dtype)


def finish(place, attended, ordered, w_out, mask, kind):
    groups, rows, size = attended[0].shape
    depth = w_out.shape[0]
    out_width = w_out.shape[1] // lax.axis_size("head")
    parts = 4 if out_width % 512 == 0 else 1
    tile = out_width // parts
    column = lambda i, place: (0, lax.bitwise_xor(place[2], mask) * parts + i)
    return pl.pallas_call(
        functools.partial(finish_body, ordered=ordered),
        grid_spec=pltpu.PrefetchScalarGridSpec(
            num_scalar_prefetch=1,
            grid=(parts,),
            in_specs=[pl.BlockSpec((groups, rows, size), lambda i, place: (0, 0, 0))] * len(attended)
            + [pl.BlockSpec((depth, tile), column)],
            out_specs=pl.BlockSpec((rows, tile), lambda i, place: (0, i)),
            scratch_shapes=[pltpu.VMEM((rows, depth), bf16)],
        ),
        out_shape=jax.ShapeDtypeStruct((rows, out_width), kind),
        compiler_params=params,
        cost_estimate=cost(2 * rows * depth * out_width, 2 * depth * out_width + 4 * rows * out_width),
        name="finish",
    )(place, *attended, w_out)


def close_body(back_ref, mine_ref, *refs):
    out_ref = refs[-1]
    total = mine_ref[...].astype(f32)
    for ref in refs[:-1]:
        total += ref[...].astype(f32)
    rounded = total.astype(bf16)
    out_ref[...] = jnp.dot(back_ref[...], rounded, preferred_element_type=f32).astype(bf16)


def close(back, mine, others):
    rows, width = mine.shape
    parts = 4 if width % 512 == 0 else 1
    tile = pl.BlockSpec((rows, width // parts), lambda i: (0, i))
    return pl.pallas_call(
        close_body,
        grid=(parts,),
        in_specs=[pl.BlockSpec((rows, rows), lambda i: (0, 0))] + [tile] * (1 + len(others)),
        out_specs=tile,
        out_shape=jax.ShapeDtypeStruct((rows, width), bf16),
        compiler_params=params,
        cost_estimate=cost(2 * rows * rows * width, 10 * rows * width),
        name="close",
    )(back, mine, *others)


def per_device(tokens, survive, norm_gain, w_qkv, qk_gain, w_out):
    heads, size = qk_gain.shape[1:]
    shards, head_shards = lax.axis_size("seq"), lax.axis_size("head")
    groups = math.gcd(heads & -heads, shards & -shards)
    ring = shards // groups
    chunks = heads // groups
    me, side = lax.axis_index("seq"), lax.axis_index("head")
    place = jnp.stack([me // ring, me % ring, side]).astype(jnp.int32)
    planes = [[i + ring * g for g in range(groups)] for i in range(ring)]

    def swap(blocks):
        return [blocks[0]] + [flip(blocks[k], "seq", k * ring) for k in range(1, groups)]

    def stack(blocks):
        return jnp.concatenate([block[:, :, : 2 * size] for block in blocks])

    def everywhere(stacked, gate):
        found = {0: stacked}
        mask = ring // 2
        while mask:
            for known in list(found):
                source = found[known]
                if gate is not None and mask < ring // 2:
                    source = chain(source, gate)
                found[known | mask] = flip(source, "seq", mask)
            mask //= 2
        return [found[mask] for mask in range(ring)]

    def send_back(blocks):
        if groups == 1:
            return blocks
        return lax.all_to_all(
            blocks, "seq", split_axis=0, concat_axis=0, axis_index_groups=planes, tiled=True
        )

    weights = jnp.transpose(w_qkv, (1, 0, 2))
    gains = jnp.transpose(qk_gain, (1, 0, 2))

    def later(values, *earlier):
        return jnp.maximum(chain(values, *earlier), 0)

    def first(blocks):
        return blocks[min(1, groups - 1)]

    def send(blocks, *earlier):
        return swap(list(chain(tuple(blocks), *earlier)) if earlier else blocks)

    operands = (survive, tokens, norm_gain)
    sets = [((1, 2, 0), (0,))]
    (blocks,), rest = project(place, None, weights, gains, sets, groups, operands)
    normed, chosen, back, count = rest
    arrived = [swap(blocks)]

    rest, asked, hops = range(1, chunks), None, []
    if chunks > 1:
        prepared = (count, chain(normed, first(arrived[0])), chosen)
        sets = [((1, 2), (chunk,)) for chunk in rest]
        made, _ = project(place, prepared, weights, gains, sets, groups, joined=True)
        stacks = [stack(list(chain(tuple(arrived[0]), made[0])))]
        shape = (groups, survive.shape[0], 2 * size)
        for blocks in made:
            stacks.append(send_back(chain(blocks.reshape(shape), stacks[-1])))
        hop = flip(stacks[0], "seq", ring // 2) if ring > 1 else stacks[0]
        sets = [((0,), tuple(rest))]
        ready = later(count, hop, stacks[1])
        (gate,), _ = project(
            place, (ready, normed, chosen), weights, gains, sets, groups, joined=True
        )
        stacks[2:] = [chain(blocks, gate) for blocks in stacks[2:]]
        asked = [send_back(gate)]
        hops = [flip(stacks[-1], "seq", ring // 2)] if ring > 1 else []
    else:
        gate, stacks = None, [stack(arrived[0])]

    attended, returned = [], []
    query, low_lane = arrived[0], 2 * size
    for chunk in range(chunks):
        final = chunk == chunks - 1
        keyvals = everywhere(stacks[chunk], gate)
        before = ([stacks[-1]] if chunk else []) + attended[-1:]
        before += (hops if chunk else []) + (returned[:1] if final else [])
        ready = later(place, *query[1 if chunk == 0 else 0 :], *before)
        row = max(chunk - 1, 0)
        found = attend(ready, query, row, low_lane, keyvals, shards, not final)
        attended.append(found[0])
        returned.append(jnp.concatenate(swap(found)) if final else send_back(found[0]))
        if not final:
            query, low_lane, gate = asked, 0, None
    ordered = (True,) * (chunks - 1) + (False,)
    final = functools.partial(finish, place, returned, ordered, w_out)
    sent = [final(mask, bf16) for mask in range(1, head_shards)]
    others = [flip(part, "head", mask) for mask, part in enumerate(sent, 1)]
    returned[0] = chain(returned[0], *sent)
    return close(back, final(0, bf16), others)


def solution(mesh):
    placed = (
        P("seq", None),
        P("seq"),
        P(),
        P(None, None, "head"),
        P(None, "head", None),
        P("head", None),
    )
    return jax.shard_map(
        per_device, mesh=mesh, in_specs=placed, out_specs=P("seq", "head"), check_vma=False
    )
```

```python
import functools
import math

import jax
import jax.numpy as jnp
from jax import lax
from jax.experimental import pallas as pl
from jax.experimental.pallas import tpu as pltpu
from jax.sharding import PartitionSpec as P

epsilon = 1e-06
dead_mark = 1e30
dead_limit = 1e15
mib = 1 << 20
f32 = jnp.float32
bf16 = jnp.bfloat16
params = pltpu.CompilerParams(vmem_limit_bytes=60 * mib)


def cost(flops, bytes_accessed, exps=0):
    return pl.CostEstimate(
        flops=int(flops), bytes_accessed=int(bytes_accessed), transcendentals=int(exps)
    )


def flip(values, axis, mask):
    size = lax.axis_size(axis)
    return lax.ppermute(values, axis, [(i, i ^ mask) for i in range(size)])


def chain(values, *earlier):
    return lax.optimization_barrier((values, earlier))[0]


def layer_norm(values, gain):
    center = values - jnp.mean(values, axis=-1, keepdims=True)
    spread = jnp.mean(center * center, axis=-1, keepdims=True)
    return center * lax.rsqrt(spread + epsilon) * gain


def prepare(survive_ref, tokens_ref, gain_ref, normed_ref, chosen_ref, back_ref, count_ref):
    positions = tokens_ref.shape[0]
    first = lax.broadcasted_iota(jnp.int32, (positions, positions), 0)
    second = lax.broadcasted_iota(jnp.int32, (positions, positions), 1)
    live = jnp.broadcast_to(survive_ref[...].reshape(1, positions), (8, positions)).astype(f32)
    upper = (first <= second).astype(f32).astype(bf16)
    rank = jnp.dot(live.astype(bf16), upper, preferred_element_type=f32)
    target = jnp.where(live > 0.5, rank - 1.0, -1.0)
    chosen_ref[...] = (first == target[:1].astype(jnp.int32)).astype(f32).astype(bf16)
    home = jnp.transpose(target)[:, :1].astype(jnp.int32)
    back_ref[...] = (second == home).astype(f32).astype(bf16)
    count_ref[0, 0] = jnp.max(rank).astype(jnp.int32)
    gain = gain_ref[...].reshape(1, gain_ref.shape[0])
    rows = 128 if positions % 128 == 0 else positions
    for low in range(0, positions, rows):
        part = tokens_ref[low : low + rows, :].astype(f32)
        normed_ref[low : low + rows, :] = layer_norm(part, gain).astype(bf16)


def project_body(place_ref, *refs, steps, groups, first, joined):
    refs = list(refs)
    result_ref = refs.pop()
    weight_ref, gain_ref = refs[:2]
    if first:
        survive_ref, tokens_ref, norm_gain_ref = refs[2:5]
        outs, (normed_ref, chosen_ref, back_ref, count_ref) = refs[5:-4], refs[-4:]

        @pl.when(pl.program_id(0) == 0)
        def _():
            prepare(
                survive_ref, tokens_ref, norm_gain_ref, normed_ref, chosen_ref, back_ref, count_ref
            )

    else:
        (count_ref, normed_ref, chosen_ref), outs = refs[2:5], refs[5:]
    rows = normed_ref.shape[0]
    size = gain_ref.shape[2]
    plane = place_ref[0]
    for step, (kind, chunk, target, row, low) in enumerate(steps):

        @pl.when(pl.program_id(0) == step)
        def _():
            result = jnp.dot(normed_ref[...], weight_ref[0], preferred_element_type=f32)
            for g in range(groups):
                part = result[:, g * size : (g + 1) * size]
                if kind != 2:
                    gain = gain_ref[chunk * groups + g, kind : kind + 1, :]
                    if kind == 0:
                        gain = gain * (1.0 / math.sqrt(size))
                    part = layer_norm(part, gain)
                result_ref[:, g * size : (g + 1) * size] = part.astype(bf16)
            packed = jnp.dot(chosen_ref[...], result_ref[...], preferred_element_type=f32)
            if kind == 1:
                line = lax.broadcasted_iota(jnp.int32, (rows, groups * size), 0)
                packed = jnp.where(line < count_ref[0, 0], packed, dead_mark)
            result_ref[...] = packed.astype(bf16)
            for k in range(groups):
                if joined and kind == 0:
                    outs[-1][k, row] = result_ref[:, k * size : (k + 1) * size]
                else:
                    start = pl.multiple_of(lax.bitwise_xor(plane, k) * size, size)
                    found = result_ref[:, pl.ds(start, size)]
                    outs[target * groups + k][row, :, low : low + size] = found


def project(place, prepared, weights, gains, sets, groups, first=None, joined=False):
    size = gains.shape[2]
    width = weights.shape[1]
    columns = groups * size
    fixed = lambda t, place: (0, 0)
    line = lambda t, place: (0,)
    smem = pl.BlockSpec(memory_space=pltpu.SMEM)
    rows = (first or prepared)[1].shape[0]
    square = pl.BlockSpec((rows, rows), fixed)
    whole = pl.BlockSpec((rows, width), fixed)
    steps = [
        (kind, chunk, target, row, i * size)
        for target, (kinds, which) in enumerate(sets)
        for row, chunk in enumerate(which)
        for i, kind in enumerate(kinds)
    ]

    def weight_index(t, place):
        kind, chunk = steps[0][:2]
        for step, found in enumerate(steps):
            kind = jnp.where(t == step, found[0], kind)
            chunk = jnp.where(t == step, found[1], chunk)
        return (kind, 0, chunk)

    shapes = [
        (len(which), rows, len(kinds) * size) for kinds, which in sets for _ in range(groups)
    ]
    if joined:
        shapes = shapes[:-groups] + [(groups, len(sets[-1][1]), rows, size)]
    out_specs = [
        pl.BlockSpec(shape, lambda t, place, zeros=(0,) * len(shape): zeros) for shape in shapes
    ]
    out_shape = [jax.ShapeDtypeStruct(shape, bf16) for shape in shapes]
    if first:
        in_specs = [pl.BlockSpec((rows,), line), whole, pl.BlockSpec((width,), line)]
        out_specs += [whole, square, square, smem]
        out_shape += [
            jax.ShapeDtypeStruct((rows, width), bf16),
            jax.ShapeDtypeStruct((rows, rows), bf16),
            jax.ShapeDtypeStruct((rows, rows), bf16),
            jax.ShapeDtypeStruct((1, 1), jnp.int32),
        ]
    else:
        in_specs = [smem, whole, square]
    found = pl.pallas_call(
        functools.partial(
            project_body, steps=steps, groups=groups, first=first is not None, joined=joined
        ),
        grid_spec=pltpu.PrefetchScalarGridSpec(
            num_scalar_prefetch=1,
            grid=(len(steps),),
            in_specs=[
                pl.BlockSpec((1, width, columns), weight_index),
                pl.BlockSpec(gains.shape, lambda t, place: (0, 0, 0)),
            ]
            + in_specs,
            out_specs=out_specs,
            scratch_shapes=[pltpu.VMEM((rows, columns), bf16)],
        ),
        out_shape=out_shape,
        compiler_params=params,
        cost_estimate=cost(
            2 * rows * width * len(steps) * columns,
            2 * width * len(steps) * columns + 2 * rows * width,
        ),
        name="project",
    )(place, weights, gains, *(first or prepared))
    if joined:
        blocks = [found[i * groups : (i + 1) * groups] for i in range(len(sets) - 1)]
        return blocks, found[-1]
    blocks = [found[i * groups : (i + 1) * groups] for i in range(len(sets))]
    return blocks, found[len(sets) * groups :]


def attend_body(place_ref, *refs, groups, asked, joined, ordered, low_lane, key_room, query_rows, key_cols):
    outs = 1 if ordered else groups
    query_refs, sources, out_refs = refs[:asked], refs[asked : -4 - outs], refs[-4 - outs : -4]
    keys, values, queries, results = refs[-4:]
    rows, size = out_refs[0].shape[1:]
    plane = place_ref[0]
    blocks = [(source, k) for source in sources for k in range(groups)]
    piece = 128 if rows % 128 == 0 else rows
    align = lambda count: pl.multiple_of((count + 15) // 16 * 16, 16)
    line = lax.broadcasted_iota(jnp.int32, (piece, size), 0)

    found = []
    for source, block in blocks:
        live = (source[block, :, :size].astype(f32) < dead_limit).astype(f32)
        found.append(jnp.max(jnp.sum(live, axis=0, keepdims=True)).astype(jnp.int32))

    offset = jnp.int32(0)
    for (source, block), count in zip(blocks, found):
        for part in range(rows // piece):

            @pl.when(part * piece < count)
            def _():
                here = pl.ds(pl.multiple_of(offset + part * piece, 16), piece)
                there = pl.ds(part * piece, piece)
                live = line + part * piece < count
                key = jnp.where(live, source[block, there, :size].astype(f32), 0.0)
                keys[here, :] = key.astype(bf16)
                values[here, :size] = source[block, there, size:]
                values[here, size:] = live.astype(f32).astype(bf16)

        offset = pl.multiple_of(offset + align(count), 16)

    def clear(step, carry):
        here = pl.ds(pl.multiple_of(offset + step * 16, 16), 16)
        keys[here, :] = jnp.zeros((16, size), bf16)
        values[here, :] = jnp.zeros((16, 2 * size), bf16)
        return carry

    lax.fori_loop(0, (key_room - offset) // 16, clear, 0)

    mine = found[:groups]
    starts = []
    start = jnp.int32(0)
    for k in range(groups):
        starts.append(start)
        for part in range(rows // piece):

            @pl.when(part * piece < mine[k])
            def _():
                here = pl.ds(pl.multiple_of(start + part * piece, 16), piece)
                there = pl.ds(part * piece, piece)
                if joined:
                    found = query_refs[0][lax.bitwise_xor(plane, k), 0, there, :]
                else:
                    found = query_refs[k][0, there, low_lane : low_lane + size]
                queries[here, :] = found

        start = pl.multiple_of(start + align(mine[k]), 16)

    def one_tile(tile, carry):
        here = pl.ds(pl.multiple_of(tile * query_rows, query_rows), query_rows)
        query = queries[here, :]
        total = jnp.zeros((query_rows, 2 * size), f32)
        for low in range(0, key_room, key_cols):
            high = min(low + key_cols, key_room)
            scores = lax.dot_general(
                query, keys[low:high, :], (((1,), (1,)), ((), ())), preferred_element_type=f32
            )
            weights = jnp.exp(scores).astype(bf16)
            total += jnp.dot(weights, values[low:high, :], preferred_element_type=f32)
        results[here, :] = (total[:, :size] / total[:, size:]).astype(bf16)
        return carry

    lax.fori_loop(0, (start + query_rows - 1) // query_rows, one_tile, 0)

    for k in range(groups):
        for part in range(rows // piece):
            here = pl.ds(pl.multiple_of(starts[k] + part * piece, 16), piece)
            live = line + part * piece < mine[k]
            kept = jnp.where(live, results[here, :].astype(f32), 0.0).astype(bf16)
            block = lax.bitwise_xor(plane, k) if ordered else 0
            out_refs[0 if ordered else k][block, part * piece : (part + 1) * piece, :] = kept


def attend(place, queries, which, low_lane, keyvals, shards, ordered):
    groups = keyvals[0].shape[0]
    joined = queries[0].ndim == 4
    rows = keyvals[0].shape[1]
    size = keyvals[0].shape[2] // 2
    running = shards * rows // 2
    key_room = -(-(running + 16 * shards) // 256) * 256
    query_rows = 256
    query_room = -(-groups * rows // query_rows) * query_rows + rows
    if joined:
        query_block = pl.BlockSpec((groups, 1, rows, size), lambda i, place: (0, which, 0, 0))
    else:
        query_block = pl.BlockSpec((1,) + queries[0].shape[1:], lambda i, place: (which, 0, 0))
    outs, wide = (1, groups) if ordered else (groups, 1)
    return pl.pallas_call(
        functools.partial(
            attend_body,
            groups=groups,
            asked=len(queries),
            joined=joined,
            ordered=ordered,
            low_lane=low_lane,
            key_room=key_room,
            query_rows=query_rows,
            key_cols=256,
        ),
        grid_spec=pltpu.PrefetchScalarGridSpec(
            num_scalar_prefetch=1,
            grid=(1,),
            in_specs=[query_block] * len(queries)
            + [pl.BlockSpec(keyvals[0].shape, lambda i, place: (0, 0, 0))] * len(keyvals),
            out_specs=[pl.BlockSpec((wide, rows, size), lambda i, place: (0, 0, 0))] * outs,
            scratch_shapes=[
                pltpu.VMEM((key_room + rows, size), bf16),
                pltpu.VMEM((key_room + rows, 2 * size), bf16),
                pltpu.VMEM((query_room, size), bf16),
                pltpu.VMEM((query_room, size), bf16),
            ],
        ),
        out_shape=[jax.ShapeDtypeStruct((wide, rows, size), bf16)] * outs,
        compiler_params=params,
        cost_estimate=cost(
            8 * groups * rows // 2 * running * size,
            4 * shards * rows * size,
            groups * rows // 2 * running,
        ),
        name="attend",
    )(place, *queries, *keyvals)


def finish_body(place_ref, *refs, ordered):
    chunks = len(ordered)
    attended_refs, weight_ref, out_ref, wide_ref = refs[:chunks], *refs[chunks:]

    @pl.when(pl.program_id(0) == 0)
    def _():
        for i, ref in enumerate(attended_refs):
            groups, _, size = ref.shape
            for g in range(groups):
                if ordered[i]:
                    start = (i * groups + g) * size
                else:
                    head = i * groups + lax.bitwise_xor(place_ref[0], g)
                    start = pl.multiple_of(head * size, size)
                wide_ref[:, pl.ds(start, size)] = ref[g]

    total = jnp.dot(wide_ref[...], weight_ref[...], preferred_element_type=f32)
    out_ref[...] = total.astype(out_ref.dtype)


def finish(place, attended, ordered, w_out, mask, kind):
    groups, rows, size = attended[0].shape
    depth = w_out.shape[0]
    out_width = w_out.shape[1] // lax.axis_size("head")
    parts = 4 if out_width % 512 == 0 else 1
    tile = out_width // parts
    column = lambda i, place: (0, lax.bitwise_xor(place[2], mask) * parts + i)
    return pl.pallas_call(
        functools.partial(finish_body, ordered=ordered),
        grid_spec=pltpu.PrefetchScalarGridSpec(
            num_scalar_prefetch=1,
            grid=(parts,),
            in_specs=[pl.BlockSpec((groups, rows, size), lambda i, place: (0, 0, 0))] * len(attended)
            + [pl.BlockSpec((depth, tile), column)],
            out_specs=pl.BlockSpec((rows, tile), lambda i, place: (0, i)),
            scratch_shapes=[pltpu.VMEM((rows, depth), bf16)],
        ),
        out_shape=jax.ShapeDtypeStruct((rows, out_width), kind),
        compiler_params=params,
        cost_estimate=cost(2 * rows * depth * out_width, 2 * depth * out_width + 4 * rows * out_width),
        name="finish",
    )(place, *attended, w_out)


def close_body(back_ref, mine_ref, *refs):
    out_ref = refs[-1]
    total = mine_ref[...].astype(f32)
    for ref in refs[:-1]:
        total += ref[...].astype(f32)
    rounded = total.astype(bf16)
    out_ref[...] = jnp.dot(back_ref[...], rounded, preferred_element_type=f32).astype(bf16)


def close(back, mine, others):
    rows, width = mine.shape
    parts = 4 if width % 512 == 0 else 1
    tile = pl.BlockSpec((rows, width // parts), lambda i: (0, i))
    return pl.pallas_call(
        close_body,
        grid=(parts,),
        in_specs=[pl.BlockSpec((rows, rows), lambda i: (0, 0))] + [tile] * (1 + len(others)),
        out_specs=tile,
        out_shape=jax.ShapeDtypeStruct((rows, width), bf16),
        compiler_params=params,
        cost_estimate=cost(2 * rows * rows * width, 10 * rows * width),
        name="close",
    )(back, mine, *others)


def per_device(tokens, survive, norm_gain, w_qkv, qk_gain, w_out):
    heads, size = qk_gain.shape[1:]
    shards, head_shards = lax.axis_size("seq"), lax.axis_size("head")
    groups = math.gcd(heads & -heads, shards & -shards)
    ring = shards // groups
    chunks = heads // groups
    me, side = lax.axis_index("seq"), lax.axis_index("head")
    place = jnp.stack([me // ring, me % ring, side]).astype(jnp.int32)
    planes = [[i + ring * g for g in range(groups)] for i in range(ring)]

    def swap(blocks):
        return [blocks[0]] + [flip(blocks[k], "seq", k * ring) for k in range(1, groups)]

    def stack(blocks):
        return jnp.concatenate([block[:, :, : 2 * size] for block in blocks])

    def everywhere(stacked, gate):
        found = {0: stacked}
        mask = ring // 2
        while mask:
            for known in list(found):
                source = found[known]
                if gate is not None and mask < ring // 2:
                    source = chain(source, gate)
                found[known | mask] = flip(source, "seq", mask)
            mask //= 2
        return [found[mask] for mask in range(ring)]

    def send_back(blocks):
        if groups == 1:
            return blocks
        return lax.all_to_all(
            blocks, "seq", split_axis=0, concat_axis=0, axis_index_groups=planes, tiled=True
        )

    weights = jnp.transpose(w_qkv, (1, 0, 2))
    gains = jnp.transpose(qk_gain, (1, 0, 2))

    def later(values, *earlier):
        return jnp.maximum(chain(values, *earlier), 0)

    def first(blocks):
        return blocks[min(1, groups - 1)]

    def send(blocks, *earlier):
        return swap(list(chain(tuple(blocks), *earlier)) if earlier else blocks)

    operands = (survive, tokens, norm_gain)
    sets = [((1, 2, 0), (0,))]
    (blocks,), rest = project(place, None, weights, gains, sets, groups, operands)
    normed, chosen, back, count = rest
    arrived = [swap(blocks)]

    rest, asked, hops = range(1, chunks), None, []
    if chunks > 1:
        prepared = (count, chain(normed, first(arrived[0])), chosen)
        sets = [((1, 2), (chunk,)) for chunk in rest] + [((0,), tuple(rest))]
        made, wanted = project(place, prepared, weights, gains, sets, groups, joined=True)
        stacks = [stack(list(chain(tuple(arrived[0]), made[0][0])))]
        arrived.append(send(made[0]))
        for blocks in made[1:]:
            arrived.append(send(blocks, first(arrived[-1])))
        gate = stack(arrived[1])
        stacks.append(gate)
        asked = [send_back(chain(wanted, gate))]
        hops = []
    else:
        gate, stacks = None, [stack(arrived[0])]

    attended, returned = [], []
    query, low_lane = arrived[0], 2 * size
    for chunk in range(chunks):
        final = chunk == chunks - 1
        keyvals = everywhere(stacks[chunk], gate)
        before = [stacks[-1]] + attended[-1:] + (hops if chunk else []) + (returned[:1] if final else [])
        ready = later(place, *query[1 if chunk == 0 else 0 :], *before)
        row = max(chunk - 1, 0)
        found = attend(ready, query, row, low_lane, keyvals, shards, not final)
        attended.append(found[0])
        if chunk == 0:
            stacks += [stack(list(chain(tuple(blocks), found[0]))) for blocks in arrived[2:]]
            if chunks > 1 and ring > 1:
                hops = [flip(stacks[-1], "seq", ring // 2)]
        returned.append(jnp.concatenate(swap(found)) if final else send_back(found[0]))
        if not final:
            query, low_lane, gate = asked, 0, None
    ordered = (True,) * (chunks - 1) + (False,)
    final = functools.partial(finish, place, returned, ordered, w_out)
    sent = [final(mask, bf16) for mask in range(1, head_shards)]
    others = [flip(part, "head", mask) for mask, part in enumerate(sent, 1)]
    returned[0] = chain(returned[0], *sent)
    return close(back, final(0, bf16), others)


def solution(mesh):
    placed = (
        P("seq", None),
        P("seq"),
        P(),
        P(None, None, "head"),
        P(None, "head", None),
        P("head", None),
    )
    return jax.shard_map(
        per_device, mesh=mesh, in_specs=placed, out_specs=P("seq", "head"), check_vma=False
    )
```

```python
import functools
import math

import jax
import jax.numpy as jnp
from jax import lax
from jax.experimental import pallas as pl
from jax.experimental.pallas import tpu as pltpu
from jax.sharding import PartitionSpec as P

epsilon = 1e-06
dead_mark = 1e30
dead_limit = 1e15
mib = 1 << 20
f32 = jnp.float32
bf16 = jnp.bfloat16
params = pltpu.CompilerParams(vmem_limit_bytes=60 * mib)


def cost(flops, bytes_accessed, exps=0):
    return pl.CostEstimate(
        flops=int(flops), bytes_accessed=int(bytes_accessed), transcendentals=int(exps)
    )


def flip(values, axis, mask):
    size = lax.axis_size(axis)
    return lax.ppermute(values, axis, [(i, i ^ mask) for i in range(size)])


def chain(values, *earlier):
    return lax.optimization_barrier((values, earlier))[0]


def layer_norm(values, gain):
    center = values - jnp.mean(values, axis=-1, keepdims=True)
    spread = jnp.mean(center * center, axis=-1, keepdims=True)
    return center * lax.rsqrt(spread + epsilon) * gain


def prepare(survive_ref, tokens_ref, gain_ref, normed_ref, chosen_ref, back_ref, count_ref):
    positions = tokens_ref.shape[0]
    first = lax.broadcasted_iota(jnp.int32, (positions, positions), 0)
    second = lax.broadcasted_iota(jnp.int32, (positions, positions), 1)
    live = jnp.broadcast_to(survive_ref[...].reshape(1, positions), (8, positions)).astype(f32)
    upper = (first <= second).astype(f32).astype(bf16)
    rank = jnp.dot(live.astype(bf16), upper, preferred_element_type=f32)
    target = jnp.where(live > 0.5, rank - 1.0, -1.0)
    chosen_ref[...] = (first == target[:1].astype(jnp.int32)).astype(f32).astype(bf16)
    home = jnp.transpose(target)[:, :1].astype(jnp.int32)
    back_ref[...] = (second == home).astype(f32).astype(bf16)
    count_ref[0, 0] = jnp.max(rank).astype(jnp.int32)
    gain = gain_ref[...].reshape(1, gain_ref.shape[0])
    rows = 128 if positions % 128 == 0 else positions
    for low in range(0, positions, rows):
        part = tokens_ref[low : low + rows, :].astype(f32)
        normed_ref[low : low + rows, :] = layer_norm(part, gain).astype(bf16)


def project_body(place_ref, *refs, steps, groups, first, joined):
    refs = list(refs)
    result_ref = refs.pop()
    weight_ref, gain_ref = refs[:2]
    if first:
        survive_ref, tokens_ref, norm_gain_ref = refs[2:5]
        outs, (normed_ref, chosen_ref, back_ref, count_ref) = refs[5:-4], refs[-4:]

        @pl.when(pl.program_id(0) == 0)
        def _():
            prepare(
                survive_ref, tokens_ref, norm_gain_ref, normed_ref, chosen_ref, back_ref, count_ref
            )

    else:
        (count_ref, normed_ref, chosen_ref), outs = refs[2:5], refs[5:]
    rows = normed_ref.shape[0]
    size = gain_ref.shape[2]
    plane = place_ref[0]
    for step, (kind, chunk, target, row, low) in enumerate(steps):

        @pl.when(pl.program_id(0) == step)
        def _():
            result = jnp.dot(normed_ref[...], weight_ref[0], preferred_element_type=f32)
            for g in range(groups):
                part = result[:, g * size : (g + 1) * size]
                if kind != 2:
                    gain = gain_ref[chunk * groups + g, kind : kind + 1, :]
                    if kind == 0:
                        gain = gain * (1.0 / math.sqrt(size))
                    part = layer_norm(part, gain)
                result_ref[:, g * size : (g + 1) * size] = part.astype(bf16)
            packed = jnp.dot(chosen_ref[...], result_ref[...], preferred_element_type=f32)
            if kind == 1:
                line = lax.broadcasted_iota(jnp.int32, (rows, groups * size), 0)
                packed = jnp.where(line < count_ref[0, 0], packed, dead_mark)
            result_ref[...] = packed.astype(bf16)
            for k in range(groups):
                if joined:
                    outs[k // groups][k, row] = result_ref[:, k * size : (k + 1) * size]
                else:
                    start = pl.multiple_of(lax.bitwise_xor(plane, k) * size, size)
                    found = result_ref[:, pl.ds(start, size)]
                    outs[target * groups + k][row, :, low : low + size] = found


def project(place, prepared, weights, gains, sets, groups, first=None, joined=False):
    size = gains.shape[2]
    width = weights.shape[1]
    columns = groups * size
    fixed = lambda t, place: (0, 0)
    line = lambda t, place: (0,)
    smem = pl.BlockSpec(memory_space=pltpu.SMEM)
    rows = (first or prepared)[1].shape[0]
    square = pl.BlockSpec((rows, rows), fixed)
    whole = pl.BlockSpec((rows, width), fixed)
    steps = [
        (kind, chunk, target, row, i * size)
        for target, (kinds, which) in enumerate(sets)
        for row, chunk in enumerate(which)
        for i, kind in enumerate(kinds)
    ]

    def weight_index(t, place):
        kind, chunk = steps[0][:2]
        for step, found in enumerate(steps):
            kind = jnp.where(t == step, found[0], kind)
            chunk = jnp.where(t == step, found[1], chunk)
        return (kind, 0, chunk)

    shapes = [
        (len(which), rows, len(kinds) * size) for kinds, which in sets for _ in range(groups)
    ]
    if joined:
        shapes = [(groups, len(sets[0][1]), rows, size)]
    out_specs = [
        pl.BlockSpec(shape, lambda t, place, zeros=(0,) * len(shape): zeros) for shape in shapes
    ]
    out_shape = [jax.ShapeDtypeStruct(shape, bf16) for shape in shapes]
    if first:
        in_specs = [pl.BlockSpec((rows,), line), whole, pl.BlockSpec((width,), line)]
        out_specs += [whole, square, square, smem]
        out_shape += [
            jax.ShapeDtypeStruct((rows, width), bf16),
            jax.ShapeDtypeStruct((rows, rows), bf16),
            jax.ShapeDtypeStruct((rows, rows), bf16),
            jax.ShapeDtypeStruct((1, 1), jnp.int32),
        ]
    else:
        in_specs = [smem, whole, square]
    found = pl.pallas_call(
        functools.partial(
            project_body, steps=steps, groups=groups, first=first is not None, joined=joined
        ),
        grid_spec=pltpu.PrefetchScalarGridSpec(
            num_scalar_prefetch=1,
            grid=(len(steps),),
            in_specs=[
                pl.BlockSpec((1, width, columns), weight_index),
                pl.BlockSpec(gains.shape, lambda t, place: (0, 0, 0)),
            ]
            + in_specs,
            out_specs=out_specs,
            scratch_shapes=[pltpu.VMEM((rows, columns), bf16)],
        ),
        out_shape=out_shape,
        compiler_params=params,
        cost_estimate=cost(
            2 * rows * width * len(steps) * columns,
            2 * width * len(steps) * columns + 2 * rows * width,
        ),
        name="project",
    )(place, weights, gains, *(first or prepared))
    if joined:
        return found[0], []
    blocks = [found[i * groups : (i + 1) * groups] for i in range(len(sets))]
    return blocks, found[len(sets) * groups :]


def attend_body(place_ref, *refs, groups, asked, joined, ordered, low_lane, key_room, query_rows, key_cols):
    outs = 1 if ordered else groups
    query_refs, sources, out_refs = refs[:asked], refs[asked : -4 - outs], refs[-4 - outs : -4]
    keys, values, queries, results = refs[-4:]
    rows, size = out_refs[0].shape[1:]
    plane = place_ref[0]
    blocks = [(source, k) for source in sources for k in range(groups)]
    piece = 128 if rows % 128 == 0 else rows
    align = lambda count: pl.multiple_of((count + 15) // 16 * 16, 16)
    line = lax.broadcasted_iota(jnp.int32, (piece, size), 0)

    found = []
    for source, block in blocks:
        live = (source[block, :, :size].astype(f32) < dead_limit).astype(f32)
        found.append(jnp.max(jnp.sum(live, axis=0, keepdims=True)).astype(jnp.int32))

    offset = jnp.int32(0)
    for (source, block), count in zip(blocks, found):
        for part in range(rows // piece):

            @pl.when(part * piece < count)
            def _():
                here = pl.ds(pl.multiple_of(offset + part * piece, 16), piece)
                there = pl.ds(part * piece, piece)
                live = line + part * piece < count
                key = jnp.where(live, source[block, there, :size].astype(f32), 0.0)
                keys[here, :] = key.astype(bf16)
                values[here, :size] = source[block, there, size:]
                values[here, size:] = live.astype(f32).astype(bf16)

        offset = pl.multiple_of(offset + align(count), 16)

    def clear(step, carry):
        here = pl.ds(pl.multiple_of(offset + step * 16, 16), 16)
        keys[here, :] = jnp.zeros((16, size), bf16)
        values[here, :] = jnp.zeros((16, 2 * size), bf16)
        return carry

    lax.fori_loop(0, (key_room - offset) // 16, clear, 0)

    mine = found[:groups]
    starts = []
    start = jnp.int32(0)
    for k in range(groups):
        starts.append(start)
        for part in range(rows // piece):

            @pl.when(part * piece < mine[k])
            def _():
                here = pl.ds(pl.multiple_of(start + part * piece, 16), piece)
                there = pl.ds(part * piece, piece)
                if joined:
                    found = query_refs[0][lax.bitwise_xor(plane, k), 0, there, :]
                else:
                    found = query_refs[k][0, there, low_lane : low_lane + size]
                queries[here, :] = found

        start = pl.multiple_of(start + align(mine[k]), 16)

    def one_tile(tile, carry):
        here = pl.ds(pl.multiple_of(tile * query_rows, query_rows), query_rows)
        query = queries[here, :]
        total = jnp.zeros((query_rows, 2 * size), f32)
        for low in range(0, key_room, key_cols):
            high = min(low + key_cols, key_room)
            scores = lax.dot_general(
                query, keys[low:high, :], (((1,), (1,)), ((), ())), preferred_element_type=f32
            )
            weights = jnp.exp(scores).astype(bf16)
            total += jnp.dot(weights, values[low:high, :], preferred_element_type=f32)
        results[here, :] = (total[:, :size] / total[:, size:]).astype(bf16)
        return carry

    lax.fori_loop(0, (start + query_rows - 1) // query_rows, one_tile, 0)

    for k in range(groups):
        for part in range(rows // piece):
            here = pl.ds(pl.multiple_of(starts[k] + part * piece, 16), piece)
            live = line + part * piece < mine[k]
            kept = jnp.where(live, results[here, :].astype(f32), 0.0).astype(bf16)
            block = lax.bitwise_xor(plane, k) if ordered else 0
            out_refs[0 if ordered else k][block, part * piece : (part + 1) * piece, :] = kept


def attend(place, queries, which, low_lane, keyvals, shards, ordered):
    groups = keyvals[0].shape[0]
    joined = queries[0].ndim == 4
    rows = keyvals[0].shape[1]
    size = keyvals[0].shape[2] // 2
    running = shards * rows // 2
    key_room = -(-(running + 16 * shards) // 256) * 256
    query_rows = 256
    query_room = -(-groups * rows // query_rows) * query_rows + rows
    if joined:
        query_block = pl.BlockSpec((groups, 1, rows, size), lambda i, place: (0, which, 0, 0))
    else:
        query_block = pl.BlockSpec((1,) + queries[0].shape[1:], lambda i, place: (which, 0, 0))
    outs, wide = (1, groups) if ordered else (groups, 1)
    return pl.pallas_call(
        functools.partial(
            attend_body,
            groups=groups,
            asked=len(queries),
            joined=joined,
            ordered=ordered,
            low_lane=low_lane,
            key_room=key_room,
            query_rows=query_rows,
            key_cols=256,
        ),
        grid_spec=pltpu.PrefetchScalarGridSpec(
            num_scalar_prefetch=1,
            grid=(1,),
            in_specs=[query_block] * len(queries)
            + [pl.BlockSpec(keyvals[0].shape, lambda i, place: (0, 0, 0))] * len(keyvals),
            out_specs=[pl.BlockSpec((wide, rows, size), lambda i, place: (0, 0, 0))] * outs,
            scratch_shapes=[
                pltpu.VMEM((key_room + rows, size), bf16),
                pltpu.VMEM((key_room + rows, 2 * size), bf16),
                pltpu.VMEM((query_room, size), bf16),
                pltpu.VMEM((query_room, size), bf16),
            ],
        ),
        out_shape=[jax.ShapeDtypeStruct((wide, rows, size), bf16)] * outs,
        compiler_params=params,
        cost_estimate=cost(
            8 * groups * rows // 2 * running * size,
            4 * shards * rows * size,
            groups * rows // 2 * running,
        ),
        name="attend",
    )(place, *queries, *keyvals)


def finish_body(place_ref, *refs, ordered):
    chunks = len(ordered)
    attended_refs, weight_ref, out_ref, wide_ref = refs[:chunks], *refs[chunks:]

    @pl.when(pl.program_id(0) == 0)
    def _():
        for i, ref in enumerate(attended_refs):
            groups, _, size = ref.shape
            for g in range(groups):
                if ordered[i]:
                    start = (i * groups + g) * size
                else:
                    head = i * groups + lax.bitwise_xor(place_ref[0], g)
                    start = pl.multiple_of(head * size, size)
                wide_ref[:, pl.ds(start, size)] = ref[g]

    total = jnp.dot(wide_ref[...], weight_ref[...], preferred_element_type=f32)
    out_ref[...] = total.astype(out_ref.dtype)


def finish(place, attended, ordered, w_out, mask, kind):
    groups, rows, size = attended[0].shape
    depth = w_out.shape[0]
    out_width = w_out.shape[1] // lax.axis_size("head")
    parts = 4 if out_width % 512 == 0 else 1
    tile = out_width // parts
    column = lambda i, place: (0, lax.bitwise_xor(place[2], mask) * parts + i)
    return pl.pallas_call(
        functools.partial(finish_body, ordered=ordered),
        grid_spec=pltpu.PrefetchScalarGridSpec(
            num_scalar_prefetch=1,
            grid=(parts,),
            in_specs=[pl.BlockSpec((groups, rows, size), lambda i, place: (0, 0, 0))] * len(attended)
            + [pl.BlockSpec((depth, tile), column)],
            out_specs=pl.BlockSpec((rows, tile), lambda i, place: (0, i)),
            scratch_shapes=[pltpu.VMEM((rows, depth), bf16)],
        ),
        out_shape=jax.ShapeDtypeStruct((rows, out_width), kind),
        compiler_params=params,
        cost_estimate=cost(2 * rows * depth * out_width, 2 * depth * out_width + 4 * rows * out_width),
        name="finish",
    )(place, *attended, w_out)


def close_body(back_ref, mine_ref, *refs):
    out_ref = refs[-1]
    total = mine_ref[...].astype(f32)
    for ref in refs[:-1]:
        total += ref[...].astype(f32)
    rounded = total.astype(bf16)
    out_ref[...] = jnp.dot(back_ref[...], rounded, preferred_element_type=f32).astype(bf16)


def close(back, mine, others):
    rows, width = mine.shape
    parts = 4 if width % 512 == 0 else 1
    tile = pl.BlockSpec((rows, width // parts), lambda i: (0, i))
    return pl.pallas_call(
        close_body,
        grid=(parts,),
        in_specs=[pl.BlockSpec((rows, rows), lambda i: (0, 0))] + [tile] * (1 + len(others)),
        out_specs=tile,
        out_shape=jax.ShapeDtypeStruct((rows, width), bf16),
        compiler_params=params,
        cost_estimate=cost(2 * rows * rows * width, 10 * rows * width),
        name="close",
    )(back, mine, *others)


def per_device(tokens, survive, norm_gain, w_qkv, qk_gain, w_out):
    heads, size = qk_gain.shape[1:]
    shards, head_shards = lax.axis_size("seq"), lax.axis_size("head")
    groups = math.gcd(heads & -heads, shards & -shards)
    ring = shards // groups
    chunks = heads // groups
    me, side = lax.axis_index("seq"), lax.axis_index("head")
    place = jnp.stack([me // ring, me % ring, side]).astype(jnp.int32)
    planes = [[i + ring * g for g in range(groups)] for i in range(ring)]

    def swap(blocks):
        return [blocks[0]] + [flip(blocks[k], "seq", k * ring) for k in range(1, groups)]

    def stack(blocks):
        return jnp.concatenate([block[:, :, : 2 * size] for block in blocks])

    def everywhere(stacked, gate):
        found = {0: stacked}
        mask = ring // 2
        while mask:
            for known in list(found):
                source = found[known]
                if gate is not None and mask < ring // 2:
                    source = chain(source, gate)
                found[known | mask] = flip(source, "seq", mask)
            mask //= 2
        return [found[mask] for mask in range(ring)]

    def send_back(blocks):
        if groups == 1:
            return blocks
        return lax.all_to_all(
            blocks, "seq", split_axis=0, concat_axis=0, axis_index_groups=planes, tiled=True
        )

    weights = jnp.transpose(w_qkv, (1, 0, 2))
    gains = jnp.transpose(qk_gain, (1, 0, 2))

    def later(values, *earlier):
        return jnp.maximum(chain(values, *earlier), 0)

    def first(blocks):
        return blocks[min(1, groups - 1)]

    def send(blocks, *earlier):
        return swap(list(chain(tuple(blocks), *earlier)) if earlier else blocks)

    operands = (survive, tokens, norm_gain)
    sets = [((1, 2, 0), (0,))]
    (blocks,), rest = project(place, None, weights, gains, sets, groups, operands)
    normed, chosen, back, count = rest
    arrived = [swap(blocks)]

    rest, asked, hops = range(1, chunks), None, []
    if chunks > 1:
        prepared = (count, chain(normed, first(arrived[0])), chosen)
        sets = [((1, 2), (chunk,)) for chunk in rest]
        made, _ = project(place, prepared, weights, gains, sets, groups)
        stacks = [stack(list(chain(tuple(arrived[0]), made[0][0])))]
        arrived.append(send(made[0]))
        for blocks in made[1:]:
            arrived.append(send(blocks, first(arrived[-1])))
        hop = flip(stacks[0], "seq", ring // 2) if ring > 1 else stacks[0]
        stacks.append(stack(arrived[1]))
        ready = later(count, hop, stacks[1])
        sets = [((0,), tuple(rest))]
        made, _ = project(
            place, (ready, normed, chosen), weights, gains, sets, groups, joined=True
        )
        gate = None
        stacks += [stack(list(chain(tuple(blocks), made))) for blocks in arrived[2:]]
        asked = [send_back(made)]
        hops = [flip(stacks[-1], "seq", ring // 2)] if ring > 1 else []
    else:
        gate, stacks = None, [stack(arrived[0])]

    attended, returned = [], []
    query, low_lane = arrived[0], 2 * size
    for chunk in range(chunks):
        final = chunk == chunks - 1
        keyvals = everywhere(stacks[chunk], gate)
        before = [stacks[-1]] + attended[-1:] + (hops if chunk else []) + (returned[:1] if final else [])
        ready = later(place, *query[1 if chunk == 0 else 0 :], *before)
        row = max(chunk - 1, 0)
        found = attend(ready, query, row, low_lane, keyvals, shards, not final)
        attended.append(found[0])
        returned.append(jnp.concatenate(swap(found)) if final else send_back(found[0]))
        if not final:
            query, low_lane, gate = asked, 0, None
    ordered = (True,) * (chunks - 1) + (False,)
    final = functools.partial(finish, place, returned, ordered, w_out)
    sent = [final(mask, bf16) for mask in range(1, head_shards)]
    others = [flip(part, "head", mask) for mask, part in enumerate(sent, 1)]
    returned[0] = chain(returned[0], *sent)
    return close(back, final(0, bf16), others)


def solution(mesh):
    placed = (
        P("seq", None),
        P("seq"),
        P(),
        P(None, None, "head"),
        P(None, "head", None),
        P("head", None),
    )
    return jax.shard_map(
        per_device, mesh=mesh, in_specs=placed, out_specs=P("seq", "head"), check_vma=False
    )
```

```python
import functools
import math

import jax
import jax.numpy as jnp
from jax import lax
from jax.experimental import pallas as pl
from jax.experimental.pallas import tpu as pltpu
from jax.sharding import PartitionSpec as P

epsilon = 1e-06
dead_mark = 1e30
dead_limit = 1e15
mib = 1 << 20
f32 = jnp.float32
bf16 = jnp.bfloat16
params = pltpu.CompilerParams(vmem_limit_bytes=60 * mib)


def cost(flops, bytes_accessed, exps=0):
    return pl.CostEstimate(
        flops=int(flops), bytes_accessed=int(bytes_accessed), transcendentals=int(exps)
    )


def flip(values, axis, mask):
    size = lax.axis_size(axis)
    return lax.ppermute(values, axis, [(i, i ^ mask) for i in range(size)])


def chain(values, *earlier):
    return lax.optimization_barrier((values, earlier))[0]


def layer_norm(values, gain):
    center = values - jnp.mean(values, axis=-1, keepdims=True)
    spread = jnp.mean(center * center, axis=-1, keepdims=True)
    return center * lax.rsqrt(spread + epsilon) * gain


def prepare(survive_ref, tokens_ref, gain_ref, normed_ref, chosen_ref, back_ref, count_ref):
    positions = tokens_ref.shape[0]
    first = lax.broadcasted_iota(jnp.int32, (positions, positions), 0)
    second = lax.broadcasted_iota(jnp.int32, (positions, positions), 1)
    live = jnp.broadcast_to(survive_ref[...].reshape(1, positions), (8, positions)).astype(f32)
    upper = (first <= second).astype(f32).astype(bf16)
    rank = jnp.dot(live.astype(bf16), upper, preferred_element_type=f32)
    target = jnp.where(live > 0.5, rank - 1.0, -1.0)
    chosen_ref[...] = (first == target[:1].astype(jnp.int32)).astype(f32).astype(bf16)
    home = jnp.transpose(target)[:, :1].astype(jnp.int32)
    back_ref[...] = (second == home).astype(f32).astype(bf16)
    count_ref[0, 0] = jnp.max(rank).astype(jnp.int32)
    gain = gain_ref[...].reshape(1, gain_ref.shape[0])
    rows = 128 if positions % 128 == 0 else positions
    for low in range(0, positions, rows):
        part = tokens_ref[low : low + rows, :].astype(f32)
        normed_ref[low : low + rows, :] = layer_norm(part, gain).astype(bf16)


def project_body(place_ref, *refs, steps, groups, first, joined):
    refs = list(refs)
    result_ref = refs.pop()
    weight_ref, gain_ref = refs[:2]
    if first:
        survive_ref, tokens_ref, norm_gain_ref = refs[2:5]
        outs, (normed_ref, chosen_ref, back_ref, count_ref) = refs[5:-4], refs[-4:]

        @pl.when(pl.program_id(0) == 0)
        def _():
            prepare(
                survive_ref, tokens_ref, norm_gain_ref, normed_ref, chosen_ref, back_ref, count_ref
            )

    else:
        (count_ref, normed_ref, chosen_ref), outs = refs[2:5], refs[5:]
    rows = normed_ref.shape[0]
    size = gain_ref.shape[2]
    plane = place_ref[0]
    for step, (kind, chunk, target, row, low) in enumerate(steps):

        @pl.when(pl.program_id(0) == step)
        def _():
            result = jnp.dot(normed_ref[...], weight_ref[0], preferred_element_type=f32)
            for g in range(groups):
                part = result[:, g * size : (g + 1) * size]
                if kind != 2:
                    gain = gain_ref[chunk * groups + g, kind : kind + 1, :]
                    if kind == 0:
                        gain = gain * (1.0 / math.sqrt(size))
                    part = layer_norm(part, gain)
                result_ref[:, g * size : (g + 1) * size] = part.astype(bf16)
            packed = jnp.dot(chosen_ref[...], result_ref[...], preferred_element_type=f32)
            if kind == 1:
                line = lax.broadcasted_iota(jnp.int32, (rows, groups * size), 0)
                packed = jnp.where(line < count_ref[0, 0], packed, dead_mark)
            result_ref[...] = packed.astype(bf16)
            for k in range(groups):
                if joined:
                    outs[k // groups][k, row] = result_ref[:, k * size : (k + 1) * size]
                else:
                    start = pl.multiple_of(lax.bitwise_xor(plane, k) * size, size)
                    found = result_ref[:, pl.ds(start, size)]
                    outs[target * groups + k][row, :, low : low + size] = found


def project(place, prepared, weights, gains, sets, groups, first=None, joined=False):
    size = gains.shape[2]
    width = weights.shape[1]
    columns = groups * size
    fixed = lambda t, place: (0, 0)
    line = lambda t, place: (0,)
    smem = pl.BlockSpec(memory_space=pltpu.SMEM)
    rows = (first or prepared)[1].shape[0]
    square = pl.BlockSpec((rows, rows), fixed)
    whole = pl.BlockSpec((rows, width), fixed)
    steps = [
        (kind, chunk, target, row, i * size)
        for target, (kinds, which) in enumerate(sets)
        for row, chunk in enumerate(which)
        for i, kind in enumerate(kinds)
    ]

    def weight_index(t, place):
        kind, chunk = steps[0][:2]
        for step, found in enumerate(steps):
            kind = jnp.where(t == step, found[0], kind)
            chunk = jnp.where(t == step, found[1], chunk)
        return (kind, 0, chunk)

    shapes = [
        (len(which), rows, len(kinds) * size) for kinds, which in sets for _ in range(groups)
    ]
    if joined:
        shapes = [(groups, len(sets[0][1]), rows, size)]
    out_specs = [
        pl.BlockSpec(shape, lambda t, place, zeros=(0,) * len(shape): zeros) for shape in shapes
    ]
    out_shape = [jax.ShapeDtypeStruct(shape, bf16) for shape in shapes]
    if first:
        in_specs = [pl.BlockSpec((rows,), line), whole, pl.BlockSpec((width,), line)]
        out_specs += [whole, square, square, smem]
        out_shape += [
            jax.ShapeDtypeStruct((rows, width), bf16),
            jax.ShapeDtypeStruct((rows, rows), bf16),
            jax.ShapeDtypeStruct((rows, rows), bf16),
            jax.ShapeDtypeStruct((1, 1), jnp.int32),
        ]
    else:
        in_specs = [smem, whole, square]
    found = pl.pallas_call(
        functools.partial(
            project_body, steps=steps, groups=groups, first=first is not None, joined=joined
        ),
        grid_spec=pltpu.PrefetchScalarGridSpec(
            num_scalar_prefetch=1,
            grid=(len(steps),),
            in_specs=[
                pl.BlockSpec((1, width, columns), weight_index),
                pl.BlockSpec(gains.shape, lambda t, place: (0, 0, 0)),
            ]
            + in_specs,
            out_specs=out_specs,
            scratch_shapes=[pltpu.VMEM((rows, columns), bf16)],
        ),
        out_shape=out_shape,
        compiler_params=params,
        cost_estimate=cost(
            2 * rows * width * len(steps) * columns,
            2 * width * len(steps) * columns + 2 * rows * width,
        ),
        name="project",
    )(place, weights, gains, *(first or prepared))
    if joined:
        return found[0], []
    blocks = [found[i * groups : (i + 1) * groups] for i in range(len(sets))]
    return blocks, found[len(sets) * groups :]


def attend_body(place_ref, *refs, groups, asked, joined, ordered, low_lane, key_room, query_rows, key_cols):
    outs = 1 if ordered else groups
    query_refs, sources, out_refs = refs[:asked], refs[asked : -4 - outs], refs[-4 - outs : -4]
    keys, values, queries, results = refs[-4:]
    rows, size = out_refs[0].shape[1:]
    plane = place_ref[0]
    blocks = [(source, k) for source in sources for k in range(groups)]
    piece = 128 if rows % 128 == 0 else rows
    align = lambda count: pl.multiple_of((count + 15) // 16 * 16, 16)
    line = lax.broadcasted_iota(jnp.int32, (piece, size), 0)

    found = []
    for source, block in blocks:
        live = (source[block, :, :size].astype(f32) < dead_limit).astype(f32)
        found.append(jnp.max(jnp.sum(live, axis=0, keepdims=True)).astype(jnp.int32))

    offset = jnp.int32(0)
    for (source, block), count in zip(blocks, found):
        for part in range(rows // piece):

            @pl.when(part * piece < count)
            def _():
                here = pl.ds(pl.multiple_of(offset + part * piece, 16), piece)
                there = pl.ds(part * piece, piece)
                live = line + part * piece < count
                key = jnp.where(live, source[block, there, :size].astype(f32), 0.0)
                keys[here, :] = key.astype(bf16)
                values[here, :size] = source[block, there, size:]
                values[here, size:] = live.astype(f32).astype(bf16)

        offset = pl.multiple_of(offset + align(count), 16)

    def clear(step, carry):
        here = pl.ds(pl.multiple_of(offset + step * 16, 16), 16)
        keys[here, :] = jnp.zeros((16, size), bf16)
        values[here, :] = jnp.zeros((16, 2 * size), bf16)
        return carry

    lax.fori_loop(0, (key_room - offset) // 16, clear, 0)

    mine = found[:groups]
    starts = []
    start = jnp.int32(0)
    for k in range(groups):
        starts.append(start)
        for part in range(rows // piece):

            @pl.when(part * piece < mine[k])
            def _():
                here = pl.ds(pl.multiple_of(start + part * piece, 16), piece)
                there = pl.ds(part * piece, piece)
                if joined:
                    found = query_refs[0][lax.bitwise_xor(plane, k), 0, there, :]
                else:
                    found = query_refs[k][0, there, low_lane : low_lane + size]
                queries[here, :] = found

        start = pl.multiple_of(start + align(mine[k]), 16)

    def one_tile(tile, carry):
        here = pl.ds(pl.multiple_of(tile * query_rows, query_rows), query_rows)
        query = queries[here, :]
        total = jnp.zeros((query_rows, 2 * size), f32)
        for low in range(0, key_room, key_cols):
            high = min(low + key_cols, key_room)
            scores = lax.dot_general(
                query, keys[low:high, :], (((1,), (1,)), ((), ())), preferred_element_type=f32
            )
            weights = jnp.exp(scores).astype(bf16)
            total += jnp.dot(weights, values[low:high, :], preferred_element_type=f32)
        results[here, :] = (total[:, :size] / total[:, size:]).astype(bf16)
        return carry

    lax.fori_loop(0, (start + query_rows - 1) // query_rows, one_tile, 0)

    for k in range(groups):
        for part in range(rows // piece):
            here = pl.ds(pl.multiple_of(starts[k] + part * piece, 16), piece)
            live = line + part * piece < mine[k]
            kept = jnp.where(live, results[here, :].astype(f32), 0.0).astype(bf16)
            block = lax.bitwise_xor(plane, k) if ordered else 0
            out_refs[0 if ordered else k][block, part * piece : (part + 1) * piece, :] = kept


def attend(place, queries, which, low_lane, keyvals, shards, ordered):
    groups = keyvals[0].shape[0]
    joined = queries[0].ndim == 4
    rows = keyvals[0].shape[1]
    size = keyvals[0].shape[2] // 2
    running = shards * rows // 2
    key_room = -(-(running + 16 * shards) // 256) * 256
    query_rows = 256
    query_room = -(-groups * rows // query_rows) * query_rows + rows
    if joined:
        query_block = pl.BlockSpec((groups, 1, rows, size), lambda i, place: (0, which, 0, 0))
    else:
        query_block = pl.BlockSpec((1,) + queries[0].shape[1:], lambda i, place: (which, 0, 0))
    outs, wide = (1, groups) if ordered else (groups, 1)
    return pl.pallas_call(
        functools.partial(
            attend_body,
            groups=groups,
            asked=len(queries),
            joined=joined,
            ordered=ordered,
            low_lane=low_lane,
            key_room=key_room,
            query_rows=query_rows,
            key_cols=256,
        ),
        grid_spec=pltpu.PrefetchScalarGridSpec(
            num_scalar_prefetch=1,
            grid=(1,),
            in_specs=[query_block] * len(queries)
            + [pl.BlockSpec(keyvals[0].shape, lambda i, place: (0, 0, 0))] * len(keyvals),
            out_specs=[pl.BlockSpec((wide, rows, size), lambda i, place: (0, 0, 0))] * outs,
            scratch_shapes=[
                pltpu.VMEM((key_room + rows, size), bf16),
                pltpu.VMEM((key_room + rows, 2 * size), bf16),
                pltpu.VMEM((query_room, size), bf16),
                pltpu.VMEM((query_room, size), bf16),
            ],
        ),
        out_shape=[jax.ShapeDtypeStruct((wide, rows, size), bf16)] * outs,
        compiler_params=params,
        cost_estimate=cost(
            8 * groups * rows // 2 * running * size,
            4 * shards * rows * size,
            groups * rows // 2 * running,
        ),
        name="attend",
    )(place, *queries, *keyvals)


def finish_body(place_ref, *refs, ordered):
    chunks = len(ordered)
    attended_refs, weight_ref, out_ref, wide_ref = refs[:chunks], *refs[chunks:]

    @pl.when(pl.program_id(0) == 0)
    def _():
        for i, ref in enumerate(attended_refs):
            groups, _, size = ref.shape
            for g in range(groups):
                if ordered[i]:
                    start = (i * groups + g) * size
                else:
                    head = i * groups + lax.bitwise_xor(place_ref[0], g)
                    start = pl.multiple_of(head * size, size)
                wide_ref[:, pl.ds(start, size)] = ref[g]

    total = jnp.dot(wide_ref[...], weight_ref[...], preferred_element_type=f32)
    out_ref[...] = total.astype(out_ref.dtype)


def finish(place, attended, ordered, w_out, mask, kind):
    groups, rows, size = attended[0].shape
    depth = w_out.shape[0]
    out_width = w_out.shape[1] // lax.axis_size("head")
    parts = 2 if out_width % 256 == 0 else 1
    tile = out_width // parts
    column = lambda i, place: (0, lax.bitwise_xor(place[2], mask) * parts + i)
    return pl.pallas_call(
        functools.partial(finish_body, ordered=ordered),
        grid_spec=pltpu.PrefetchScalarGridSpec(
            num_scalar_prefetch=1,
            grid=(parts,),
            in_specs=[pl.BlockSpec((groups, rows, size), lambda i, place: (0, 0, 0))] * len(attended)
            + [pl.BlockSpec((depth, tile), column)],
            out_specs=pl.BlockSpec((rows, tile), lambda i, place: (0, i)),
            scratch_shapes=[pltpu.VMEM((rows, depth), bf16)],
        ),
        out_shape=jax.ShapeDtypeStruct((rows, out_width), kind),
        compiler_params=params,
        cost_estimate=cost(2 * rows * depth * out_width, 2 * depth * out_width + 4 * rows * out_width),
        name="finish",
    )(place, *attended, w_out)


def close_body(back_ref, mine_ref, *refs):
    out_ref = refs[-1]
    total = mine_ref[...].astype(f32)
    for ref in refs[:-1]:
        total += ref[...].astype(f32)
    rounded = total.astype(bf16)
    out_ref[...] = jnp.dot(back_ref[...], rounded, preferred_element_type=f32).astype(bf16)


def close(back, mine, others):
    rows, width = mine.shape
    parts = 4 if width % 512 == 0 else 1
    tile = pl.BlockSpec((rows, width // parts), lambda i: (0, i))
    return pl.pallas_call(
        close_body,
        grid=(parts,),
        in_specs=[pl.BlockSpec((rows, rows), lambda i: (0, 0))] + [tile] * (1 + len(others)),
        out_specs=tile,
        out_shape=jax.ShapeDtypeStruct((rows, width), bf16),
        compiler_params=params,
        cost_estimate=cost(2 * rows * rows * width, 10 * rows * width),
        name="close",
    )(back, mine, *others)


def per_device(tokens, survive, norm_gain, w_qkv, qk_gain, w_out):
    heads, size = qk_gain.shape[1:]
    shards, head_shards = lax.axis_size("seq"), lax.axis_size("head")
    groups = math.gcd(heads & -heads, shards & -shards)
    ring = shards // groups
    chunks = heads // groups
    me, side = lax.axis_index("seq"), lax.axis_index("head")
    place = jnp.stack([me // ring, me % ring, side]).astype(jnp.int32)
    planes = [[i + ring * g for g in range(groups)] for i in range(ring)]

    def swap(blocks):
        return [blocks[0]] + [flip(blocks[k], "seq", k * ring) for k in range(1, groups)]

    def stack(blocks):
        return jnp.concatenate([block[:, :, : 2 * size] for block in blocks])

    def everywhere(stacked, gate):
        found = {0: stacked}
        mask = ring // 2
        while mask:
            for known in list(found):
                source = found[known]
                if gate is not None and mask < ring // 2:
                    source = chain(source, gate)
                found[known | mask] = flip(source, "seq", mask)
            mask //= 2
        return [found[mask] for mask in range(ring)]

    def send_back(blocks):
        if groups == 1:
            return blocks
        return lax.all_to_all(
            blocks, "seq", split_axis=0, concat_axis=0, axis_index_groups=planes, tiled=True
        )

    weights = jnp.transpose(w_qkv, (1, 0, 2))
    gains = jnp.transpose(qk_gain, (1, 0, 2))

    def later(values, *earlier):
        return jnp.maximum(chain(values, *earlier), 0)

    def first(blocks):
        return blocks[min(1, groups - 1)]

    def send(blocks, *earlier):
        return swap(list(chain(tuple(blocks), *earlier)) if earlier else blocks)

    operands = (survive, tokens, norm_gain)
    sets = [((1, 2, 0), (0,))]
    (blocks,), rest = project(place, None, weights, gains, sets, groups, operands)
    normed, chosen, back, count = rest
    arrived = [swap(blocks)]

    rest, asked, hops = range(1, chunks), None, []
    if chunks > 1:
        prepared = (count, chain(normed, first(arrived[0])), chosen)
        sets = [((1, 2), (chunk,)) for chunk in rest]
        made, _ = project(place, prepared, weights, gains, sets, groups)
        stacks = [stack(list(chain(tuple(arrived[0]), made[0][0])))]
        arrived.append(send(made[0]))
        for blocks in made[1:]:
            arrived.append(send(blocks, first(arrived[-1])))
        hop = flip(stacks[0], "seq", ring // 2) if ring > 1 else stacks[0]
        stacks.append(stack(arrived[1]))
        ready = later(count, hop, stacks[1])
        sets = [((0,), tuple(rest))]
        made, _ = project(
            place, (ready, normed, chosen), weights, gains, sets, groups, joined=True
        )
        gate = made
        stacks += [stack(list(chain(tuple(blocks), made))) for blocks in arrived[2:]]
        asked = [send_back(made)]
        hops = [flip(stacks[-1], "seq", ring // 2)] if ring > 1 else []
    else:
        gate, stacks = None, [stack(arrived[0])]

    attended, returned = [], []
    query, low_lane = arrived[0], 2 * size
    for chunk in range(chunks):
        final = chunk == chunks - 1
        keyvals = everywhere(stacks[chunk], gate)
        before = [stacks[-1]] + attended[-1:] + (hops if chunk else []) + (returned[:1] if final else [])
        ready = later(place, *query[1 if chunk == 0 else 0 :], *before)
        row = max(chunk - 1, 0)
        found = attend(ready, query, row, low_lane, keyvals, shards, not final)
        attended.append(found[0])
        returned.append(jnp.concatenate(swap(found)) if final else send_back(found[0]))
        if not final:
            query, low_lane, gate = asked, 0, None
    ordered = (True,) * (chunks - 1) + (False,)
    final = functools.partial(finish, place, returned, ordered, w_out)
    sent = [final(mask, bf16) for mask in range(1, head_shards)]
    others = [flip(part, "head", mask) for mask, part in enumerate(sent, 1)]
    returned[0] = chain(returned[0], *sent)
    return close(back, final(0, bf16), others)


def solution(mesh):
    placed = (
        P("seq", None),
        P("seq"),
        P(),
        P(None, None, "head"),
        P(None, "head", None),
        P("head", None),
    )
    return jax.shard_map(
        per_device, mesh=mesh, in_specs=placed, out_specs=P("seq", "head"), check_vma=False
    )
```
